32 devices in a mesh: tile: 4 (over y, x), proj: 2 (over core), cuts: 4 (over z).
Axes of the slice: x: 2, y: 2, z: 4, core: 2. Of those that a mesh axis runs over, the one named last changes fastest.
Arguments:
- object_field: float32 [8, 2, 384, 2048], P(('proj', 'cuts'), None, None, 'tile'), may hold values from -5 to 5
- probe_field: float32 [2, 256, 256], replicated, may hold values from -6 to 6
- amplitudes: bfloat16 [8, 4, 6, 256, 256], P(('proj', 'cuts'), 'tile'), may hold values from 0 to 16
- pos_rows: int32 [8, 4, 6], P(('proj', 'cuts'), 'tile'), may hold values from 0 to 128
- pos_cols: int32 [8, 4, 6], P(('proj', 'cuts'), 'tile'), may hold values from 0 to 512
- counts: int32 [8, 4], P(('proj', 'cuts'), 'tile'), may hold values from 1 to 6, as said below
- admm_dual: float32 [8, 32, 2048], P(('proj', 'cuts'), None, 'tile'), may hold values from -4 to 4
- volume: float32 [32, 2048, 2048], P('cuts', ('tile', 'proj')), may hold values from -6 to 6
- proj_weights: bfloat16 [16, 2048, 2048], P(None, ('tile', 'proj')), may hold values from -0.125 to 0.125
- ray_weights: float32 [16, 2048], replicated, may hold values from -0.125 to 0.125
- angle_ids: int32 [8], replicated, may hold values from 0 to 15
Outputs:
- new_object: float32 [8, 2, 384, 2048], P(('proj', 'cuts'), None, None, 'tile')
- new_probe: float32 [2, 256, 256], replicated
- new_volume: float32 [32, 2048, 2048], P('cuts', ('tile', 'proj'))
The draws below stay inside these ranges and needn't reach their ends.
Inputs may be any that keep to these rules, and one draw needn't show every extreme that they name: `counts`: every tile holds at least one live position and at most 6; exactly one tile of one projection holds 6, every other holds at most 3.
All inputs are finite; a program needn't handle non-finite values.
Results may differ from the reference program's by a relative error of at most 0.00095.
The reference program's roundings to bfloat16 on the way count: a program that leaves them out, or rounds other values in their place, can miss the bound.
Values may be sent and summed in bfloat16 or wider, within the bound.
No kernel may reach another device: no remote copies, remote signals or barrier semaphores. Data moves between devices by JAX's collectives and lax.ppermute only.
A program may use at most 128 MiB of HBM per device.

```python
import math
import jax
import jax.numpy as jnp
from jax import lax

PB = 256
W = 2048
PR = 384
CAP = 6
SLAB = 32
NANG = 16
A = 8
COLS_DEV = 512
N_TILE = 4


def draw_counts(key, part):
    first_key, second_key = jax.random.split(jax.random.fold_in(key, 17))
    base = jax.random.randint(first_key, (A, N_TILE), 1, CAP // 2 + 1)
    chosen = jax.random.randint(second_key, (), 0, A * N_TILE)
    positions = jnp.arange(A * N_TILE, dtype=jnp.int32).reshape(A, N_TILE)
    return jnp.where(positions == chosen, CAP, base).astype(jnp.int32)


def with_ends(values, own_key, smallest, high):
    shape = values.shape
    place = [jax.random.randint(jax.random.fold_in(own_key, axis), (), 0, shape[axis]) for axis in range(len(shape))]
    values = values.at[tuple(place)].set(smallest)
    longest = shape.index(max(shape))
    place[longest] = (place[longest] + 1) % shape[longest]
    return values.at[tuple(place)].set(high)


def level_of(key, dims, cuts, least, high):
    loudness, own = 1.0, jax.random.fold_in(key, 6)
    for dim, blocks in cuts:
        steps = jnp.exp(jax.random.uniform(jax.random.fold_in(own, dim), (blocks,), jnp.float32, least / len(cuts), high / len(cuts)))
        loudness = loudness * jnp.repeat(steps, dims[dim] // blocks).reshape([-1 if axis == dim else 1 for axis in range(len(dims))])
    return loudness


def noise(own_key, shape, spread, limit, pieces=(), kind=jnp.bfloat16):
    array = jax.random.normal(own_key, shape, jnp.float32) * spread
    if len(pieces) > 0:
        array = level_of(own_key, shape, pieces, -0.22, 0.18) * array
    return jnp.clip(array, min=-limit, max=limit).astype(kind)


def setup_inputs(seed: int = 0) -> dict:
    arg_keys = jax.random.split(jax.random.key(seed), 12)
    object_field = noise(arg_keys[0], (A, 2, PR, W), 0.7, 5.0, ((0, 8), (3, 4)), jnp.float32)
    probe_field = noise(arg_keys[1], (2, PB, PB), 1.0, 6.0, (), jnp.float32)
    amplitudes = jnp.clip(16.0 * jax.random.uniform(arg_keys[2], (A, N_TILE, CAP, PB, PB), jnp.float32) ** level_of(arg_keys[2], (A, N_TILE, CAP, PB, PB), ((0, 8), (1, 4)), -0.2, 0.2), 0.0, 16.0).astype(jnp.bfloat16)
    pos_rows = with_ends(jax.random.randint(arg_keys[3], (A, N_TILE, CAP), 0, PR - PB + 1), jax.random.fold_in(arg_keys[3], 1), 0, PR - PB).astype(jnp.int32)
    pos_cols = with_ends(jax.random.randint(arg_keys[4], (A, N_TILE, CAP), 0, COLS_DEV + 1), jax.random.fold_in(arg_keys[4], 1), 0, COLS_DEV).astype(jnp.int32)
    counts = draw_counts(jax.random.fold_in(arg_keys[11], 71), 0)
    admm_dual = noise(arg_keys[6], (A, SLAB, W), 0.5, 4.0, ((0, 8), (2, 4)), jnp.float32)
    volume = noise(arg_keys[7], (SLAB, W, W), 1.0, 6.0, ((0, 4), (1, 8)), jnp.float32)
    proj_weights = noise(arg_keys[8], (NANG, W, W), W ** -0.5, 0.125, ((1, 8),))
    ray_weights = noise(arg_keys[9], (NANG, W), W ** -0.5, 0.125, (), jnp.float32)
    angle_ids = with_ends(jax.random.randint(arg_keys[10], (A,), 0, NANG), jax.random.fold_in(arg_keys[10], 1), 0, NANG - 1).astype(jnp.int32)
    return {"object_field": object_field, "probe_field": probe_field, "amplitudes": amplitudes, "pos_rows": pos_rows, "pos_cols": pos_cols, "counts": counts, "admm_dual": admm_dual, "volume": volume, "proj_weights": proj_weights, "ray_weights": ray_weights, "angle_ids": angle_ids}


tomo_step = 1.0

def dft_tables(side):
    indices = jnp.arange(side, dtype=jnp.int32)
    products = indices[:, None] * indices[None, :] % side
    phase_angle = products.astype(jnp.float32) * (2.0 * math.pi / side)
    norm_factor = 1.0 / math.sqrt(side)
    return ((jnp.cos(phase_angle) * norm_factor).astype(jnp.bfloat16), (-jnp.sin(phase_angle) * norm_factor).astype(jnp.bfloat16))

def matmul(left, right):
    return jnp.dot(left, right, preferred_element_type=jnp.float32)

def complex_matmul(left_real, left_imag, right_real, right_imag):
    out_real = matmul(left_real, right_real) - matmul(left_imag, right_imag)
    out_imag = matmul(left_real, right_imag) + matmul(left_imag, right_real)
    return (out_real, out_imag)

def patch_terms(patch_real, patch_imag, probe_real, probe_imag, amplitude, dft_real, dft_imag):
    wave_real = (probe_real * patch_real - probe_imag * patch_imag).astype(jnp.bfloat16)
    wave_imag = (probe_real * patch_imag + probe_imag * patch_real).astype(jnp.bfloat16)
    half_real, half_imag = complex_matmul(dft_real, dft_imag, wave_real, wave_imag)
    half_real = half_real.astype(jnp.bfloat16)
    half_imag = half_imag.astype(jnp.bfloat16)
    far_real, far_imag = complex_matmul(half_real, half_imag, dft_real, dft_imag)
    modulus = jnp.sqrt(far_real * far_real + far_imag * far_imag + 0.25)
    factor = amplitude.astype(jnp.float32) / modulus - 1.0
    diff_real = (far_real * factor).astype(jnp.bfloat16)
    diff_imag = (far_imag * factor).astype(jnp.bfloat16)
    conj_imag = -dft_imag
    back_half_real, back_half_imag = complex_matmul(dft_real, conj_imag, diff_real, diff_imag)
    back_half_real = back_half_real.astype(jnp.bfloat16)
    back_half_imag = back_half_imag.astype(jnp.bfloat16)
    back_real, back_imag = complex_matmul(back_half_real, back_half_imag, dft_real, conj_imag)
    object_real = probe_real * back_real + probe_imag * back_imag
    object_imag = probe_real * back_imag - probe_imag * back_real
    probe_grad_real = patch_real * back_real + patch_imag * back_imag
    probe_grad_imag = patch_real * back_imag - patch_imag * back_real
    energy = jnp.mean(patch_real * patch_real + patch_imag * patch_imag)
    return (jnp.stack([object_real, object_imag]), jnp.stack([probe_grad_real, probe_grad_imag]), energy)

def reference(object_field, probe_field, amplitudes, pos_rows, pos_cols, counts, admm_dual, volume, proj_weights, ray_weights, angle_ids):
    half_side = PB // 2
    tile_cols = W // N_TILE
    dft_real, dft_imag = dft_tables(PB)
    probe_real = probe_field[0]
    probe_imag = probe_field[1]
    zero_index = jnp.zeros((), jnp.int32)

    def one_projection(inputs):
        object_one, amp_one, rows_one, cols_one, count_one = inputs
        padded = jnp.pad(object_one, ((0, 0), (0, 0), (half_side, half_side)))
        running = (jnp.zeros(padded.shape, jnp.float32), jnp.zeros((2, PB, PB), jnp.float32), jnp.zeros((), jnp.float32))
        for tile_number in range(N_TILE):

            def slot_step(slot_index, state_tuple):
                grad_sum, probe_sum, energy_sum = state_tuple
                row_at = rows_one[tile_number, slot_index].astype(jnp.int32)
                col_at = (cols_one[tile_number, slot_index] + tile_number * tile_cols).astype(jnp.int32)
                anchor = (zero_index, row_at, col_at)
                object_patch = lax.dynamic_slice(padded, anchor, (2, PB, PB))
                object_part, probe_part, energy = patch_terms(object_patch[0], object_patch[1], probe_real, probe_imag, amp_one[tile_number, slot_index], dft_real, dft_imag)
                current = lax.dynamic_slice(grad_sum, anchor, (2, PB, PB))
                grad_sum = lax.dynamic_update_slice(grad_sum, current + object_part, anchor)
                return (grad_sum, probe_sum + probe_part, energy_sum + energy)
            running = lax.fori_loop(zero_index, count_one[tile_number].astype(jnp.int32), slot_step, running)
        grad_sum, probe_sum, energy_sum = running
        return (grad_sum[:, :, half_side:half_side + W], probe_sum, energy_sum)
    object_grad, probe_parts, energy_parts = lax.map(one_projection, (object_field, amplitudes, pos_rows, pos_cols, counts))
    probe_grad = lax.optimization_barrier(jnp.sum(probe_parts, axis=0))
    energy = jnp.sum(energy_parts)
    new_probe = probe_field + probe_grad / (energy + 1e-05)
    probe_peak = jnp.max(probe_real * probe_real + probe_imag * probe_imag)
    new_object = object_field + object_grad / (probe_peak + 1e-05)
    first_row = (PR - SLAB) // 2
    target = new_object[:, 1, first_row:first_row + SLAB, :] + admm_dual
    ray_table = ray_weights[angle_ids]
    ray_sums = jnp.einsum('zxy,ay->azx', volume, ray_table, precision=lax.Precision.HIGHEST).astype(jnp.bfloat16)

    def one_angle(inputs):
        sums_one, target_one, angle_one = inputs
        weights_one = lax.dynamic_index_in_dim(proj_weights, angle_one.astype(jnp.int32), 0, keepdims=False)
        forward = matmul(sums_one, weights_one)
        residual = (forward - target_one).astype(jnp.bfloat16)
        return lax.dot_general(residual, weights_one, (((1,), (1,)), ((), ())), preferred_element_type=jnp.float32)
    back_sums = lax.map(one_angle, (ray_sums, target, angle_ids))
    gradient = jnp.einsum('azx,ay->zxy', back_sums, ray_table, precision=lax.Precision.HIGHEST)
    new_volume = volume - tomo_step * gradient
    return (new_object, new_probe, new_volume)
```

```python
import math

import jax
import jax.numpy as jnp
import numpy as np
from jax import lax
from jax.experimental import pallas as pl
from jax.experimental.pallas import tpu as pltpu
from jax.sharding import PartitionSpec as P

MIB = 1024 * 1024
VMEM = pltpu.VMEM
F32 = jnp.float32
BF16 = jnp.bfloat16
LANES = 128
SUBLANES = 8
ENERGY_ROWS = 8

tomo_step = 1.0


def shifted(value, axis, steps):
    count = lax.axis_size(axis)
    leading, last = (max(0, -steps), min(count, count - steps))
    return lax.ppermute(value, axis, [(source, source + steps) for source in range(leading, last)])


def dft_blocks(side):
    indices = np.arange(side)
    products = (indices[:, None] * indices[None, :]) % side
    phase = products.astype(np.float32) * np.float32(2.0 * math.pi / side)
    norm = np.float32(1.0 / math.sqrt(side))
    real = np.cos(phase).astype(np.float32) * norm
    imag = -np.sin(phase).astype(np.float32) * norm
    left = np.block([[real, -imag], [imag, real]])
    right = np.block([[real, imag], [-imag, real]])
    return left.astype(jnp.bfloat16), right.astype(jnp.bfloat16)


def dot(left, right):
    return jnp.dot(left, right, preferred_element_type=F32)


def split_bf16(values):
    high = values.astype(BF16).astype(F32)
    low = (values - high).astype(BF16).astype(F32)
    return high, low


def forward_kernel(ids_ref, volume_ref, weights_ref, rays_ref, out_ref, table_ref, sums_ref):
    step = pl.program_id(0)
    depth, projections, _ = sums_ref.shape
    lanes = table_ref.shape[1]
    parts, _, _, share = out_ref.shape

    @pl.when(step == 0)
    def _():
        rows = jnp.concatenate(
            [rays_ref[pl.ds(ids_ref[a], 1), :] for a in range(projections)], axis=0
        )
        high, low = split_bf16(rows)
        stacked = [high, low]
        if lanes > 2 * projections:
            stacked.append(jnp.zeros((lanes - 2 * projections, rows.shape[1]), F32))
        table_ref[...] = jnp.concatenate(stacked, axis=0).T.astype(BF16)

    @pl.when(step < depth)
    def _():
        block = volume_ref[0]
        high = block.astype(BF16)
        low = (block - high.astype(F32)).astype(BF16)
        first = dot(high, table_ref[...]).T
        second = dot(low, table_ref[...]).T
        sums_ref[step] = first[:projections] + (
            first[projections : 2 * projections] + second[:projections]
        )

    @pl.when(step >= depth)
    def _():
        a = step - depth
        rows = sums_ref[:, pl.ds(a, 1), :].reshape(depth, sums_ref.shape[2])
        result = dot(rows.astype(BF16), weights_ref[0])
        for part in range(parts):
            out_ref[part, a] = result[:, part * share : (part + 1) * share]


def forward_parts(angle_ids, volume, proj_weights, ray_weights, parts):
    depth, rows, width = volume.shape
    projections = angle_ids.shape[0]
    angles = ray_weights.shape[0]
    lanes = -(-2 * projections // LANES) * LANES
    share = width // parts
    return pl.pallas_call(
        forward_kernel,
        grid_spec=pltpu.PrefetchScalarGridSpec(
            num_scalar_prefetch=1,
            grid=(depth + projections,),
            in_specs=[
                pl.BlockSpec((1, rows, width), lambda i, ids: (jnp.minimum(i, depth - 1), 0, 0)),
                pl.BlockSpec(
                    (1, rows, width), lambda i, ids: (ids[jnp.maximum(i - depth, 0)], 0, 0)
                ),
                pl.BlockSpec((angles, width), lambda i, ids: (0, 0)),
            ],
            out_specs=pl.BlockSpec((parts, projections, depth, share), lambda i, ids: (0, 0, 0, 0)),
            scratch_shapes=[
                VMEM((width, lanes), BF16),
                VMEM((depth, projections, rows), F32),
            ],
        ),
        out_shape=jax.ShapeDtypeStruct((parts, projections, depth, share), F32),
        compiler_params=pltpu.CompilerParams(vmem_limit_bytes=40 * MIB),
        cost_estimate=pl.CostEstimate(
            flops=4 * depth * rows * width * lanes,
            bytes_accessed=depth * rows * width * 4 + projections * rows * width * 2,
            transcendentals=0,
        ),
        name="forward",
    )(angle_ids, volume, proj_weights, ray_weights)


def placed(values, down, across):
    rows, cols = values.shape
    tall = jnp.concatenate([values, jnp.zeros((SUBLANES, cols), F32)], axis=0)
    tall = pltpu.roll(tall, down, axis=0)
    wide = jnp.concatenate([tall, jnp.zeros((rows + SUBLANES, LANES), F32)], axis=1)
    return pltpu.roll(wide, across, axis=1)


def patch_kernel(
    rows_ref,
    cols_ref,
    count_ref,
    own_ref,
    left_ref,
    right_ref,
    probe_ref,
    amp_ref,
    dft_a_ref,
    dft_b_ref,
    dual_ref,
    new_ref,
    edge_left_ref,
    edge_right_ref,
    slab_ref,
    slab_left_ref,
    slab_right_ref,
    grad_ref,
    ext_ref,
    sum_ref,
    patch_ref,
    wave_ref,
    half_ref,
    far_ref,
    energy_ref,
):
    side = probe_ref.shape[1]
    margin = left_ref.shape[2]
    tile_cols = own_ref.shape[2]
    window = side + LANES
    chunk = 32
    tall = chunk + SUBLANES
    height = own_ref.shape[1]

    for c in range(2):
        ext_ref[c, :height, :margin] = left_ref[c]
        ext_ref[c, :height, margin : margin + tile_cols] = own_ref[c]
        ext_ref[c, :height, margin + tile_cols : 2 * margin + tile_cols] = right_ref[c]
    sum_ref[...] = jnp.zeros(sum_ref.shape, F32)
    grad_ref[...] = jnp.zeros(grad_ref.shape, F32)
    energy_ref[...] = jnp.zeros(energy_ref.shape, F32)

    def slot_step(slot, carry):
        row = rows_ref[slot]
        col = cols_ref[slot]
        lane = lax.rem(col, LANES)
        base = pl.multiple_of(col - lane, LANES)
        back_shift = lax.rem(window - lane, window)
        notch = lax.rem(row, SUBLANES)
        top = pl.multiple_of(row - notch, SUBLANES)
        up_shift = lax.rem(tall - notch, tall)
        for r in range(0, side, chunk):
            cells = pl.ds(top + r, tall)
            here = slice(r, r + chunk)
            below = slice(side + r, side + r + chunk)
            x_re = pltpu.roll(ext_ref[0, cells, pl.ds(base, window)], back_shift, axis=1)[:, :side]
            x_im = pltpu.roll(ext_ref[1, cells, pl.ds(base, window)], back_shift, axis=1)[:, :side]
            x_re = pltpu.roll(x_re, up_shift, axis=0)[:chunk]
            x_im = pltpu.roll(x_im, up_shift, axis=0)[:chunk]
            p_re = probe_ref[0, here, :]
            p_im = probe_ref[1, here, :]
            patch_ref[here, :] = x_re
            patch_ref[below, :] = x_im
            wave_ref[here, :] = (p_re * x_re - p_im * x_im).astype(BF16)
            wave_ref[below, :] = (p_re * x_im + p_im * x_re).astype(BF16)
            power = x_re * x_re + x_im * x_im
            energy_ref[...] += jnp.sum(power.reshape(chunk // 8, 8, side), axis=0)
        half_ref[:, :side] = dot(dft_a_ref[:side, :], wave_ref[...]).astype(BF16)
        half_ref[:, side:] = dot(dft_a_ref[side:, :], wave_ref[...]).astype(BF16)
        far_ref[...] = dot(half_ref[...], dft_b_ref[...])
        for r in range(0, side, chunk):
            here = slice(r, r + chunk)
            below = slice(side + r, side + r + chunk)
            f_re = far_ref[here, :side]
            f_im = far_ref[here, side:]
            inverse = lax.rsqrt(f_re * f_re + f_im * f_im + 0.25)
            factor = amp_ref[slot, here, :].astype(F32) * inverse - 1.0
            wave_ref[here, :] = (f_re * factor).astype(BF16)
            wave_ref[below, :] = (f_im * factor).astype(BF16)
        half_ref[:, :side] = dot(dft_b_ref[:side, :], wave_ref[...]).astype(BF16)
        half_ref[:, side:] = dot(dft_b_ref[side:, :], wave_ref[...]).astype(BF16)
        far_ref[...] = dot(half_ref[...], dft_a_ref[...])
        for r in range(0, side, chunk):
            cells = pl.ds(top + r, tall)
            here = slice(r, r + chunk)
            below = slice(side + r, side + r + chunk)
            b_re = far_ref[here, :side]
            b_im = far_ref[here, side:]
            p_re = probe_ref[0, here, :]
            p_im = probe_ref[1, here, :]
            x_re = patch_ref[here, :]
            x_im = patch_ref[below, :]
            o_re = p_re * b_re + p_im * b_im
            o_im = p_re * b_im - p_im * b_re
            sum_ref[0, cells, pl.ds(base, window)] += placed(o_re, notch, lane)
            sum_ref[1, cells, pl.ds(base, window)] += placed(o_im, notch, lane)
            grad_ref[here, :] += x_re * b_re + x_im * b_im
            grad_ref[below, :] += x_re * b_im - x_im * b_re
        return carry

    lax.fori_loop(0, count_ref[0], slot_step, 0)

    grad_ref[2 * side :, :] = energy_ref[...]
    p_re = probe_ref[0]
    p_im = probe_ref[1]
    peak = jnp.max(p_re * p_re + p_im * p_im)
    scale = 1.0 / (jnp.full((1, LANES), peak, F32) + 1e-05)
    wide = jnp.tile(scale, (1, tile_cols // LANES))
    for c in range(2):
        new_ref[c] = own_ref[c] + sum_ref[c, :height, margin : margin + tile_cols] * wide
        edge_left_ref[c] = sum_ref[c, :height, :margin] * scale
        edge_right_ref[c] = sum_ref[c, :height, margin + tile_cols : 2 * margin + tile_cols] * scale
    slab_rows = dual_ref.shape[0]
    first = (own_ref.shape[1] - slab_rows) // 2
    slab_ref[...] = new_ref[1, first : first + slab_rows, :] + dual_ref[...]
    slab_left_ref[...] = edge_left_ref[1, first : first + slab_rows, :]
    slab_right_ref[...] = edge_right_ref[1, first : first + slab_rows, :]


def patch_updates(rows, cols, count, own, left, right, probe, amplitudes, dual):
    side = probe.shape[1]
    _, height, tile_cols = own.shape
    margin = left.shape[2]
    slots = amplitudes.shape[0]
    slab_rows = dual.shape[0]
    dft_a, dft_b = dft_blocks(side)
    full = pl.BlockSpec(memory_space=VMEM)
    scalars = pl.BlockSpec(memory_space=pltpu.SMEM)
    extent = tile_cols + 2 * margin + LANES
    shape = jax.ShapeDtypeStruct
    return pl.pallas_call(
        patch_kernel,
        in_specs=[scalars] * 3 + [full] * 8,
        out_specs=[full] * 7,
        out_shape=[
            shape((2, height, tile_cols), F32),
            shape((2, height, margin), F32),
            shape((2, height, margin), F32),
            shape((slab_rows, tile_cols), F32),
            shape((slab_rows, margin), F32),
            shape((slab_rows, margin), F32),
            shape((2 * side + ENERGY_ROWS, side), F32),
        ],
        scratch_shapes=[
            VMEM((2, height + SUBLANES, extent), F32),
            VMEM((2, height + SUBLANES, extent), F32),
            VMEM((2 * side, side), F32),
            VMEM((2 * side, side), BF16),
            VMEM((side, 2 * side), BF16),
            VMEM((side, 2 * side), F32),
            VMEM((ENERGY_ROWS, side), F32),
        ],
        compiler_params=pltpu.CompilerParams(vmem_limit_bytes=40 * MIB),
        cost_estimate=pl.CostEstimate(
            flops=slots * 32 * side**3,
            bytes_accessed=8 * height * tile_cols * 4,
            transcendentals=slots * side * side,
        ),
        name="patches",
    )(
        rows,
        cols,
        count,
        own,
        left,
        right,
        probe,
        amplitudes,
        jnp.asarray(dft_a),
        jnp.asarray(dft_b),
        dual,
    )


def update_kernel(
    ids_ref, residual_ref, weights_ref, rays_ref, volume_ref, out_ref, turned_ref, total_ref, stack_ref, rays_bf_ref
):
    step = pl.program_id(0)
    parts, projections, depth, share = residual_ref.shape
    both = projections * depth

    @pl.when(step == 0)
    def _():
        for part in range(parts):
            block = residual_ref[part].astype(F32).reshape(both, share)
            turned_ref[part * share : (part + 1) * share, :] = block.T
        total_ref[...] = jnp.zeros(total_ref.shape, F32)
        width = rays_ref.shape[1]
        rows = jnp.concatenate(
            [
                jnp.broadcast_to(rays_ref[pl.ds(ids_ref[a], 1), :], (depth, width))
                for a in range(projections)
            ],
            axis=0,
        )
        high, low = split_bf16(rows)
        for place, block in enumerate((high, high, low, low)):
            rays_bf_ref[place * both : (place + 1) * both, :] = block.astype(BF16)

    @pl.when(step < projections)
    def _():
        lane = lax.broadcasted_iota(jnp.int32, turned_ref.shape, 1)
        begin = step * depth
        kept = jnp.logical_and(lane >= begin, lane < begin + depth)
        chosen = jnp.where(kept, turned_ref[...], 0.0).astype(BF16)
        total_ref[...] += dot(weights_ref[0], chosen)

    @pl.when(step == projections)
    def _():
        high, low = split_bf16(total_ref[...])
        stack_ref[...] = jnp.concatenate([high, low, high, low], axis=1)

    @pl.when(step >= projections)
    def _():
        lane = lax.broadcasted_iota(jnp.int32, stack_ref.shape, 1)
        kept = lax.rem(lane, depth) == step - projections
        chosen = jnp.where(kept, stack_ref[...], 0.0).astype(BF16)
        out_ref[0] = volume_ref[0] - tomo_step * dot(chosen, rays_bf_ref[...])


def volume_update(angle_ids, residual, proj_weights, ray_weights, volume):
    depth, rows, width = volume.shape
    projections = angle_ids.shape[0]
    angles = ray_weights.shape[0]
    parts, _, _, share = residual.shape
    both = projections * depth
    return pl.pallas_call(
        update_kernel,
        grid_spec=pltpu.PrefetchScalarGridSpec(
            num_scalar_prefetch=1,
            grid=(projections + depth,),
            in_specs=[
                pl.BlockSpec((parts, projections, depth, share), lambda i, ids: (0, 0, 0, 0)),
                pl.BlockSpec(
                    (1, rows, width), lambda i, ids: (ids[jnp.minimum(i, projections - 1)], 0, 0)
                ),
                pl.BlockSpec((angles, width), lambda i, ids: (0, 0)),
                pl.BlockSpec(
                    (1, rows, width), lambda i, ids: (jnp.maximum(i - projections, 0), 0, 0)
                ),
            ],
            out_specs=pl.BlockSpec(
                (1, rows, width), lambda i, ids: (jnp.maximum(i - projections, 0), 0, 0)
            ),
            scratch_shapes=[
                VMEM((width, both), F32),
                VMEM((rows, both), F32),
                VMEM((rows, 4 * both), F32),
                VMEM((4 * both, width), BF16),
            ],
        ),
        out_shape=jax.ShapeDtypeStruct((depth, rows, width), F32),
        compiler_params=pltpu.CompilerParams(vmem_limit_bytes=48 * MIB),
        cost_estimate=pl.CostEstimate(
            flops=2 * rows * width * both * (projections + 4 * depth),
            bytes_accessed=2 * depth * rows * width * 4 + projections * rows * width * 2,
            transcendentals=0,
        ),
        name="update",
    )(angle_ids, residual, proj_weights, ray_weights, volume)


def probe_update(grad, probe):
    side = probe.shape[1]
    flat_axes = ("tile", "proj")
    plane = lax.axis_size("tile") * lax.axis_size("proj")
    layers = lax.axis_size("cuts")
    plane_rows = 2 * side // plane
    layer_rows = plane_rows // layers
    values = grad[: 2 * side].reshape(plane, plane_rows, side)
    energy = jnp.broadcast_to(grad[2 * side :][None], (plane, ENERGY_ROWS, side))
    sent = jnp.concatenate([values, energy], axis=1)
    summed = jnp.sum(lax.all_to_all(sent, flat_axes, 0, 0, tiled=True), axis=0)
    values = summed[:plane_rows].reshape(layers, layer_rows, side)
    energy = jnp.broadcast_to(summed[plane_rows:][None], (layers, ENERGY_ROWS, side))
    sent = jnp.concatenate([values, energy], axis=1)
    summed = jnp.sum(lax.all_to_all(sent, "cuts", 0, 0, tiled=True), axis=0)
    energy = jnp.sum(summed[layer_rows:]) / (side * side)
    part = lax.axis_index(flat_axes) * layers + lax.axis_index("cuts")
    own = lax.dynamic_slice(
        probe.reshape(2 * side, side), (part * layer_rows, jnp.zeros((), jnp.int32)), (layer_rows, side)
    )
    new_rows = own + summed[:layer_rows] / (energy + 1e-05)
    new_rows = lax.all_gather(new_rows, "cuts", axis=0, tiled=True)
    new_rows = lax.all_gather(new_rows, flat_axes, axis=0, tiled=True)
    return new_rows.reshape(2, side, side)


def on_device(
    object_field,
    probe_field,
    amplitudes,
    pos_rows,
    pos_cols,
    counts,
    admm_dual,
    volume,
    proj_weights,
    ray_weights,
    angle_ids,
):
    margin = probe_field.shape[1] // 2
    own = object_field[0]
    tile_cols = own.shape[2]
    flat_axes = ("tile", "proj")
    plane = lax.axis_size("tile") * lax.axis_size("proj")
    proj_count = lax.axis_size("proj")
    layers = lax.axis_size("cuts")
    from_left = shifted(own[:, :, tile_cols - margin :], "tile", 1)
    from_right = shifted(own[:, :, :margin], "tile", -1)
    forward = forward_parts(angle_ids, volume, proj_weights, ray_weights, plane)
    arrived = lax.all_to_all(forward, flat_axes, 0, 0, tiled=True)
    partial_new, edge_left, edge_right, slab, slab_left, slab_right, grad = patch_updates(
        pos_rows[0, 0],
        pos_cols[0, 0],
        counts[0],
        own,
        from_left,
        from_right,
        probe_field,
        amplitudes[0, 0],
        admm_dual[0],
    )
    slab_from_right = shifted(slab_left, "tile", -1)
    slab_from_left = shifted(slab_right, "tile", 1)
    edge_from_right = shifted(edge_left, "tile", -1)
    edge_from_left = shifted(edge_right, "tile", 1)
    slab = slab + jnp.pad(slab_from_left, ((0, 0), (0, tile_cols - margin)))
    slab = slab + jnp.pad(slab_from_right, ((0, 0), (tile_cols - margin, 0)))
    slab_rows = slab.shape[0]
    depth = slab_rows // layers
    share = tile_cols // proj_count
    pieces = slab.reshape(layers, depth, proj_count, share).transpose(2, 0, 1, 3)
    pieces = pieces.reshape(proj_count * layers, depth, share)
    target = lax.all_to_all(pieces, ("proj", "cuts"), 0, 0, tiled=True)
    residual = (jnp.sum(arrived, axis=0) - target).astype(BF16)
    residual = lax.all_gather(residual[None], flat_axes, axis=0, tiled=True)
    new_volume = volume_update(angle_ids, residual, proj_weights, ray_weights, volume)
    new_object = partial_new.at[:, :, :margin].add(edge_from_left)
    new_object = new_object.at[:, :, tile_cols - margin :].add(edge_from_right)
    new_probe = probe_update(grad, probe_field)
    return (new_object[None], new_probe, new_volume)


def solution(mesh):
    in_specs = (
        P(("proj", "cuts"), None, None, "tile"),
        P(),
        P(("proj", "cuts"), "tile", None, None, None),
        P(("proj", "cuts"), "tile", None),
        P(("proj", "cuts"), "tile", None),
        P(("proj", "cuts"), "tile"),
        P(("proj", "cuts"), None, "tile"),
        P("cuts", ("tile", "proj"), None),
        P(None, ("tile", "proj"), None),
        P(),
        P(),
    )
    out_specs = (P(("proj", "cuts"), None, None, "tile"), P(), P("cuts", ("tile", "proj"), None))
    return jax.shard_map(
        on_device, mesh=mesh, in_specs=in_specs, out_specs=out_specs, check_vma=False
    )
```

```python
import math

import jax
import jax.numpy as jnp
import numpy as np
from jax import lax
from jax.experimental import pallas as pl
from jax.experimental.pallas import tpu as pltpu
from jax.sharding import PartitionSpec as P

MIB = 1024 * 1024
VMEM = pltpu.VMEM
F32 = jnp.float32
BF16 = jnp.bfloat16
LANES = 128
SUBLANES = 8
ENERGY_ROWS = 8
AHEAD = 4

tomo_step = 1.0


def shifted(value, axis, steps):
    count = lax.axis_size(axis)
    leading, last = (max(0, -steps), min(count, count - steps))
    return lax.ppermute(value, axis, [(source, source + steps) for source in range(leading, last)])


def dft_blocks(side):
    indices = np.arange(side)
    products = (indices[:, None] * indices[None, :]) % side
    phase = products.astype(np.float32) * np.float32(2.0 * math.pi / side)
    norm = np.float32(1.0 / math.sqrt(side))
    real = np.cos(phase).astype(np.float32) * norm
    imag = -np.sin(phase).astype(np.float32) * norm
    left = np.block([[real, -imag], [imag, real]])
    right = np.block([[real, imag], [-imag, real]])
    return left.astype(jnp.bfloat16), right.astype(jnp.bfloat16)


def dot(left, right):
    return jnp.dot(left, right, preferred_element_type=F32)


def split_bf16(values):
    high = values.astype(BF16).astype(F32)
    low = (values - high).astype(BF16).astype(F32)
    return high, low


def forward_kernel(
    ids_ref,
    rays_ref,
    volume_ref,
    weights_ref,
    out_ref,
    volume_keep,
    weights_keep,
    rays_keep,
    table_ref,
    sums_ref,
    volume_sem,
    weights_sem,
):
    depth, projections, _ = sums_ref.shape
    width, lanes = table_ref.shape
    parts, _, _, share = out_ref.shape
    both = projections * depth

    def volume_copy(z):
        return pltpu.make_async_copy(volume_ref.at[z], volume_keep.at[z], volume_sem.at[z])

    def weights_copy(a):
        return pltpu.make_async_copy(
            weights_ref.at[ids_ref[a]], weights_keep.at[a], weights_sem.at[a]
        )

    for z in range(min(AHEAD, depth)):
        volume_copy(z).start()
    for a in range(min(max(AHEAD - depth, 0), projections)):
        weights_copy(a).start()

    rows = jnp.concatenate([rays_ref[pl.ds(ids_ref[a], 1), :] for a in range(projections)], axis=0)
    high, low = split_bf16(rows)
    stacked = [high, low]
    if lanes > 2 * projections:
        stacked.append(jnp.zeros((lanes - 2 * projections, width), F32))
    table_ref[...] = jnp.concatenate(stacked, axis=0).T.astype(BF16)
    spread = [jnp.broadcast_to(rows[a : a + 1], (depth, width)) for a in range(projections)]
    high, low = split_bf16(jnp.concatenate(spread, axis=0))
    for place, block in enumerate((high, high, low, low)):
        rays_keep[place * both : (place + 1) * both, :] = block.astype(BF16)

    @pl.loop(0, depth)
    def _(z):
        volume_copy(z).wait()

        @pl.when(z + AHEAD < depth)
        def _():
            volume_copy(z + AHEAD).start()

        @pl.when(jnp.logical_and(z + AHEAD >= depth, z + AHEAD - depth < projections))
        def _():
            weights_copy(z + AHEAD - depth).start()

        piece = min(512, width)
        first = second = None
        for k in range(0, width, piece):
            block = volume_keep[z, :, k : k + piece]
            high = block.astype(BF16)
            low = (block - high.astype(F32)).astype(BF16)
            of_high = dot(high, table_ref[k : k + piece, :])
            of_low = dot(low, table_ref[k : k + piece, :])
            first = of_high if first is None else first + of_high
            second = of_low if second is None else second + of_low
        first = first.T
        second = second.T
        sums_ref[z] = first[:projections] + (
            first[projections : 2 * projections] + second[:projections]
        )

    @pl.loop(0, projections)
    def _(a):
        weights_copy(a).wait()

        @pl.when(a + AHEAD < projections)
        def _():
            weights_copy(a + AHEAD).start()

        rows = sums_ref[:, pl.ds(a, 1), :].reshape(depth, sums_ref.shape[2])
        result = dot(rows.astype(BF16), weights_keep[a])
        for part in range(parts):
            out_ref[part, a] = result[:, part * share : (part + 1) * share]


def forward_parts(angle_ids, volume, proj_weights, ray_weights, parts):
    depth, rows, width = volume.shape
    projections = angle_ids.shape[0]
    lanes = -(-2 * projections // LANES) * LANES
    share = width // parts
    full = pl.BlockSpec(memory_space=VMEM)
    shape = jax.ShapeDtypeStruct
    return pl.pallas_call(
        forward_kernel,
        in_specs=[
            pl.BlockSpec(memory_space=pltpu.SMEM),
            full,
            pl.BlockSpec(memory_space=pl.ANY),
            pl.BlockSpec(memory_space=pl.ANY),
        ],
        out_specs=[full] * 4,
        out_shape=[
            shape((parts, projections, depth, share), F32),
            shape((depth, rows, width), F32),
            shape((projections, rows, width), BF16),
            shape((4 * projections * depth, width), BF16),
        ],
        scratch_shapes=[
            VMEM((width, lanes), BF16),
            VMEM((depth, projections, rows), F32),
            pltpu.SemaphoreType.DMA((depth,)),
            pltpu.SemaphoreType.DMA((projections,)),
        ],
        compiler_params=pltpu.CompilerParams(vmem_limit_bytes=14 * MIB),
        cost_estimate=pl.CostEstimate(
            flops=4 * depth * rows * width * lanes,
            bytes_accessed=depth * rows * width * 4 + projections * rows * width * 2,
            transcendentals=0,
        ),
        name="forward",
    )(angle_ids, ray_weights, volume, proj_weights)


def placed(values, down, across):
    rows, cols = values.shape
    tall = jnp.concatenate([values, jnp.zeros((SUBLANES, cols), F32)], axis=0)
    tall = pltpu.roll(tall, down, axis=0)
    wide = jnp.concatenate([tall, jnp.zeros((rows + SUBLANES, LANES), F32)], axis=1)
    return pltpu.roll(wide, across, axis=1)


def patch_kernel(
    rows_ref,
    cols_ref,
    count_ref,
    own_ref,
    left_ref,
    right_ref,
    probe_ref,
    amp_ref,
    dft_a_ref,
    dft_b_ref,
    dual_ref,
    new_ref,
    edge_left_ref,
    edge_right_ref,
    slab_ref,
    parts_ref,
    ext_ref,
    sum_ref,
    patch_ref,
    wave_ref,
    half_ref,
    far_ref,
    grad_ref,
    energy_ref,
):
    side = probe_ref.shape[1]
    margin = left_ref.shape[2]
    tile_cols = own_ref.shape[2]
    window = side + LANES
    chunk = 32
    tall = chunk + SUBLANES
    height = own_ref.shape[1]

    for c in range(2):
        ext_ref[c, :height, :margin] = left_ref[c]
        ext_ref[c, :height, margin : margin + tile_cols] = own_ref[c]
        ext_ref[c, :height, margin + tile_cols : 2 * margin + tile_cols] = right_ref[c]
    sum_ref[...] = jnp.zeros(sum_ref.shape, F32)
    grad_ref[...] = jnp.zeros(grad_ref.shape, F32)
    energy_ref[...] = jnp.zeros(energy_ref.shape, F32)

    def slot_step(slot, carry):
        row = rows_ref[slot]
        col = cols_ref[slot]
        lane = lax.rem(col, LANES)
        base = pl.multiple_of(col - lane, LANES)
        back_shift = lax.rem(window - lane, window)
        notch = lax.rem(row, SUBLANES)
        top = pl.multiple_of(row - notch, SUBLANES)
        up_shift = lax.rem(tall - notch, tall)
        for r in range(0, side, chunk):
            cells = pl.ds(top + r, tall)
            here = slice(r, r + chunk)
            below = slice(side + r, side + r + chunk)
            x_re = pltpu.roll(ext_ref[0, cells, pl.ds(base, window)], back_shift, axis=1)[:, :side]
            x_im = pltpu.roll(ext_ref[1, cells, pl.ds(base, window)], back_shift, axis=1)[:, :side]
            x_re = pltpu.roll(x_re, up_shift, axis=0)[:chunk]
            x_im = pltpu.roll(x_im, up_shift, axis=0)[:chunk]
            p_re = probe_ref[0, here, :]
            p_im = probe_ref[1, here, :]
            patch_ref[here, :] = x_re
            patch_ref[below, :] = x_im
            wave_ref[here, :] = (p_re * x_re - p_im * x_im).astype(BF16)
            wave_ref[below, :] = (p_re * x_im + p_im * x_re).astype(BF16)
            power = x_re * x_re + x_im * x_im
            energy_ref[...] += jnp.sum(power.reshape(chunk // 8, 8, side), axis=0)
        half_ref[:, :side] = dot(dft_a_ref[:side, :], wave_ref[...]).astype(BF16)
        half_ref[:, side:] = dot(dft_a_ref[side:, :], wave_ref[...]).astype(BF16)
        far_ref[...] = dot(half_ref[...], dft_b_ref[...])
        for r in range(0, side, chunk):
            here = slice(r, r + chunk)
            below = slice(side + r, side + r + chunk)
            f_re = far_ref[here, :side]
            f_im = far_ref[here, side:]
            inverse = lax.rsqrt(f_re * f_re + f_im * f_im + 0.25)
            factor = amp_ref[slot, here, :].astype(F32) * inverse - 1.0
            wave_ref[here, :] = (f_re * factor).astype(BF16)
            wave_ref[below, :] = (f_im * factor).astype(BF16)
        half_ref[:, :side] = dot(dft_b_ref[:side, :], wave_ref[...]).astype(BF16)
        half_ref[:, side:] = dot(dft_b_ref[side:, :], wave_ref[...]).astype(BF16)
        far_ref[...] = dot(half_ref[...], dft_a_ref[...])
        for r in range(0, side, chunk):
            cells = pl.ds(top + r, tall)
            here = slice(r, r + chunk)
            below = slice(side + r, side + r + chunk)
            b_re = far_ref[here, :side]
            b_im = far_ref[here, side:]
            p_re = probe_ref[0, here, :]
            p_im = probe_ref[1, here, :]
            x_re = patch_ref[here, :]
            x_im = patch_ref[below, :]
            o_re = p_re * b_re + p_im * b_im
            o_im = p_re * b_im - p_im * b_re
            sum_ref[0, cells, pl.ds(base, window)] += placed(o_re, notch, lane)
            sum_ref[1, cells, pl.ds(base, window)] += placed(o_im, notch, lane)
            grad_ref[here, :] += x_re * b_re + x_im * b_im
            grad_ref[below, :] += x_re * b_im - x_im * b_re
        return carry

    lax.fori_loop(0, count_ref[0], slot_step, 0)

    parts, part_rows, _ = parts_ref.shape
    part_rows -= ENERGY_ROWS
    for part in range(parts):
        parts_ref[part, :part_rows, :] = grad_ref[part * part_rows : (part + 1) * part_rows, :]
        parts_ref[part, part_rows:, :] = energy_ref[...]
    p_re = probe_ref[0]
    p_im = probe_ref[1]
    peak = jnp.max(p_re * p_re + p_im * p_im)
    scale = 1.0 / (jnp.full((1, LANES), peak, F32) + 1e-05)
    wide = jnp.tile(scale, (1, tile_cols // LANES))
    for c in range(2):
        new_ref[c] = own_ref[c] + sum_ref[c, :height, margin : margin + tile_cols] * wide
        edge_left_ref[c] = sum_ref[c, :height, :margin] * scale
        edge_right_ref[c] = sum_ref[c, :height, margin + tile_cols : 2 * margin + tile_cols] * scale
    shares, layers, depth, share = slab_ref.shape
    edge = min(share - tile_cols // shares, margin)
    share -= edge
    holders = margin // edge
    first = (height - layers * depth) // 2
    for layer in range(layers):
        rows = slice(layer * depth, (layer + 1) * depth)
        cells = slice(first + layer * depth, first + (layer + 1) * depth)
        for p in range(shares):
            cols = slice(p * share, (p + 1) * share)
            slab_ref[p, layer, :, :share] = new_ref[1, cells, cols] + dual_ref[rows, cols]
            begin = (p - shares + holders) * edge
            if p < holders:
                outgoing = edge_left_ref[1, cells, p * edge : (p + 1) * edge]
            elif p >= shares - holders:
                outgoing = edge_right_ref[1, cells, begin : begin + edge]
            else:
                outgoing = jnp.zeros((depth, edge), F32)
            slab_ref[p, layer, :, share:] = outgoing


def patch_updates(
    rows, cols, count, own, left, right, probe, amplitudes, dual, parts, shares, layers
):
    side = probe.shape[1]
    _, height, tile_cols = own.shape
    margin = left.shape[2]
    slots = amplitudes.shape[0]
    slab_rows = dual.shape[0]
    share = tile_cols // shares
    edge = min(share, margin)
    dft_a, dft_b = dft_blocks(side)
    full = pl.BlockSpec(memory_space=VMEM)
    scalars = pl.BlockSpec(memory_space=pltpu.SMEM)
    extent = tile_cols + 2 * margin + LANES
    shape = jax.ShapeDtypeStruct
    return pl.pallas_call(
        patch_kernel,
        in_specs=[scalars] * 3 + [full] * 8,
        out_specs=[full] * 5,
        out_shape=[
            shape((2, height, tile_cols), F32),
            shape((2, height, margin), F32),
            shape((2, height, margin), F32),
            shape((shares, layers, slab_rows // layers, share + edge), F32),
            shape((parts, 2 * side // parts + ENERGY_ROWS, side), F32),
        ],
        scratch_shapes=[
            VMEM((2, height + SUBLANES, extent), F32),
            VMEM((2, height + SUBLANES, extent), F32),
            VMEM((2 * side, side), F32),
            VMEM((2 * side, side), BF16),
            VMEM((side, 2 * side), BF16),
            VMEM((side, 2 * side), F32),
            VMEM((2 * side, side), F32),
            VMEM((ENERGY_ROWS, side), F32),
        ],
        compiler_params=pltpu.CompilerParams(vmem_limit_bytes=16 * MIB),
        cost_estimate=pl.CostEstimate(
            flops=slots * 32 * side**3,
            bytes_accessed=8 * height * tile_cols * 4,
            transcendentals=slots * side * side,
        ),
        name="patches",
    )(
        rows,
        cols,
        count,
        own,
        left,
        right,
        probe,
        amplitudes,
        jnp.asarray(dft_a),
        jnp.asarray(dft_b),
        dual,
    )


def backward_kernel(residual_ref, weights_ref, out_ref, turned_ref):
    parts, projections, depth, share = residual_ref.shape
    both = projections * depth
    for part in range(parts):
        block = residual_ref[part].astype(F32).reshape(both, share)
        turned_ref[part * share : (part + 1) * share, :] = block.T
    out_ref[...] = jnp.zeros(out_ref.shape, F32)

    @pl.loop(0, projections)
    def _(a):
        lane = lax.broadcasted_iota(jnp.int32, turned_ref.shape, 1)
        begin = a * depth
        kept = jnp.logical_and(lane >= begin, lane < begin + depth)
        chosen = jnp.where(kept, turned_ref[...], 0.0).astype(BF16)
        out_ref[...] += dot(weights_ref[a], chosen)


def backward_sums(residual, weights):
    projections, rows, width = weights.shape
    depth = residual.shape[2]
    full = pl.BlockSpec(memory_space=VMEM)
    return pl.pallas_call(
        backward_kernel,
        in_specs=[full] * 2,
        out_specs=full,
        out_shape=jax.ShapeDtypeStruct((rows, projections * depth), F32),
        scratch_shapes=[VMEM((width, projections * depth), F32)],
        compiler_params=pltpu.CompilerParams(vmem_limit_bytes=14 * MIB),
        cost_estimate=pl.CostEstimate(
            flops=2 * rows * width * projections * projections * depth,
            bytes_accessed=projections * rows * width * 2,
            transcendentals=0,
        ),
        name="backward",
    )(residual, weights)


def update_kernel(
    sums_ref,
    rays_ref,
    volume_ref,
    object_ref,
    from_left_ref,
    from_right_ref,
    out_ref,
    new_object_ref,
    stack_ref,
    done_ref,
    cells_ref,
    out_sem,
    object_sem,
):
    depth = volume_ref.shape[0]
    slots = done_ref.shape[0]
    margin = from_left_ref.shape[2]
    tile_cols = object_ref.shape[2]
    high, low = split_bf16(sums_ref[...])
    stack_ref[...] = jnp.concatenate([high, low, high, low], axis=1)

    def out_copy(z):
        slot = lax.rem(z, slots)
        return pltpu.make_async_copy(done_ref.at[slot], out_ref.at[z], out_sem.at[slot])

    @pl.loop(0, depth)
    def _(z):
        @pl.when(z >= slots)
        def _():
            out_copy(z - slots).wait()

        lane = lax.broadcasted_iota(jnp.int32, stack_ref.shape, 1)
        kept = lax.rem(lane, depth) == z
        chosen = jnp.where(kept, stack_ref[...], 0.0).astype(BF16)
        done_ref[lax.rem(z, slots)] = volume_ref[z] - tomo_step * dot(chosen, rays_ref[...])
        out_copy(z).start()

    cells_ref[...] = object_ref[...]
    cells_ref[:, :, :margin] += from_left_ref[...]
    cells_ref[:, :, tile_cols - margin :] += from_right_ref[...]
    object_copy = pltpu.make_async_copy(cells_ref, new_object_ref, object_sem)
    object_copy.start()
    for z in range(max(depth - slots, 0), depth):
        out_copy(z).wait()
    object_copy.wait()


def volume_update(sums, rays, volume, partial_object, from_left, from_right):
    depth, rows, width = volume.shape
    slots = min(4, depth)
    full = pl.BlockSpec(memory_space=VMEM)
    anywhere = pl.BlockSpec(memory_space=pl.ANY)
    return pl.pallas_call(
        update_kernel,
        in_specs=[full] * 6,
        out_specs=[anywhere] * 2,
        out_shape=[
            jax.ShapeDtypeStruct(volume.shape, F32),
            jax.ShapeDtypeStruct(partial_object.shape, F32),
        ],
        scratch_shapes=[
            VMEM((rows, 4 * sums.shape[1]), F32),
            VMEM((slots, rows, width), F32),
            VMEM(partial_object.shape, F32),
            pltpu.SemaphoreType.DMA((slots,)),
            pltpu.SemaphoreType.DMA,
        ],
        compiler_params=pltpu.CompilerParams(vmem_limit_bytes=18 * MIB),
        cost_estimate=pl.CostEstimate(
            flops=8 * rows * width * sums.shape[1] * depth,
            bytes_accessed=depth * rows * width * 4,
            transcendentals=0,
        ),
        name="update",
    )(sums, rays, volume, partial_object, from_left, from_right)


def spread_to(value, axes, count):
    copies = jnp.broadcast_to(value[None], (count, *value.shape))
    return lax.all_to_all(copies, axes, 0, 0, tiled=True)


def on_device(
    object_field,
    probe_field,
    amplitudes,
    pos_rows,
    pos_cols,
    counts,
    admm_dual,
    volume,
    proj_weights,
    ray_weights,
    angle_ids,
):
    margin = probe_field.shape[1] // 2
    own = object_field[0]
    tile_cols = own.shape[2]
    flat_axes = ("tile", "proj")
    plane = lax.axis_size("tile") * lax.axis_size("proj")
    proj_count = lax.axis_size("proj")
    layers = lax.axis_size("cuts")
    from_left = shifted(own[:, :, tile_cols - margin :], "tile", 1)
    from_right = shifted(own[:, :, :margin], "tile", -1)
    forward, volume_kept, weights_kept, rays_kept = forward_parts(
        angle_ids, volume, proj_weights, ray_weights, plane
    )
    arrived = lax.all_to_all(forward, flat_axes, 0, 0, tiled=True)
    partial_object, edge_left, edge_right, slab, grad_parts = patch_updates(
        pos_rows[0, 0],
        pos_cols[0, 0],
        counts[0],
        own,
        from_left,
        from_right,
        probe_field,
        amplitudes[0, 0],
        admm_dual[0],
        plane,
        proj_count,
        layers,
    )

    share = tile_cols // proj_count
    edge = slab.shape[3] - share
    holders = margin // edge
    pieces = slab.reshape(proj_count * layers, *slab.shape[2:])
    pieces = lax.all_to_all(pieces, ("proj", "cuts"), 0, 0, tiled=True)
    pairs = []
    for tile in range(lax.axis_size("tile") - 1):
        for k in range(holders):
            lower = tile * proj_count + proj_count - holders + k
            upper = (tile + 1) * proj_count + k
            pairs += [(lower, upper), (upper, lower)]
    grads_in = lax.ppermute(pieces[:, :, share:], flat_axes, pairs)
    at_start = jnp.pad(grads_in, ((0, 0), (0, 0), (0, share - edge)))
    at_end = jnp.pad(grads_in, ((0, 0), (0, 0), (share - edge, 0)))
    target = pieces[:, :, :share] + jnp.where(
        lax.axis_index("proj") < holders, at_start, at_end
    )
    residual = (jnp.sum(arrived, axis=0) - target).astype(BF16)
    residual = spread_to(residual, flat_axes, plane)
    back_sums = backward_sums(residual, weights_kept)

    edge_from_right = shifted(edge_left, "tile", -1)
    edge_from_left = shifted(edge_right, "tile", 1)

    side = probe_field.shape[1]
    part_rows = grad_parts.shape[1] - ENERGY_ROWS
    summed = jnp.sum(lax.all_to_all(grad_parts, flat_axes, 0, 0, tiled=True), axis=0)
    summed = jnp.sum(spread_to(summed, "cuts", layers), axis=0)
    energy = jnp.sum(summed[part_rows:]) / (side * side)
    begin = lax.axis_index(flat_axes) * part_rows
    own_rows = lax.dynamic_slice(
        probe_field.reshape(2 * side, side),
        (begin, jnp.zeros((), begin.dtype)),
        (part_rows, side),
    )
    new_rows = own_rows + summed[:part_rows] / (energy + 1e-05)
    new_probe = spread_to(new_rows, flat_axes, plane).reshape(2, side, side)

    new_volume, new_object = volume_update(
        back_sums, rays_kept, volume_kept, partial_object, edge_from_left, edge_from_right
    )
    return (new_object[None], new_probe, new_volume)


def solution(mesh):
    in_specs = (
        P(("proj", "cuts"), None, None, "tile"),
        P(),
        P(("proj", "cuts"), "tile", None, None, None),
        P(("proj", "cuts"), "tile", None),
        P(("proj", "cuts"), "tile", None),
        P(("proj", "cuts"), "tile"),
        P(("proj", "cuts"), None, "tile"),
        P("cuts", ("tile", "proj"), None),
        P(None, ("tile", "proj"), None),
        P(),
        P(),
    )
    out_specs = (P(("proj", "cuts"), None, None, "tile"), P(), P("cuts", ("tile", "proj"), None))
    return jax.shard_map(
        on_device, mesh=mesh, in_specs=in_specs, out_specs=out_specs, check_vma=False
    )
```

```python
import functools
import math

import jax
import jax.numpy as jnp
import numpy as np
from jax import lax
from jax.experimental import pallas as pl
from jax.experimental.pallas import tpu as pltpu
from jax.sharding import PartitionSpec as P

MIB = 1024 * 1024
VMEM = pltpu.VMEM
F32 = jnp.float32
BF16 = jnp.bfloat16
LANES = 128
SUBLANES = 8
ENERGY_ROWS = 8
AHEAD = 6
ANYWHERE = pl.BlockSpec(memory_space=pl.ANY)
IN_HBM = pl.BlockSpec(memory_space=pltpu.HBM)
WHOLE = pl.BlockSpec(memory_space=pltpu.VMEM)
SCALARS = pl.BlockSpec(memory_space=pltpu.SMEM)
DMA = pltpu.SemaphoreType.DMA

tomo_step = 1.0


def shifted(value, axis, steps):
    count = lax.axis_size(axis)
    leading, last = (max(0, -steps), min(count, count - steps))
    return lax.ppermute(value, axis, [(source, source + steps) for source in range(leading, last)])


def dft_blocks(side):
    indices = np.arange(side)
    products = (indices[:, None] * indices[None, :]) % side
    phase = products.astype(np.float32) * np.float32(2.0 * math.pi / side)
    norm = np.float32(1.0 / math.sqrt(side))
    real = np.cos(phase).astype(np.float32) * norm
    imag = -np.sin(phase).astype(np.float32) * norm
    left = np.block([[real, -imag], [imag, real]])
    right = np.block([[real, imag], [-imag, real]])
    return left.astype(jnp.bfloat16), right.astype(jnp.bfloat16)


def dot(left, right):
    return jnp.dot(left, right, preferred_element_type=F32)


def split_bf16(values):
    high = values.astype(BF16).astype(F32)
    low = (values - high).astype(BF16).astype(F32)
    return high, low


def forward_kernel(
    ids_ref,
    rays_hbm,
    volume_hbm,
    weights_hbm,
    out_hbm,
    rays_ref,
    volume_ref,
    weights_ref,
    out_ref,
    table_ref,
    sums_ref,
    rays_sem,
    volume_sem,
    weights_sem,
    out_sem,
):
    depth, projections, _ = sums_ref.shape
    width, lanes = table_ref.shape
    parts, _, _, share = out_ref.shape

    def volume_copy(z):
        return pltpu.make_async_copy(volume_hbm.at[z], volume_ref.at[z], volume_sem.at[z])

    def weights_copy(a):
        return pltpu.make_async_copy(
            weights_hbm.at[ids_ref[a]], weights_ref.at[a], weights_sem.at[a]
        )

    def out_copy(a):
        return pltpu.make_async_copy(out_ref.at[:, a], out_hbm.at[:, a], out_sem.at[a])

    rays_copy = pltpu.make_async_copy(rays_hbm, rays_ref, rays_sem)
    rays_copy.start()
    for z in range(min(AHEAD, depth)):
        volume_copy(z).start()
    for a in range(min(max(AHEAD - depth, 0), projections)):
        weights_copy(a).start()

    rays_copy.wait()
    rows = jnp.concatenate([rays_ref[pl.ds(ids_ref[a], 1), :] for a in range(projections)], axis=0)
    high, low = split_bf16(rows)
    stacked = [high, low]
    if lanes > 2 * projections:
        stacked.append(jnp.zeros((lanes - 2 * projections, width), F32))
    table_ref[...] = jnp.concatenate(stacked, axis=0).T.astype(BF16)

    @pl.loop(0, depth)
    def _(z):
        volume_copy(z).wait()

        @pl.when(z + AHEAD < depth)
        def _():
            volume_copy(z + AHEAD).start()

        @pl.when(jnp.logical_and(z + AHEAD >= depth, z + AHEAD - depth < projections))
        def _():
            weights_copy(z + AHEAD - depth).start()

        piece = min(512, width)
        first = second = None
        for k in range(0, width, piece):
            block = volume_ref[z, :, k : k + piece]
            high = block.astype(BF16)
            low = (block - high.astype(F32)).astype(BF16)
            of_high = dot(high, table_ref[k : k + piece, :])
            of_low = dot(low, table_ref[k : k + piece, :])
            first = of_high if first is None else first + of_high
            second = of_low if second is None else second + of_low
        first = first.T
        second = second.T
        sums_ref[z] = first[:projections] + (
            first[projections : 2 * projections] + second[:projections]
        )

    @pl.loop(0, projections)
    def _(a):
        weights_copy(a).wait()

        @pl.when(a + AHEAD < projections)
        def _():
            weights_copy(a + AHEAD).start()

        rows = sums_ref[:, pl.ds(a, 1), :].reshape(depth, sums_ref.shape[2])
        result = dot(rows.astype(BF16), weights_ref[a])
        for part in range(parts):
            out_ref[part, a] = result[:, part * share : (part + 1) * share]
        out_copy(a).start()

    @pl.loop(0, projections)
    def _(a):
        out_copy(a).wait()


def forward_parts(angle_ids, volume, proj_weights, ray_weights, parts):
    depth, rows, width = volume.shape
    projections = angle_ids.shape[0]
    lanes = -(-2 * projections // LANES) * LANES
    share = width // parts
    return pl.pallas_call(
        forward_kernel,
        in_specs=[SCALARS] + [IN_HBM] * 3,
        out_specs=IN_HBM,
        out_shape=jax.ShapeDtypeStruct((parts, projections, depth, share), F32),
        scratch_shapes=[
            VMEM(ray_weights.shape, F32),
            VMEM(volume.shape, F32),
            VMEM((projections, rows, width), BF16),
            VMEM((parts, projections, depth, share), F32),
            VMEM((width, lanes), BF16),
            VMEM((depth, projections, rows), F32),
            DMA,
            pltpu.SemaphoreType.DMA((depth,)),
            pltpu.SemaphoreType.DMA((projections,)),
            pltpu.SemaphoreType.DMA((projections,)),
        ],
        compiler_params=pltpu.CompilerParams(vmem_limit_bytes=44 * MIB),
        cost_estimate=pl.CostEstimate(
            flops=4 * depth * rows * width * lanes,
            bytes_accessed=depth * rows * width * 4 + projections * rows * width * 2,
            transcendentals=0,
        ),
        name="forward",
    )(angle_ids, ray_weights, volume, proj_weights)


def placed(values, down, across):
    rows, cols = values.shape
    tall = jnp.concatenate([values, jnp.zeros((SUBLANES, cols), F32)], axis=0)
    tall = pltpu.roll(tall, down, axis=0)
    wide = jnp.concatenate([tall, jnp.zeros((rows + SUBLANES, LANES), F32)], axis=1)
    return pltpu.roll(wide, across, axis=1)


def patch_kernel(
    rows_ref,
    cols_ref,
    count_ref,
    place_ref,
    own_hbm,
    left_hbm,
    right_hbm,
    probe_hbm,
    amp_hbm,
    dft_a_hbm,
    dft_b_hbm,
    dual_hbm,
    new_hbm,
    edge_left_hbm,
    edge_right_hbm,
    slab_hbm,
    *rest,
):
    shares = len(rest) - 26
    parts_hbm = rest[:shares]
    (
        probe_ref,
        amp_ref,
        dft_a_ref,
        dft_b_ref,
        dual_ref,
        new_ref,
        edge_left_ref,
        edge_right_ref,
        slab_ref,
        parts_ref,
        ext_ref,
        sum_ref,
        grad_ref,
        energy_ref,
        patch_a_ref,
        patch_b_ref,
        wave_a_ref,
        wave_b_ref,
        half_a_ref,
        half_b_ref,
        far_a_ref,
        far_b_ref,
        in_sem,
        slab_sem,
        parts_sem,
        out_sem,
    ) = rest[shares:]
    slots = amp_ref.shape[0]
    side = probe_ref.shape[1]
    _, height, margin = edge_left_ref.shape
    tile_cols = new_ref.shape[2]
    window = side + LANES
    chunk = 32
    tall = chunk + SUBLANES
    grad_rows = grad_ref.shape[1]
    extent = ext_ref.shape[2]
    inner = pl.ds(0, height)

    copies = [
        pltpu.make_async_copy(source, target, in_sem.at[k])
        for k, (source, target) in enumerate(
            (
                (left_hbm, ext_ref.at[:, inner, pl.ds(0, margin)]),
                (own_hbm, ext_ref.at[:, inner, pl.ds(margin, tile_cols)]),
                (right_hbm, ext_ref.at[:, inner, pl.ds(margin + tile_cols, margin)]),
                (probe_hbm, probe_ref),
                (dft_a_hbm, dft_a_ref),
                (dft_b_hbm, dft_b_ref),
                (amp_hbm, amp_ref),
                (dual_hbm, dual_ref),
            )
        )
    ]
    for copy in copies:
        copy.start()
    sum_ref[...] = jnp.zeros(sum_ref.shape, F32)
    grad_ref[...] = jnp.zeros(grad_ref.shape, F32)
    energy_ref[...] = jnp.zeros(energy_ref.shape, F32)
    for copy in copies:
        copy.wait()

    def pair_step(pair, carry):
        chains = []
        for k, refs in enumerate(
            (
                (patch_a_ref, wave_a_ref, half_a_ref, far_a_ref),
                (patch_b_ref, wave_b_ref, half_b_ref, far_b_ref),
            )
        ):
            slot = jnp.minimum(2 * pair + k, slots - 1)
            live = (2 * pair + k < count_ref[0]).astype(F32)
            row = rows_ref[slot]
            col = cols_ref[slot]
            lane = lax.rem(col, LANES)
            notch = lax.rem(row, SUBLANES)
            base = pl.multiple_of(col - lane, LANES)
            top = pl.multiple_of(row - notch, SUBLANES)
            chains.append((slot, live, lane, notch, base, top, *refs))
        for slot, live, lane, notch, base, top, patch_ref, wave_ref, half_ref, far_ref in chains:
            back_shift = lax.rem(window - lane, window)
            up_shift = lax.rem(tall - notch, tall)
            for r in range(0, side, chunk):
                cells = pl.ds(top + r, tall)
                here = slice(r, r + chunk)
                below = slice(side + r, side + r + chunk)
                x_re = pltpu.roll(ext_ref[0, cells, pl.ds(base, window)], back_shift, axis=1)
                x_im = pltpu.roll(ext_ref[1, cells, pl.ds(base, window)], back_shift, axis=1)
                x_re = pltpu.roll(x_re[:, :side], up_shift, axis=0)[:chunk]
                x_im = pltpu.roll(x_im[:, :side], up_shift, axis=0)[:chunk]
                p_re = probe_ref[0, here, :]
                p_im = probe_ref[1, here, :]
                patch_ref[here, :] = x_re
                patch_ref[below, :] = x_im
                wave_ref[here, :] = (p_re * x_re - p_im * x_im).astype(BF16)
                wave_ref[below, :] = (p_re * x_im + p_im * x_re).astype(BF16)
                power = x_re * x_re + x_im * x_im
                energy_ref[...] += live * jnp.sum(
                    power.reshape(chunk // SUBLANES, SUBLANES, side), axis=0
                )
        for *_, wave_ref, half_ref, far_ref in chains:
            half_ref[:, :side] = dot(dft_a_ref[:side, :], wave_ref[...]).astype(BF16)
            half_ref[:, side:] = dot(dft_a_ref[side:, :], wave_ref[...]).astype(BF16)
        for *_, half_ref, far_ref in chains:
            far_ref[...] = dot(half_ref[...], dft_b_ref[...])
        for slot, live, *_, wave_ref, half_ref, far_ref in chains:
            for r in range(0, side, chunk):
                here = slice(r, r + chunk)
                below = slice(side + r, side + r + chunk)
                f_re = far_ref[here, :side]
                f_im = far_ref[here, side:]
                inverse = lax.rsqrt(f_re * f_re + f_im * f_im + 0.25)
                factor = amp_ref[slot, here, :].astype(F32) * inverse - 1.0
                wave_ref[here, :] = (f_re * factor).astype(BF16)
                wave_ref[below, :] = (f_im * factor).astype(BF16)
        for *_, wave_ref, half_ref, far_ref in chains:
            half_ref[:, :side] = dot(dft_b_ref[:side, :], wave_ref[...]).astype(BF16)
            half_ref[:, side:] = dot(dft_b_ref[side:, :], wave_ref[...]).astype(BF16)
        for *_, half_ref, far_ref in chains:
            far_ref[...] = dot(half_ref[...], dft_a_ref[...])
        for slot, live, lane, notch, base, top, patch_ref, wave_ref, half_ref, far_ref in chains:
            for r in range(0, side, chunk):
                cells = pl.ds(top + r, tall)
                here = slice(r, r + chunk)
                below = slice(side + r, side + r + chunk)
                b_re = live * far_ref[here, :side]
                b_im = live * far_ref[here, side:]
                p_re = probe_ref[0, here, :]
                p_im = probe_ref[1, here, :]
                x_re = patch_ref[here, :]
                x_im = patch_ref[below, :]
                o_re = p_re * b_re + p_im * b_im
                o_im = p_re * b_im - p_im * b_re
                sum_ref[0, cells, pl.ds(base, window)] += placed(o_re, notch, lane)
                sum_ref[1, cells, pl.ds(base, window)] += placed(o_im, notch, lane)
                at = r % grad_rows
                part = r // grad_rows
                rows = slice(at, at + chunk)
                grad_ref[part, rows, :] += x_re * b_re + x_im * b_im
                part += side // grad_rows
                grad_ref[part, rows, :] += x_re * b_im - x_im * b_re
        return carry

    lax.fori_loop(0, lax.div(count_ref[0] + 1, 2), pair_step, 0)

    p_re = probe_ref[0]
    p_im = probe_ref[1]
    peak = jnp.max(p_re * p_re + p_im * p_im)
    scale = 1.0 / (jnp.full((1, LANES), peak, F32) + 1e-05)
    wide = jnp.tile(scale, (1, tile_cols // LANES))
    shares, layers, depth, share = slab_ref.shape
    edge = min(share - tile_cols // shares, margin)
    share -= edge
    holders = margin // edge
    first = (height - layers * depth) // 2
    band = pl.ds(first, layers * depth)
    mid = slice(margin, margin + tile_cols)
    far_side = slice(margin + tile_cols, 2 * margin + tile_cols)
    own_band = ext_ref[1, band, mid] + sum_ref[1, band, mid] * wide + dual_ref[...]
    left_band = sum_ref[1, band, :margin] * scale
    right_band = sum_ref[1, band, far_side] * scale
    for layer in range(layers):
        rows = slice(layer * depth, (layer + 1) * depth)
        for p in range(shares):
            slab_ref[p, layer, :, :share] = own_band[rows, p * share : (p + 1) * share]
            begin = (p - shares + holders) * edge
            if p < holders:
                outgoing = left_band[rows, p * edge : (p + 1) * edge]
            elif p >= shares - holders:
                outgoing = right_band[rows, begin : begin + edge]
            else:
                outgoing = jnp.zeros((depth, edge), F32)
            slab_ref[p, layer, :, share:] = outgoing
    slab_copy = pltpu.make_async_copy(slab_ref, slab_hbm, slab_sem)
    slab_copy.start()
    part_copies = []
    for step in range(shares):
        part = lax.rem(place_ref[0] + step, shares)
        parts_ref[step, :grad_rows, :] = grad_ref[part]
        parts_ref[step, grad_rows:, :] = energy_ref[...]
        part_copies.append(
            pltpu.make_async_copy(parts_ref.at[step], parts_hbm[step], parts_sem.at[step])
        )
        part_copies[-1].start()
    for c in range(2):
        new_ref[c] = ext_ref[c, inner, mid] + sum_ref[c, inner, mid] * wide
        edge_left_ref[c] = sum_ref[c, inner, :margin] * scale
        edge_right_ref[c] = sum_ref[c, inner, far_side] * scale
    last_copies = [
        pltpu.make_async_copy(source, target, out_sem.at[k])
        for k, (source, target) in enumerate(
            (
                (new_ref, new_hbm),
                (edge_left_ref, edge_left_hbm),
                (edge_right_ref, edge_right_hbm),
            )
        )
    ]
    for copy in last_copies:
        copy.start()
    slab_copy.wait()
    for copy in part_copies + last_copies:
        copy.wait()


def patch_updates(
    rows, cols, count, place, own, left, right, probe, amplitudes, dual, shares, layers
):
    side = probe.shape[1]
    _, height, tile_cols = own.shape
    margin = left.shape[2]
    slots = amplitudes.shape[0]
    slab_rows = dual.shape[0]
    share = tile_cols // shares
    edge = min(share, margin)
    dft_a, dft_b = dft_blocks(side)
    extent = tile_cols + 2 * margin + LANES
    shape = jax.ShapeDtypeStruct
    slab_shape = (shares, layers, slab_rows // layers, share + edge)
    part_rows = 2 * side // shares
    return pl.pallas_call(
        patch_kernel,
        in_specs=[SCALARS] * 4 + [IN_HBM, ANYWHERE, ANYWHERE] + [IN_HBM] * 5,
        out_specs=[IN_HBM] * (4 + shares),
        out_shape=[
            shape((2, height, tile_cols), F32),
            shape((2, height, margin), F32),
            shape((2, height, margin), F32),
            shape(slab_shape, F32),
        ]
        + [shape((part_rows + ENERGY_ROWS, side), F32)] * shares,
        scratch_shapes=[
            VMEM(probe.shape, F32),
            VMEM(amplitudes.shape, BF16),
            VMEM(dft_a.shape, BF16),
            VMEM(dft_b.shape, BF16),
            VMEM(dual.shape, F32),
            VMEM((2, height, tile_cols), F32),
            VMEM((2, height, margin), F32),
            VMEM((2, height, margin), F32),
            VMEM(slab_shape, F32),
            VMEM((shares, part_rows + ENERGY_ROWS, side), F32),
            VMEM((2, height + SUBLANES, extent), F32),
            VMEM((2, height + SUBLANES, extent), F32),
            VMEM((shares, part_rows, side), F32),
            VMEM((ENERGY_ROWS, side), F32),
            VMEM((2 * side, side), F32),
            VMEM((2 * side, side), F32),
            VMEM((2 * side, side), BF16),
            VMEM((2 * side, side), BF16),
            VMEM((side, 2 * side), BF16),
            VMEM((side, 2 * side), BF16),
            VMEM((side, 2 * side), F32),
            VMEM((side, 2 * side), F32),
            pltpu.SemaphoreType.DMA((8,)),
            DMA,
            pltpu.SemaphoreType.DMA((shares,)),
            pltpu.SemaphoreType.DMA((3,)),
        ],
        compiler_params=pltpu.CompilerParams(vmem_limit_bytes=32 * MIB),
        cost_estimate=pl.CostEstimate(
            flops=slots * 32 * side**3,
            bytes_accessed=8 * height * tile_cols * 4,
            transcendentals=slots * side * side,
        ),
        name="patches",
    )(
        rows,
        cols,
        count,
        place,
        own,
        left,
        right,
        probe,
        amplitudes,
        jnp.asarray(dft_a),
        jnp.asarray(dft_b),
        dual,
    )


def backward_kernel(
    ids_ref, residual_hbm, weights_hbm, out_ref, residual_ref, weights_ref, turned_ref, sem, weights_sem
):
    parts, projections, depth, share = residual_ref.shape
    both = projections * depth

    def weights_copy(a):
        return pltpu.make_async_copy(
            weights_hbm.at[ids_ref[a]], weights_ref.at[a], weights_sem.at[a]
        )

    residual_copy = pltpu.make_async_copy(residual_hbm, residual_ref, sem)
    residual_copy.start()
    for a in range(projections):
        weights_copy(a).start()
    residual_copy.wait()
    for part in range(parts):
        block = residual_ref[part].astype(F32).reshape(both, share)
        turned_ref[part * share : (part + 1) * share, :] = block.T
    out_ref[...] = jnp.zeros(out_ref.shape, F32)

    @pl.loop(0, projections)
    def _(a):
        weights_copy(a).wait()
        lane = lax.broadcasted_iota(jnp.int32, turned_ref.shape, 1)
        begin = a * depth
        kept = jnp.logical_and(lane >= begin, lane < begin + depth)
        chosen = jnp.where(kept, turned_ref[...], 0.0).astype(BF16)
        out_ref[...] += dot(weights_ref[a], chosen)


def backward_sums(angle_ids, residual, proj_weights):
    _, rows, width = proj_weights.shape
    _, projections, depth, _ = residual.shape
    return pl.pallas_call(
        backward_kernel,
        in_specs=[SCALARS, ANYWHERE, IN_HBM],
        out_specs=WHOLE,
        out_shape=jax.ShapeDtypeStruct((rows, projections * depth), F32),
        scratch_shapes=[
            VMEM(residual.shape, BF16),
            VMEM((projections, rows, width), BF16),
            VMEM((width, projections * depth), F32),
            DMA,
            pltpu.SemaphoreType.DMA((projections,)),
        ],
        compiler_params=pltpu.CompilerParams(vmem_limit_bytes=32 * MIB),
        cost_estimate=pl.CostEstimate(
            flops=2 * rows * width * projections * projections * depth,
            bytes_accessed=projections * rows * width * 2,
            transcendentals=0,
        ),
        name="backward",
    )(angle_ids, residual, proj_weights)


def update_kernel(
    ids_ref,
    sums_ref,
    rays_hbm,
    volume_hbm,
    object_hbm,
    from_left_hbm,
    from_right_hbm,
    out_hbm,
    new_object_hbm,
    rays_ref,
    stack_ref,
    spread_ref,
    volume_ref,
    done_ref,
    cells_ref,
    left_ref,
    right_ref,
    rays_sem,
    volume_sem,
    out_sem,
    object_sem,
):
    depth = volume_ref.shape[0]
    slots = done_ref.shape[0]
    margin = left_ref.shape[2]
    tile_cols = cells_ref.shape[2]
    width = rays_ref.shape[1]
    projections = sums_ref.shape[1] // depth
    both = sums_ref.shape[1]

    def volume_copy(z):
        return pltpu.make_async_copy(volume_hbm.at[z], volume_ref.at[z], volume_sem.at[z])

    def out_copy(z):
        slot = lax.rem(z, slots)
        return pltpu.make_async_copy(done_ref.at[slot], out_hbm.at[z], out_sem.at[slot])

    rays_copy = pltpu.make_async_copy(rays_hbm, rays_ref, rays_sem)
    rays_copy.start()
    for z in range(min(AHEAD, depth)):
        volume_copy(z).start()
    copies = [
        pltpu.make_async_copy(source, target, object_sem.at[k])
        for k, (source, target) in enumerate(
            ((object_hbm, cells_ref), (from_left_hbm, left_ref), (from_right_hbm, right_ref))
        )
    ]
    for copy in copies:
        copy.start()
    high, low = split_bf16(sums_ref[...])
    stack_ref[...] = jnp.concatenate([high, low, high, low], axis=1)
    rays_copy.wait()
    rows = [
        jnp.broadcast_to(rays_ref[pl.ds(ids_ref[a], 1), :], (depth, width))
        for a in range(projections)
    ]
    high, low = split_bf16(jnp.concatenate(rows, axis=0))
    for place, block in enumerate((high, high, low, low)):
        spread_ref[place * both : (place + 1) * both, :] = block.astype(BF16)

    @pl.loop(0, depth)
    def _(z):
        volume_copy(z).wait()

        @pl.when(z + AHEAD < depth)
        def _():
            volume_copy(z + AHEAD).start()

        @pl.when(z >= slots)
        def _():
            out_copy(z - slots).wait()

        lane = lax.broadcasted_iota(jnp.int32, stack_ref.shape, 1)
        kept = lax.rem(lane, depth) == z
        chosen = jnp.where(kept, stack_ref[...], 0.0).astype(BF16)
        done_ref[lax.rem(z, slots)] = volume_ref[z] - tomo_step * dot(chosen, spread_ref[...])
        out_copy(z).start()

    for copy in copies:
        copy.wait()
    cells_ref[:, :, :margin] += left_ref[...]
    cells_ref[:, :, tile_cols - margin :] += right_ref[...]
    object_copy = pltpu.make_async_copy(cells_ref, new_object_hbm, object_sem.at[0])
    object_copy.start()
    for z in range(max(depth - slots, 0), depth):
        out_copy(z).wait()
    object_copy.wait()


def volume_update(angle_ids, sums, rays, volume, partial_object, from_left, from_right):
    depth, rows, width = volume.shape
    slots = min(4, depth)
    return pl.pallas_call(
        update_kernel,
        in_specs=[SCALARS, WHOLE] + [IN_HBM] * 3 + [ANYWHERE] * 2,
        out_specs=[IN_HBM] * 2,
        out_shape=[
            jax.ShapeDtypeStruct(volume.shape, F32),
            jax.ShapeDtypeStruct(partial_object.shape, F32),
        ],
        scratch_shapes=[
            VMEM(rays.shape, F32),
            VMEM((rows, 4 * sums.shape[1]), F32),
            VMEM((4 * sums.shape[1], width), BF16),
            VMEM(volume.shape, F32),
            VMEM((slots, rows, width), F32),
            VMEM(partial_object.shape, F32),
            VMEM(from_left.shape, F32),
            VMEM(from_right.shape, F32),
            DMA,
            pltpu.SemaphoreType.DMA((depth,)),
            pltpu.SemaphoreType.DMA((slots,)),
            pltpu.SemaphoreType.DMA((3,)),
        ],
        compiler_params=pltpu.CompilerParams(vmem_limit_bytes=48 * MIB),
        cost_estimate=pl.CostEstimate(
            flops=8 * rows * width * sums.shape[1] * depth,
            bytes_accessed=2 * depth * rows * width * 4,
            transcendentals=0,
        ),
        name="update",
    )(angle_ids, sums, rays, volume, partial_object, from_left, from_right)


def gather_parts_kernel(group, *refs):
    *given, out_hbm, out_ref, sem = refs
    total = given[0][...]
    for ref in given[1:]:
        total = total + ref[...]
    _, rows, _ = out_ref.shape
    rows -= ENERGY_ROWS
    for k in range(group):
        out_ref[k, :rows, :] = total[k * rows : (k + 1) * rows]
        out_ref[k, rows:, :] = total[group * rows :]
    copy = pltpu.make_async_copy(out_ref, out_hbm, sem)
    copy.start()
    copy.wait()


def gather_parts(given, group):
    total_rows, side = given[0].shape
    rows = (total_rows - ENERGY_ROWS) // group + ENERGY_ROWS
    return pl.pallas_call(
        functools.partial(gather_parts_kernel, group),
        in_specs=[WHOLE] * len(given),
        out_specs=IN_HBM,
        out_shape=jax.ShapeDtypeStruct((group, rows, side), F32),
        scratch_shapes=[VMEM((group, rows, side), F32), DMA],
        name="probe_parts",
    )(*given)


def probe_rows_kernel(given_ref, probe_ref, out_hbm, out_ref, sem):
    group, rows, side = given_ref.shape
    rows -= ENERGY_ROWS
    total = given_ref[0]
    for k in range(1, group):
        total = total + given_ref[k]
    energy = jnp.sum(total[rows:], keepdims=True) / (side * side)
    new_rows = probe_ref[...] + total[:rows] / (energy + 1e-05)
    for k in range(group):
        out_ref[k] = new_rows
    copy = pltpu.make_async_copy(out_ref, out_hbm, sem)
    copy.start()
    copy.wait()


def probe_rows(given, own_rows):
    group, rows, side = given.shape
    shape = (group, rows - ENERGY_ROWS, side)
    return pl.pallas_call(
        probe_rows_kernel,
        in_specs=[WHOLE] * 2,
        out_specs=IN_HBM,
        out_shape=jax.ShapeDtypeStruct(shape, F32),
        scratch_shapes=[VMEM(shape, F32), DMA],
        name="probe_rows",
    )(given, own_rows)


def turned(value, axis, steps):
    count = lax.axis_size(axis)
    return lax.ppermute(value, axis, [(k, (k + steps) % count) for k in range(count)])


def on_device(
    object_field,
    probe_field,
    amplitudes,
    pos_rows,
    pos_cols,
    counts,
    admm_dual,
    volume,
    proj_weights,
    ray_weights,
    angle_ids,
):
    margin = probe_field.shape[1] // 2
    own = object_field[0]
    tile_cols = own.shape[2]
    flat_axes = ("tile", "proj")
    plane = lax.axis_size("tile") * lax.axis_size("proj")
    proj_count = lax.axis_size("proj")
    layers = lax.axis_size("cuts")
    from_left = shifted(own[:, :, tile_cols - margin :], "tile", 1)
    from_right = shifted(own[:, :, :margin], "tile", -1)
    forward = forward_parts(angle_ids, volume, proj_weights, ray_weights, plane)
    arrived = lax.all_to_all(forward, flat_axes, 0, 0, tiled=True)
    place = lax.axis_index("proj")
    partial_object, edge_left, edge_right, slab, *grad_parts = patch_updates(
        pos_rows[0, 0],
        pos_cols[0, 0],
        counts[0],
        place[None],
        own,
        from_left,
        from_right,
        probe_field,
        amplitudes[0, 0],
        admm_dual[0],
        proj_count,
        layers,
    )

    share = tile_cols // proj_count
    edge = slab.shape[3] - share
    holders = margin // edge
    pieces = slab.reshape(proj_count * layers, *slab.shape[2:])
    pieces = lax.all_to_all(pieces, ("proj", "cuts"), 0, 0, tiled=True)
    pairs = []
    for tile in range(lax.axis_size("tile") - 1):
        for k in range(holders):
            lower = tile * proj_count + proj_count - holders + k
            upper = (tile + 1) * proj_count + k
            pairs += [(lower, upper), (upper, lower)]
    grads_in = lax.ppermute(pieces[:, :, share:], flat_axes, pairs)
    at_start = jnp.pad(grads_in, ((0, 0), (0, 0), (0, share - edge)))
    at_end = jnp.pad(grads_in, ((0, 0), (0, 0), (share - edge, 0)))
    target = pieces[:, :, :share] + jnp.where(place < holders, at_start, at_end)
    residual = (jnp.sum(arrived, axis=0) - target).astype(BF16)
    copies = jnp.broadcast_to(residual[None], (plane, *residual.shape))

    group_axes = ("tile", "cuts")
    group = lax.axis_size("tile") * layers
    given = [grad_parts[0]]
    for step in range(1, proj_count):
        given.append(turned(grad_parts[step], "proj", step))
    by_receiver = gather_parts(given, group)
    copies, by_receiver = lax.optimization_barrier((copies, by_receiver))
    residual = lax.all_to_all(copies, flat_axes, 0, 0, tiled=True)
    received = lax.all_to_all(by_receiver, group_axes, 0, 0, tiled=True)

    residual, edge_left, edge_right = lax.optimization_barrier((residual, edge_left, edge_right))
    edge_from_right = shifted(edge_left, "tile", -1)
    edge_from_left = shifted(edge_right, "tile", 1)
    back_sums = backward_sums(angle_ids, residual, proj_weights)

    back_sums, received = lax.optimization_barrier((back_sums, received))
    side = probe_field.shape[1]
    rows = received.shape[1] - ENERGY_ROWS
    begin = (place * group + lax.axis_index(group_axes)) * rows
    own_rows = lax.dynamic_slice(
        probe_field.reshape(2 * side, side), (begin, jnp.zeros((), begin.dtype)), (rows, side)
    )
    new_rows = lax.all_to_all(probe_rows(received, own_rows), group_axes, 0, 0, tiled=True)

    new_volume, new_object = volume_update(
        angle_ids,
        back_sums,
        ray_weights,
        volume,
        partial_object,
        edge_from_left,
        edge_from_right,
    )
    new_volume, new_rows = lax.optimization_barrier((new_volume, new_rows))
    new_rows = new_rows.reshape(group * rows, side)
    if proj_count == 2:
        other = turned(new_rows, "proj", 1)
        first = place == 0
        new_probe = jnp.concatenate(
            [jnp.where(first, new_rows, other), jnp.where(first, other, new_rows)], axis=0
        )
    else:
        new_probe = lax.all_gather(new_rows, "proj", axis=0, tiled=True)
    return (new_object[None], new_probe.reshape(2, side, side), new_volume)


def solution(mesh):
    in_specs = (
        P(("proj", "cuts"), None, None, "tile"),
        P(),
        P(("proj", "cuts"), "tile", None, None, None),
        P(("proj", "cuts"), "tile", None),
        P(("proj", "cuts"), "tile", None),
        P(("proj", "cuts"), "tile"),
        P(("proj", "cuts"), None, "tile"),
        P("cuts", ("tile", "proj"), None),
        P(None, ("tile", "proj"), None),
        P(),
        P(),
    )
    out_specs = (P(("proj", "cuts"), None, None, "tile"), P(), P("cuts", ("tile", "proj"), None))
    return jax.shard_map(
        on_device, mesh=mesh, in_specs=in_specs, out_specs=out_specs, check_vma=False
    )
```

```python
import functools
import math

import jax
import jax.numpy as jnp
import numpy as np
from jax import lax
from jax.experimental import pallas as pl
from jax.experimental.pallas import tpu as pltpu
from jax.sharding import PartitionSpec as P

VMEM_LIMIT = 60 * 1024 * 1024
VMEM = pltpu.VMEM
F32 = jnp.float32
BF16 = jnp.bfloat16
LANES = 128
SUBLANES = 8
AHEAD = 6
ANYWHERE = pl.BlockSpec(memory_space=pl.ANY)
WHOLE = pl.BlockSpec(memory_space=pltpu.VMEM)
SCALARS = pl.BlockSpec(memory_space=pltpu.SMEM)
DMA = pltpu.SemaphoreType.DMA

tomo_step = 1.0


def shifted(value, axis, steps):
    count = lax.axis_size(axis)
    leading, last = (max(0, -steps), min(count, count - steps))
    return lax.ppermute(value, axis, [(source, source + steps) for source in range(leading, last)])


def dft_blocks(side):
    indices = np.arange(side)
    products = (indices[:, None] * indices[None, :]) % side
    phase = products.astype(np.float32) * np.float32(2.0 * math.pi / side)
    norm = np.float32(1.0 / math.sqrt(side))
    real = np.cos(phase).astype(np.float32) * norm
    imag = -np.sin(phase).astype(np.float32) * norm
    left = np.block([[real, -imag], [imag, real]])
    right = np.block([[real, imag], [-imag, real]])
    return left.astype(jnp.bfloat16), right.astype(jnp.bfloat16)


def dot(left, right):
    return jnp.dot(left, right, preferred_element_type=F32)


def split_bf16(values):
    high = values.astype(BF16).astype(F32)
    low = (values - high).astype(BF16).astype(F32)
    return high, low


def forward_kernel(
    ids_ref,
    rays_hbm,
    volume_hbm,
    weights_hbm,
    out_hbm,
    rays_ref,
    volume_ref,
    weights_ref,
    out_ref,
    table_ref,
    sums_ref,
    rays_sem,
    volume_sem,
    weights_sem,
    out_sem,
):
    depth, projections, _ = sums_ref.shape
    width, lanes = table_ref.shape
    parts, _, _, share = out_ref.shape

    def volume_copy(z):
        return pltpu.make_async_copy(volume_hbm.at[z], volume_ref.at[z], volume_sem.at[z])

    def weights_copy(a):
        return pltpu.make_async_copy(
            weights_hbm.at[ids_ref[a]], weights_ref.at[a], weights_sem.at[a]
        )

    def out_copy(a):
        return pltpu.make_async_copy(out_ref.at[:, a], out_hbm.at[:, a], out_sem.at[a])

    rays_copy = pltpu.make_async_copy(rays_hbm, rays_ref, rays_sem)
    rays_copy.start()
    for z in range(min(AHEAD, depth)):
        volume_copy(z).start()
    for a in range(min(max(AHEAD - depth, 0), projections)):
        weights_copy(a).start()

    rays_copy.wait()
    rows = jnp.concatenate([rays_ref[pl.ds(ids_ref[a], 1), :] for a in range(projections)], axis=0)
    high, low = split_bf16(rows)
    stacked = [high, low]
    if lanes > 2 * projections:
        stacked.append(jnp.zeros((lanes - 2 * projections, width), F32))
    table_ref[...] = jnp.concatenate(stacked, axis=0).T.astype(BF16)

    @pl.loop(0, depth)
    def _(z):
        volume_copy(z).wait()

        @pl.when(z + AHEAD < depth)
        def _():
            volume_copy(z + AHEAD).start()

        @pl.when(jnp.logical_and(z + AHEAD >= depth, z + AHEAD - depth < projections))
        def _():
            weights_copy(z + AHEAD - depth).start()

        piece = min(512, width)
        first = second = None
        for k in range(0, width, piece):
            block = volume_ref[z, :, k : k + piece]
            high = block.astype(BF16)
            low = (block - high.astype(F32)).astype(BF16)
            of_high = dot(high, table_ref[k : k + piece, :])
            of_low = dot(low, table_ref[k : k + piece, :])
            first = of_high if first is None else first + of_high
            second = of_low if second is None else second + of_low
        first = first.T
        second = second.T
        sums_ref[z] = first[:projections] + (
            first[projections : 2 * projections] + second[:projections]
        )

    @pl.loop(0, projections)
    def _(a):
        weights_copy(a).wait()

        @pl.when(a + AHEAD < projections)
        def _():
            weights_copy(a + AHEAD).start()

        rows = sums_ref[:, pl.ds(a, 1), :].reshape(depth, sums_ref.shape[2])
        result = dot(rows.astype(BF16), weights_ref[a])
        for part in range(parts):
            out_ref[part, a] = result[:, part * share : (part + 1) * share]
        out_copy(a).start()

    @pl.loop(0, projections)
    def _(a):
        out_copy(a).wait()


def forward_parts(angle_ids, volume, proj_weights, ray_weights, parts):
    depth, rows, width = volume.shape
    projections = angle_ids.shape[0]
    lanes = -(-2 * projections // LANES) * LANES
    share = width // parts
    return pl.pallas_call(
        forward_kernel,
        in_specs=[SCALARS] + [ANYWHERE] * 3,
        out_specs=ANYWHERE,
        out_shape=jax.ShapeDtypeStruct((parts, projections, depth, share), F32),
        scratch_shapes=[
            VMEM(ray_weights.shape, F32),
            VMEM(volume.shape, F32),
            VMEM((projections, rows, width), BF16),
            VMEM((parts, projections, depth, share), F32),
            VMEM((width, lanes), BF16),
            VMEM((depth, projections, rows), F32),
            DMA,
            pltpu.SemaphoreType.DMA((depth,)),
            pltpu.SemaphoreType.DMA((projections,)),
            pltpu.SemaphoreType.DMA((projections,)),
        ],
        compiler_params=pltpu.CompilerParams(vmem_limit_bytes=VMEM_LIMIT),
        cost_estimate=pl.CostEstimate(
            flops=4 * depth * rows * width * lanes,
            bytes_accessed=depth * rows * width * 4 + projections * rows * width * 2,
            transcendentals=0,
        ),
        name="forward",
    )(angle_ids, ray_weights, volume, proj_weights)


def placed(values, down, across):
    rows, cols = values.shape
    tall = jnp.concatenate([values, jnp.zeros((SUBLANES, cols), F32)], axis=0)
    tall = pltpu.roll(tall, down, axis=0)
    wide = jnp.concatenate([tall, jnp.zeros((rows + SUBLANES, LANES), F32)], axis=1)
    return pltpu.roll(wide, across, axis=1)


def patch_kernel(
    rows_ref,
    cols_ref,
    count_ref,
    own_hbm,
    left_hbm,
    right_hbm,
    probe_hbm,
    amp_hbm,
    dft_a_hbm,
    dft_b_hbm,
    dual_hbm,
    new_hbm,
    edge_left_hbm,
    edge_right_hbm,
    slab_hbm,
    parts_hbm,
    probe_ref,
    amp_ref,
    dft_a_ref,
    dft_b_ref,
    dual_ref,
    new_ref,
    edge_left_ref,
    edge_right_ref,
    slab_ref,
    parts_ref,
    ext_ref,
    sum_ref,
    grad_ref,
    energy_ref,
    patch_a_ref,
    patch_b_ref,
    wave_a_ref,
    wave_b_ref,
    half_a_ref,
    half_b_ref,
    far_a_ref,
    far_b_ref,
    in_sem,
    slab_sem,
    parts_sem,
    out_sem,
):
    slots = amp_ref.shape[0]
    side = probe_ref.shape[1]
    _, height, margin = edge_left_ref.shape
    tile_cols = new_ref.shape[2]
    window = side + LANES
    chunk = 32
    tall = chunk + SUBLANES
    inner = pl.ds(0, height)

    copies = [
        pltpu.make_async_copy(source, target, in_sem.at[k])
        for k, (source, target) in enumerate(
            (
                (left_hbm, ext_ref.at[:, inner, pl.ds(0, margin)]),
                (own_hbm, ext_ref.at[:, inner, pl.ds(margin, tile_cols)]),
                (right_hbm, ext_ref.at[:, inner, pl.ds(margin + tile_cols, margin)]),
                (probe_hbm, probe_ref),
                (dft_a_hbm, dft_a_ref),
                (dft_b_hbm, dft_b_ref),
                (amp_hbm, amp_ref),
                (dual_hbm, dual_ref),
            )
        )
    ]
    for copy in copies:
        copy.start()
    sum_ref[...] = jnp.zeros(sum_ref.shape, F32)
    grad_ref[...] = jnp.zeros(grad_ref.shape, F32)
    energy_ref[...] = jnp.zeros(energy_ref.shape, F32)
    for copy in copies:
        copy.wait()

    def pair_step(pair, carry):
        chains = []
        for k, refs in enumerate(
            (
                (patch_a_ref, wave_a_ref, half_a_ref, far_a_ref),
                (patch_b_ref, wave_b_ref, half_b_ref, far_b_ref),
            )
        ):
            slot = jnp.minimum(2 * pair + k, slots - 1)
            live = (2 * pair + k < count_ref[0]).astype(F32)
            row = rows_ref[slot]
            col = cols_ref[slot]
            lane = lax.rem(col, LANES)
            notch = lax.rem(row, SUBLANES)
            base = pl.multiple_of(col - lane, LANES)
            top = pl.multiple_of(row - notch, SUBLANES)
            chains.append((slot, live, lane, notch, base, top, *refs))
        for slot, live, lane, notch, base, top, patch_ref, wave_ref, half_ref, far_ref in chains:
            back_shift = lax.rem(window - lane, window)
            up_shift = lax.rem(tall - notch, tall)
            for r in range(0, side, chunk):
                cells = pl.ds(top + r, tall)
                here = slice(r, r + chunk)
                below = slice(side + r, side + r + chunk)
                x_re = pltpu.roll(ext_ref[0, cells, pl.ds(base, window)], back_shift, axis=1)
                x_im = pltpu.roll(ext_ref[1, cells, pl.ds(base, window)], back_shift, axis=1)
                x_re = pltpu.roll(x_re[:, :side], up_shift, axis=0)[:chunk]
                x_im = pltpu.roll(x_im[:, :side], up_shift, axis=0)[:chunk]
                p_re = probe_ref[0, here, :]
                p_im = probe_ref[1, here, :]
                patch_ref[here, :] = x_re
                patch_ref[below, :] = x_im
                wave_ref[here, :] = (p_re * x_re - p_im * x_im).astype(BF16)
                wave_ref[below, :] = (p_re * x_im + p_im * x_re).astype(BF16)
                power = x_re * x_re + x_im * x_im
                energy_ref[...] += live * jnp.sum(
                    power.reshape(chunk // SUBLANES, SUBLANES, side), axis=0
                )
        for *_, wave_ref, half_ref, far_ref in chains:
            half_ref[:, :side] = dot(dft_a_ref[:side, :], wave_ref[...]).astype(BF16)
            half_ref[:, side:] = dot(dft_a_ref[side:, :], wave_ref[...]).astype(BF16)
        for *_, half_ref, far_ref in chains:
            far_ref[...] = dot(half_ref[...], dft_b_ref[...])
        for slot, live, *_, wave_ref, half_ref, far_ref in chains:
            for r in range(0, side, chunk):
                here = slice(r, r + chunk)
                below = slice(side + r, side + r + chunk)
                f_re = far_ref[here, :side]
                f_im = far_ref[here, side:]
                inverse = lax.rsqrt(f_re * f_re + f_im * f_im + 0.25)
                factor = amp_ref[slot, here, :].astype(F32) * inverse - 1.0
                wave_ref[here, :] = (f_re * factor).astype(BF16)
                wave_ref[below, :] = (f_im * factor).astype(BF16)
        for *_, wave_ref, half_ref, far_ref in chains:
            half_ref[:, :side] = dot(dft_b_ref[:side, :], wave_ref[...]).astype(BF16)
            half_ref[:, side:] = dot(dft_b_ref[side:, :], wave_ref[...]).astype(BF16)
        for *_, half_ref, far_ref in chains:
            far_ref[...] = dot(half_ref[...], dft_a_ref[...])
        for slot, live, lane, notch, base, top, patch_ref, wave_ref, half_ref, far_ref in chains:
            for r in range(0, side, chunk):
                cells = pl.ds(top + r, tall)
                here = slice(r, r + chunk)
                below = slice(side + r, side + r + chunk)
                b_re = live * far_ref[here, :side]
                b_im = live * far_ref[here, side:]
                p_re = probe_ref[0, here, :]
                p_im = probe_ref[1, here, :]
                x_re = patch_ref[here, :]
                x_im = patch_ref[below, :]
                o_re = p_re * b_re + p_im * b_im
                o_im = p_re * b_im - p_im * b_re
                sum_ref[0, cells, pl.ds(base, window)] += placed(o_re, notch, lane)
                sum_ref[1, cells, pl.ds(base, window)] += placed(o_im, notch, lane)
                grad_ref[here, :] += x_re * b_re + x_im * b_im
                grad_ref[below, :] += x_re * b_im - x_im * b_re
        return carry

    lax.fori_loop(0, lax.div(count_ref[0] + 1, 2), pair_step, 0)

    p_re = probe_ref[0]
    p_im = probe_ref[1]
    peak = jnp.max(p_re * p_re + p_im * p_im)
    scale = 1.0 / (jnp.full((1, LANES), peak, F32) + 1e-05)
    wide = jnp.tile(scale, (1, tile_cols // LANES))
    shares, layers, depth, share = slab_ref.shape
    edge = min(share - tile_cols // shares, margin)
    share -= edge
    holders = margin // edge
    first = (height - layers * depth) // 2
    band = pl.ds(first, layers * depth)
    mid = slice(margin, margin + tile_cols)
    far_side = slice(margin + tile_cols, 2 * margin + tile_cols)
    own_band = ext_ref[1, band, mid] + sum_ref[1, band, mid] * wide + dual_ref[...]
    left_band = sum_ref[1, band, :margin] * scale
    right_band = sum_ref[1, band, far_side] * scale
    for layer in range(layers):
        rows = slice(layer * depth, (layer + 1) * depth)
        for p in range(shares):
            slab_ref[p, layer, :, :share] = own_band[rows, p * share : (p + 1) * share]
            begin = (p - shares + holders) * edge
            if p < holders:
                outgoing = left_band[rows, p * edge : (p + 1) * edge]
            elif p >= shares - holders:
                outgoing = right_band[rows, begin : begin + edge]
            else:
                outgoing = jnp.zeros((depth, edge), F32)
            slab_ref[p, layer, :, share:] = outgoing
    slab_copy = pltpu.make_async_copy(slab_ref, slab_hbm, slab_sem)
    slab_copy.start()
    receivers, part_rows, _ = parts_ref.shape
    blocks = side // LANES
    taken = (part_rows - SUBLANES) // blocks
    energy = energy_ref[:, :LANES]
    for block in range(1, blocks):
        energy = energy + energy_ref[:, block * LANES : (block + 1) * LANES]
    for k in range(receivers):
        for block in range(blocks):
            parts_ref[k, block * taken : (block + 1) * taken, :] = grad_ref[
                k * taken : (k + 1) * taken, block * LANES : (block + 1) * LANES
            ]
        parts_ref[k, blocks * taken :, :] = energy
    parts_copy = pltpu.make_async_copy(parts_ref, parts_hbm, parts_sem)
    parts_copy.start()
    for c in range(2):
        new_ref[c] = ext_ref[c, inner, mid] + sum_ref[c, inner, mid] * wide
        edge_left_ref[c] = sum_ref[c, inner, :margin] * scale
        edge_right_ref[c] = sum_ref[c, inner, far_side] * scale
    last_copies = [
        pltpu.make_async_copy(source, target, out_sem.at[k])
        for k, (source, target) in enumerate(
            (
                (new_ref, new_hbm),
                (edge_left_ref, edge_left_hbm),
                (edge_right_ref, edge_right_hbm),
            )
        )
    ]
    for copy in last_copies:
        copy.start()
    slab_copy.wait()
    parts_copy.wait()
    for copy in last_copies:
        copy.wait()


def patch_updates(
    rows, cols, count, own, left, right, probe, amplitudes, dual, shares, layers, receivers
):
    side = probe.shape[1]
    _, height, tile_cols = own.shape
    margin = left.shape[2]
    slots = amplitudes.shape[0]
    slab_rows = dual.shape[0]
    share = tile_cols // shares
    edge = min(share, margin)
    dft_a, dft_b = dft_blocks(side)
    extent = tile_cols + 2 * margin + LANES
    shape = jax.ShapeDtypeStruct
    slab_shape = (shares, layers, slab_rows // layers, share + edge)
    part_shape = (receivers, 2 * side // receivers * (side // LANES) + SUBLANES, LANES)
    return pl.pallas_call(
        patch_kernel,
        in_specs=[SCALARS] * 3 + [ANYWHERE] * 8,
        out_specs=[ANYWHERE] * 5,
        out_shape=[
            shape((2, height, tile_cols), F32),
            shape((2, height, margin), F32),
            shape((2, height, margin), F32),
            shape(slab_shape, F32),
            shape(part_shape, F32),
        ],
        scratch_shapes=[
            VMEM(probe.shape, F32),
            VMEM(amplitudes.shape, BF16),
            VMEM(dft_a.shape, BF16),
            VMEM(dft_b.shape, BF16),
            VMEM(dual.shape, F32),
            VMEM((2, height, tile_cols), F32),
            VMEM((2, height, margin), F32),
            VMEM((2, height, margin), F32),
            VMEM(slab_shape, F32),
            VMEM(part_shape, F32),
            VMEM((2, height + SUBLANES, extent), F32),
            VMEM((2, height + SUBLANES, extent), F32),
            VMEM((2 * side, side), F32),
            VMEM((SUBLANES, side), F32),
            VMEM((2 * side, side), F32),
            VMEM((2 * side, side), F32),
            VMEM((2 * side, side), BF16),
            VMEM((2 * side, side), BF16),
            VMEM((side, 2 * side), BF16),
            VMEM((side, 2 * side), BF16),
            VMEM((side, 2 * side), F32),
            VMEM((side, 2 * side), F32),
            pltpu.SemaphoreType.DMA((8,)),
            DMA,
            DMA,
            pltpu.SemaphoreType.DMA((3,)),
        ],
        compiler_params=pltpu.CompilerParams(vmem_limit_bytes=VMEM_LIMIT),
        cost_estimate=pl.CostEstimate(
            flops=slots * 32 * side**3,
            bytes_accessed=8 * height * tile_cols * 4,
            transcendentals=slots * side * side,
        ),
        name="patches",
    )(
        rows,
        cols,
        count,
        own,
        left,
        right,
        probe,
        amplitudes,
        jnp.asarray(dft_a),
        jnp.asarray(dft_b),
        dual,
    )


def backward_kernel(
    ids_ref, residual_hbm, weights_hbm, out_ref, residual_ref, weights_ref, turned_ref, sem, weights_sem
):
    parts, projections, depth, share = residual_ref.shape
    both = projections * depth

    def weights_copy(a):
        return pltpu.make_async_copy(
            weights_hbm.at[ids_ref[a]], weights_ref.at[a], weights_sem.at[a]
        )

    residual_copy = pltpu.make_async_copy(residual_hbm, residual_ref, sem)
    residual_copy.start()
    for a in range(projections):
        weights_copy(a).start()
    residual_copy.wait()
    for part in range(parts):
        block = residual_ref[part].astype(F32).reshape(both, share)
        turned_ref[part * share : (part + 1) * share, :] = block.T
    out_ref[...] = jnp.zeros(out_ref.shape, F32)

    @pl.loop(0, projections)
    def _(a):
        weights_copy(a).wait()
        lane = lax.broadcasted_iota(jnp.int32, turned_ref.shape, 1)
        begin = a * depth
        kept = jnp.logical_and(lane >= begin, lane < begin + depth)
        chosen = jnp.where(kept, turned_ref[...], 0.0).astype(BF16)
        out_ref[...] += dot(weights_ref[a], chosen)


def backward_sums(angle_ids, residual, proj_weights):
    _, rows, width = proj_weights.shape
    _, projections, depth, _ = residual.shape
    return pl.pallas_call(
        backward_kernel,
        in_specs=[SCALARS, ANYWHERE, ANYWHERE],
        out_specs=WHOLE,
        out_shape=jax.ShapeDtypeStruct((rows, projections * depth), F32),
        scratch_shapes=[
            VMEM(residual.shape, BF16),
            VMEM((projections, rows, width), BF16),
            VMEM((width, projections * depth), F32),
            DMA,
            pltpu.SemaphoreType.DMA((projections,)),
        ],
        compiler_params=pltpu.CompilerParams(vmem_limit_bytes=VMEM_LIMIT),
        cost_estimate=pl.CostEstimate(
            flops=2 * rows * width * projections * projections * depth,
            bytes_accessed=projections * rows * width * 2,
            transcendentals=0,
        ),
        name="backward",
    )(angle_ids, residual, proj_weights)


def update_kernel(
    ids_ref,
    sums_ref,
    rays_hbm,
    volume_hbm,
    object_hbm,
    from_left_hbm,
    from_right_hbm,
    out_hbm,
    new_object_hbm,
    rays_ref,
    stack_ref,
    spread_ref,
    volume_ref,
    done_ref,
    cells_ref,
    left_ref,
    right_ref,
    rays_sem,
    volume_sem,
    out_sem,
    object_sem,
):
    depth = volume_ref.shape[0]
    slots = done_ref.shape[0]
    margin = left_ref.shape[2]
    tile_cols = cells_ref.shape[2]
    width = rays_ref.shape[1]
    projections = sums_ref.shape[1] // depth
    both = sums_ref.shape[1]

    def volume_copy(z):
        return pltpu.make_async_copy(volume_hbm.at[z], volume_ref.at[z], volume_sem.at[z])

    def out_copy(z):
        slot = lax.rem(z, slots)
        return pltpu.make_async_copy(done_ref.at[slot], out_hbm.at[z], out_sem.at[slot])

    rays_copy = pltpu.make_async_copy(rays_hbm, rays_ref, rays_sem)
    rays_copy.start()
    for z in range(min(AHEAD, depth)):
        volume_copy(z).start()
    copies = [
        pltpu.make_async_copy(source, target, object_sem.at[k])
        for k, (source, target) in enumerate(
            ((object_hbm, cells_ref), (from_left_hbm, left_ref), (from_right_hbm, right_ref))
        )
    ]
    for copy in copies:
        copy.start()
    high, low = split_bf16(sums_ref[...])
    stack_ref[...] = jnp.concatenate([high, low, high, low], axis=1)
    rays_copy.wait()
    rows = [
        jnp.broadcast_to(rays_ref[pl.ds(ids_ref[a], 1), :], (depth, width))
        for a in range(projections)
    ]
    high, low = split_bf16(jnp.concatenate(rows, axis=0))
    for place, block in enumerate((high, high, low, low)):
        spread_ref[place * both : (place + 1) * both, :] = block.astype(BF16)

    @pl.loop(0, depth)
    def _(z):
        volume_copy(z).wait()

        @pl.when(z + AHEAD < depth)
        def _():
            volume_copy(z + AHEAD).start()

        @pl.when(z >= slots)
        def _():
            out_copy(z - slots).wait()

        lane = lax.broadcasted_iota(jnp.int32, stack_ref.shape, 1)
        kept = lax.rem(lane, depth) == z
        chosen = jnp.where(kept, stack_ref[...], 0.0).astype(BF16)
        done_ref[lax.rem(z, slots)] = volume_ref[z] - tomo_step * dot(chosen, spread_ref[...])
        out_copy(z).start()

    for copy in copies:
        copy.wait()
    cells_ref[:, :, :margin] += left_ref[...]
    cells_ref[:, :, tile_cols - margin :] += right_ref[...]
    object_copy = pltpu.make_async_copy(cells_ref, new_object_hbm, object_sem.at[0])
    object_copy.start()
    for z in range(max(depth - slots, 0), depth):
        out_copy(z).wait()
    object_copy.wait()


def volume_update(angle_ids, sums, rays, volume, partial_object, from_left, from_right):
    depth, rows, width = volume.shape
    slots = min(4, depth)
    return pl.pallas_call(
        update_kernel,
        in_specs=[SCALARS, WHOLE] + [ANYWHERE] * 3 + [ANYWHERE] * 2,
        out_specs=[ANYWHERE] * 2,
        out_shape=[
            jax.ShapeDtypeStruct(volume.shape, F32),
            jax.ShapeDtypeStruct(partial_object.shape, F32),
        ],
        scratch_shapes=[
            VMEM(rays.shape, F32),
            VMEM((rows, 4 * sums.shape[1]), F32),
            VMEM((4 * sums.shape[1], width), BF16),
            VMEM(volume.shape, F32),
            VMEM((slots, rows, width), F32),
            VMEM(partial_object.shape, F32),
            VMEM(from_left.shape, F32),
            VMEM(from_right.shape, F32),
            DMA,
            pltpu.SemaphoreType.DMA((depth,)),
            pltpu.SemaphoreType.DMA((slots,)),
            pltpu.SemaphoreType.DMA((3,)),
        ],
        compiler_params=pltpu.CompilerParams(vmem_limit_bytes=VMEM_LIMIT),
        cost_estimate=pl.CostEstimate(
            flops=8 * rows * width * sums.shape[1] * depth,
            bytes_accessed=2 * depth * rows * width * 4,
            transcendentals=0,
        ),
        name="update",
    )(angle_ids, sums, rays, volume, partial_object, from_left, from_right)


def probe_rows_kernel(given_ref, out_hbm, out_ref, sem):
    group, rows, _ = given_ref.shape
    taken, side = out_ref.shape[1:]
    total = given_ref[0]
    for k in range(1, group):
        total = total + given_ref[k]
    energy = jnp.sum(total[rows - SUBLANES :], keepdims=True) / (side * side)
    steps = total[: rows - SUBLANES] / (energy + 1e-05)
    steps = jnp.concatenate(
        [steps[k * taken : (k + 1) * taken] for k in range(side // LANES)], axis=1
    )
    for k in range(group):
        out_ref[k] = steps
    copy = pltpu.make_async_copy(out_ref, out_hbm, sem)
    copy.start()
    copy.wait()


def probe_rows(given, side):
    group, rows, _ = given.shape
    shape = (group, (rows - SUBLANES) * LANES // side, side)
    return pl.pallas_call(
        probe_rows_kernel,
        in_specs=[WHOLE],
        out_specs=ANYWHERE,
        out_shape=jax.ShapeDtypeStruct(shape, F32),
        scratch_shapes=[VMEM(shape, F32), DMA],
        name="probe_rows",
    )(given)


def on_device(
    object_field,
    probe_field,
    amplitudes,
    pos_rows,
    pos_cols,
    counts,
    admm_dual,
    volume,
    proj_weights,
    ray_weights,
    angle_ids,
):
    margin = probe_field.shape[1] // 2
    own = object_field[0]
    tile_cols = own.shape[2]
    flat_axes = ("tile", "proj")
    plane = lax.axis_size("tile") * lax.axis_size("proj")
    proj_count = lax.axis_size("proj")
    layers = lax.axis_size("cuts")
    from_left = shifted(own[:, :, tile_cols - margin :], "tile", 1)
    from_right = shifted(own[:, :, :margin], "tile", -1)
    forward = forward_parts(angle_ids, volume, proj_weights, ray_weights, plane)
    forward, from_left, from_right = lax.optimization_barrier((forward, from_left, from_right))
    arrived = lax.all_to_all(forward, flat_axes, 0, 0, tiled=True)
    place = lax.axis_index("proj")
    everyone = ("proj", "tile", "cuts")
    partial_object, edge_left, edge_right, slab, grad_parts = patch_updates(
        pos_rows[0, 0],
        pos_cols[0, 0],
        counts[0],
        own,
        from_left,
        from_right,
        probe_field,
        amplitudes[0, 0],
        admm_dual[0],
        proj_count,
        layers,
        plane * layers,
    )

    share = tile_cols // proj_count
    edge = slab.shape[3] - share
    holders = margin // edge
    slab, arrived = lax.optimization_barrier((slab, arrived))
    pieces = slab.reshape(proj_count * layers, *slab.shape[2:])
    pieces = lax.all_to_all(pieces, ("proj", "cuts"), 0, 0, tiled=True)
    pairs = []
    for tile in range(lax.axis_size("tile") - 1):
        for k in range(holders):
            lower = tile * proj_count + proj_count - holders + k
            upper = (tile + 1) * proj_count + k
            pairs += [(lower, upper), (upper, lower)]
    grads_in = lax.ppermute(pieces[:, :, share:], flat_axes, pairs)
    at_start = jnp.pad(grads_in, ((0, 0), (0, 0), (0, share - edge)))
    at_end = jnp.pad(grads_in, ((0, 0), (0, 0), (share - edge, 0)))
    target = pieces[:, :, :share] + jnp.where(place < holders, at_start, at_end)
    residual = (jnp.sum(arrived, axis=0) - target).astype(BF16)
    copies = jnp.broadcast_to(residual[None], (plane, *residual.shape))

    copies, grad_parts = lax.optimization_barrier((copies, grad_parts))
    residual = lax.all_to_all(copies, flat_axes, 0, 0, tiled=True)
    received = lax.all_to_all(grad_parts, everyone, 0, 0, tiled=True)

    residual, edge_left, edge_right = lax.optimization_barrier((residual, edge_left, edge_right))
    edge_from_right = shifted(edge_left, "tile", -1)
    edge_from_left = shifted(edge_right, "tile", 1)
    back_sums = backward_sums(angle_ids, residual, proj_weights)

    back_sums, received = lax.optimization_barrier((back_sums, received))
    steps = probe_rows(received, probe_field.shape[1])
    steps = lax.all_to_all(steps, everyone, 0, 0, tiled=True)
    new_volume, new_object = volume_update(
        angle_ids,
        back_sums,
        ray_weights,
        volume,
        partial_object,
        edge_from_left,
        edge_from_right,
    )
    new_probe = probe_field + steps.reshape(probe_field.shape)
    return (new_object[None], new_probe, new_volume)


def solution(mesh):
    in_specs = (
        P(("proj", "cuts"), None, None, "tile"),
        P(),
        P(("proj", "cuts"), "tile", None, None, None),
        P(("proj", "cuts"), "tile", None),
        P(("proj", "cuts"), "tile", None),
        P(("proj", "cuts"), "tile"),
        P(("proj", "cuts"), None, "tile"),
        P("cuts", ("tile", "proj"), None),
        P(None, ("tile", "proj"), None),
        P(),
        P(),
    )
    out_specs = (P(("proj", "cuts"), None, None, "tile"), P(), P("cuts", ("tile", "proj"), None))
    return jax.shard_map(
        on_device, mesh=mesh, in_specs=in_specs, out_specs=out_specs, check_vma=False
    )
```

```python
import functools
import math

import jax
import jax.numpy as jnp
import numpy as np
from jax import lax
from jax.experimental import pallas as pl
from jax.experimental.pallas import tpu as pltpu
from jax.sharding import PartitionSpec as P

VMEM_LIMIT = 60 * 1024 * 1024
VMEM = pltpu.VMEM
F32 = jnp.float32
BF16 = jnp.bfloat16
LANES = 128
SUBLANES = 8
AHEAD = 6
WEIGHTS_AHEAD = 6
ANYWHERE = pl.BlockSpec(memory_space=pl.ANY)
WHOLE = pl.BlockSpec(memory_space=pltpu.VMEM)
SCALARS = pl.BlockSpec(memory_space=pltpu.SMEM)
DMA = pltpu.SemaphoreType.DMA

tomo_step = 1.0


def shifted(value, axis, steps):
    count = lax.axis_size(axis)
    leading, last = (max(0, -steps), min(count, count - steps))
    return lax.ppermute(value, axis, [(source, source + steps) for source in range(leading, last)])


def dft_table(side):
    indices = np.arange(side)
    products = (indices[:, None] * indices[None, :]) % side
    phase = products.astype(np.float32) * np.float32(2.0 * math.pi / side)
    norm = np.float32(1.0 / math.sqrt(side))
    real = np.cos(phase).astype(np.float32) * norm
    imag = -np.sin(phase).astype(np.float32) * norm
    return np.stack([real, imag]).astype(jnp.bfloat16)


def dot(left, right):
    return jnp.dot(left, right, preferred_element_type=F32)


def split_bf16(values):
    high = values.astype(BF16).astype(F32)
    low = (values - high).astype(BF16).astype(F32)
    return high, low


def forward_kernel(
    ids_ref,
    rays_hbm,
    volume_hbm,
    weights_hbm,
    out_hbm,
    rays_ref,
    volume_ref,
    weights_ref,
    out_ref,
    table_ref,
    sums_ref,
    rays_sem,
    volume_sem,
    weights_sem,
    out_sem,
):
    depth, projections, _ = sums_ref.shape
    width, lanes = table_ref.shape
    parts, _, _, share = out_ref.shape

    def volume_copy(z):
        return pltpu.make_async_copy(volume_hbm.at[z], volume_ref.at[z], volume_sem.at[z])

    def weights_copy(a):
        return pltpu.make_async_copy(
            weights_hbm.at[ids_ref[a]], weights_ref.at[a], weights_sem.at[a]
        )

    def out_copy(a):
        return pltpu.make_async_copy(out_ref.at[:, a], out_hbm.at[:, a], out_sem.at[a])

    rays_copy = pltpu.make_async_copy(rays_hbm, rays_ref, rays_sem)
    rays_copy.start()
    for z in range(min(AHEAD, depth)):
        volume_copy(z).start()
    for a in range(min(max(AHEAD - depth, 0), projections)):
        weights_copy(a).start()

    rays_copy.wait()
    rows = jnp.concatenate([rays_ref[pl.ds(ids_ref[a], 1), :] for a in range(projections)], axis=0)
    high, low = split_bf16(rows)
    stacked = [high, low]
    if lanes > 2 * projections:
        stacked.append(jnp.zeros((lanes - 2 * projections, width), F32))
    table_ref[...] = jnp.concatenate(stacked, axis=0).T.astype(BF16)

    @pl.loop(0, depth)
    def _(z):
        volume_copy(z).wait()

        @pl.when(z + AHEAD < depth)
        def _():
            volume_copy(z + AHEAD).start()

        @pl.when(jnp.logical_and(z + AHEAD >= depth, z + AHEAD - depth < projections))
        def _():
            weights_copy(z + AHEAD - depth).start()

        piece = min(512, width)
        first = second = None
        for k in range(0, width, piece):
            block = volume_ref[z, :, k : k + piece]
            high = block.astype(BF16)
            low = (block - high.astype(F32)).astype(BF16)
            of_high = dot(high, table_ref[k : k + piece, :])
            of_low = dot(low, table_ref[k : k + piece, :])
            first = of_high if first is None else first + of_high
            second = of_low if second is None else second + of_low
        first = first.T
        second = second.T
        sums_ref[z] = first[:projections] + (
            first[projections : 2 * projections] + second[:projections]
        )

    @pl.loop(0, projections)
    def _(a):
        weights_copy(a).wait()

        @pl.when(a + AHEAD < projections)
        def _():
            weights_copy(a + AHEAD).start()

        rows = sums_ref[:, pl.ds(a, 1), :].reshape(depth, sums_ref.shape[2])
        result = dot(rows.astype(BF16), weights_ref[a])
        for part in range(parts):
            out_ref[part, a] = result[:, part * share : (part + 1) * share]
        out_copy(a).start()

    @pl.loop(0, projections)
    def _(a):
        out_copy(a).wait()


def forward_parts(angle_ids, volume, proj_weights, ray_weights, parts):
    depth, rows, width = volume.shape
    projections = angle_ids.shape[0]
    lanes = -(-2 * projections // LANES) * LANES
    share = width // parts
    return pl.pallas_call(
        forward_kernel,
        in_specs=[SCALARS] + [ANYWHERE] * 3,
        out_specs=ANYWHERE,
        out_shape=jax.ShapeDtypeStruct((parts, projections, depth, share), F32),
        scratch_shapes=[
            VMEM(ray_weights.shape, F32),
            VMEM(volume.shape, F32),
            VMEM((projections, rows, width), BF16),
            VMEM((parts, projections, depth, share), F32),
            VMEM((width, lanes), BF16),
            VMEM((depth, projections, rows), F32),
            DMA,
            pltpu.SemaphoreType.DMA((depth,)),
            pltpu.SemaphoreType.DMA((projections,)),
            pltpu.SemaphoreType.DMA((projections,)),
        ],
        compiler_params=pltpu.CompilerParams(vmem_limit_bytes=VMEM_LIMIT),
        cost_estimate=pl.CostEstimate(
            flops=4 * depth * rows * width * lanes,
            bytes_accessed=depth * rows * width * 4 + projections * rows * width * 2,
            transcendentals=0,
        ),
        name="forward",
    )(angle_ids, ray_weights, volume, proj_weights)


def placed(values, down, across):
    rows, cols = values.shape
    tall = jnp.concatenate([values, jnp.zeros((SUBLANES, cols), F32)], axis=0)
    tall = pltpu.roll(tall, down, axis=0)
    wide = jnp.concatenate([tall, jnp.zeros((rows + SUBLANES, LANES), F32)], axis=1)
    return pltpu.roll(wide, across, axis=1)


def patch_kernel(
    rows_ref,
    cols_ref,
    count_ref,
    place_ref,
    own_hbm,
    left_hbm,
    right_hbm,
    probe_hbm,
    amp_hbm,
    table_hbm,
    dual_hbm,
    new_hbm,
    edge_left_hbm,
    edge_right_hbm,
    slab_hbm,
    *rest,
):
    shares = len(rest) - 27
    parts_hbm = rest[:shares]
    (
        probe_ref,
        amp_ref,
        table_ref,
        dft_a_ref,
        dft_b_ref,
        dual_ref,
        new_ref,
        edge_left_ref,
        edge_right_ref,
        slab_ref,
        parts_ref,
        ext_ref,
        sum_ref,
        grad_ref,
        energy_ref,
        *chain_refs,
        in_sem,
        amp_sem,
        parts_sem,
        out_sem,
    ) = rest[shares:]
    chain_refs = [chain_refs[k : k + 4] for k in range(0, len(chain_refs), 4)]
    side = probe_ref.shape[1]
    _, height, margin = edge_left_ref.shape
    tile_cols = new_ref.shape[2]
    window = side + LANES
    chunk = 32
    tall = chunk + SUBLANES
    inner = pl.ds(0, height)

    copies = [
        pltpu.make_async_copy(source, target, in_sem.at[k])
        for k, (source, target) in enumerate(
            (
                (left_hbm, ext_ref.at[:, inner, pl.ds(0, margin)]),
                (own_hbm, ext_ref.at[:, inner, pl.ds(margin, tile_cols)]),
                (right_hbm, ext_ref.at[:, inner, pl.ds(margin + tile_cols, margin)]),
                (probe_hbm, probe_ref),
                (table_hbm, table_ref),
                (dual_hbm, dual_ref),
            )
        )
    ]
    for copy in copies:
        copy.start()
    live_count = count_ref[0]

    def amp_copy(k):
        return pltpu.make_async_copy(amp_hbm.at[k], amp_ref.at[k], amp_sem.at[k])

    @pl.loop(0, live_count)
    def _(k):
        amp_copy(k).start()

    sum_ref[...] = jnp.zeros(sum_ref.shape, F32)
    grad_ref[...] = jnp.zeros(grad_ref.shape, F32)
    energy_ref[...] = jnp.zeros(energy_ref.shape, F32)
    for copy in copies:
        copy.wait()
    real = table_ref[0]
    imag = table_ref[1]
    for ref, sign in ((dft_a_ref, -1), (dft_b_ref, 1)):
        ref[:side, :side] = real
        ref[side:, side:] = real
        ref[:side, side:] = sign * imag
        ref[side:, :side] = -sign * imag

    @pl.loop(0, live_count)
    def _(k):
        amp_copy(k).wait()

    def pair_step(pair, carry):
        chains = []
        for k, refs in enumerate(chain_refs):
            slot = jnp.minimum(2 * pair + k, live_count - 1)
            live = (2 * pair + k < live_count).astype(F32)
            row = rows_ref[slot]
            col = cols_ref[slot]
            lane = lax.rem(col, LANES)
            notch = lax.rem(row, SUBLANES)
            base = pl.multiple_of(col - lane, LANES)
            top = pl.multiple_of(row - notch, SUBLANES)
            chains.append((slot, live, lane, notch, base, top, *refs))
        for slot, live, lane, notch, base, top, patch_ref, wave_ref, half_ref, far_ref in chains:
            back_shift = lax.rem(window - lane, window)
            up_shift = lax.rem(tall - notch, tall)
            for r in range(0, side, chunk):
                cells = pl.ds(top + r, tall)
                here = slice(r, r + chunk)
                below = slice(side + r, side + r + chunk)
                x_re = pltpu.roll(ext_ref[0, cells, pl.ds(base, window)], back_shift, axis=1)
                x_im = pltpu.roll(ext_ref[1, cells, pl.ds(base, window)], back_shift, axis=1)
                x_re = pltpu.roll(x_re[:, :side], up_shift, axis=0)[:chunk]
                x_im = pltpu.roll(x_im[:, :side], up_shift, axis=0)[:chunk]
                p_re = probe_ref[0, here, :]
                p_im = probe_ref[1, here, :]
                patch_ref[here, :] = x_re
                patch_ref[below, :] = x_im
                wave_ref[here, :] = (p_re * x_re - p_im * x_im).astype(BF16)
                wave_ref[below, :] = (p_re * x_im + p_im * x_re).astype(BF16)
                power = x_re * x_re + x_im * x_im
                energy_ref[...] += live * jnp.sum(
                    power.reshape(chunk // SUBLANES, SUBLANES, side), axis=0
                )
        for *_, wave_ref, half_ref, far_ref in chains:
            half_ref[:, :side] = dot(dft_a_ref[:side, :], wave_ref[...]).astype(BF16)
            half_ref[:, side:] = dot(dft_a_ref[side:, :], wave_ref[...]).astype(BF16)
        for *_, half_ref, far_ref in chains:
            far_ref[...] = dot(half_ref[...], dft_b_ref[...])
        for slot, live, *_, wave_ref, half_ref, far_ref in chains:
            for r in range(0, side, chunk):
                here = slice(r, r + chunk)
                below = slice(side + r, side + r + chunk)
                f_re = far_ref[here, :side]
                f_im = far_ref[here, side:]
                inverse = lax.rsqrt(f_re * f_re + f_im * f_im + 0.25)
                factor = amp_ref[slot, here, :].astype(F32) * inverse - 1.0
                wave_ref[here, :] = (f_re * factor).astype(BF16)
                wave_ref[below, :] = (f_im * factor).astype(BF16)
        for *_, wave_ref, half_ref, far_ref in chains:
            half_ref[:, :side] = dot(dft_b_ref[:side, :], wave_ref[...]).astype(BF16)
            half_ref[:, side:] = dot(dft_b_ref[side:, :], wave_ref[...]).astype(BF16)
        for *_, half_ref, far_ref in chains:
            far_ref[...] = dot(half_ref[...], dft_a_ref[...])
        for slot, live, lane, notch, base, top, patch_ref, wave_ref, half_ref, far_ref in chains:
            for r in range(0, side, chunk):
                cells = pl.ds(top + r, tall)
                here = slice(r, r + chunk)
                below = slice(side + r, side + r + chunk)
                b_re = live * far_ref[here, :side]
                b_im = live * far_ref[here, side:]
                p_re = probe_ref[0, here, :]
                p_im = probe_ref[1, here, :]
                x_re = patch_ref[here, :]
                x_im = patch_ref[below, :]
                o_re = p_re * b_re + p_im * b_im
                o_im = p_re * b_im - p_im * b_re
                sum_ref[0, cells, pl.ds(base, window)] += placed(o_re, notch, lane)
                sum_ref[1, cells, pl.ds(base, window)] += placed(o_im, notch, lane)
                grad_ref[here, :] += x_re * b_re + x_im * b_im
                grad_ref[below, :] += x_re * b_im - x_im * b_re
        return carry

    lax.fori_loop(0, lax.div(live_count + 1, 2), pair_step, 0)

    p_re = probe_ref[0]
    p_im = probe_ref[1]
    peak = jnp.max(p_re * p_re + p_im * p_im)
    scale = 1.0 / (jnp.full((1, LANES), peak, F32) + 1e-05)
    wide = jnp.tile(scale, (1, tile_cols // LANES))
    shares, layers, depth, share = slab_ref.shape
    edge = min(share - tile_cols // shares, margin)
    share -= edge
    holders = margin // edge
    first = (height - layers * depth) // 2
    band = pl.ds(first, layers * depth)
    mid = slice(margin, margin + tile_cols)
    far_side = slice(margin + tile_cols, 2 * margin + tile_cols)
    own_band = ext_ref[1, band, mid] + sum_ref[1, band, mid] * wide + dual_ref[...]
    left_band = sum_ref[1, band, :margin] * scale
    right_band = sum_ref[1, band, far_side] * scale
    for layer in range(layers):
        rows = slice(layer * depth, (layer + 1) * depth)
        for p in range(shares):
            slab_ref[p, layer, :, :share] = own_band[rows, p * share : (p + 1) * share]
            begin = (p - shares + holders) * edge
            if p < holders:
                outgoing = left_band[rows, p * edge : (p + 1) * edge]
            elif p >= shares - holders:
                outgoing = right_band[rows, begin : begin + edge]
            else:
                outgoing = jnp.zeros((depth, edge), F32)
            slab_ref[p, layer, :, share:] = outgoing
    slab_copy = pltpu.make_async_copy(slab_ref, slab_hbm, out_sem.at[3])
    slab_copy.start()
    part_rows = parts_ref.shape[1] - SUBLANES
    last_copies = [slab_copy]
    for step in range(shares):
        begin = pl.multiple_of(lax.rem(place_ref[0] + step, shares) * part_rows, SUBLANES)
        parts_ref[step, :part_rows, :] = grad_ref[pl.ds(begin, part_rows), :]
        parts_ref[step, part_rows:, :] = energy_ref[...]
        copy = pltpu.make_async_copy(parts_ref.at[step], parts_hbm[step], parts_sem.at[step])
        copy.start()
        last_copies.append(copy)
    for c in range(2):
        new_ref[c] = ext_ref[c, inner, mid] + sum_ref[c, inner, mid] * wide
        edge_left_ref[c] = sum_ref[c, inner, :margin] * scale
        edge_right_ref[c] = sum_ref[c, inner, far_side] * scale
    for k, (source, target) in enumerate(
        ((new_ref, new_hbm), (edge_left_ref, edge_left_hbm), (edge_right_ref, edge_right_hbm))
    ):
        copy = pltpu.make_async_copy(source, target, out_sem.at[k])
        copy.start()
        last_copies.append(copy)
    for copy in last_copies:
        copy.wait()


def patch_updates(
    rows, cols, count, place, own, left, right, probe, amplitudes, dual, shares, layers
):
    side = probe.shape[1]
    _, height, tile_cols = own.shape
    margin = left.shape[2]
    slots = amplitudes.shape[0]
    slab_rows = dual.shape[0]
    share = tile_cols // shares
    edge = min(share, margin)
    table = dft_table(side)
    extent = tile_cols + 2 * margin + LANES
    shape = jax.ShapeDtypeStruct
    slab_shape = (shares, layers, slab_rows // layers, share + edge)
    part_rows = 2 * side // shares + SUBLANES
    chain = [
        VMEM((2 * side, side), F32),
        VMEM((2 * side, side), BF16),
        VMEM((side, 2 * side), BF16),
        VMEM((side, 2 * side), F32),
    ]
    return pl.pallas_call(
        patch_kernel,
        in_specs=[SCALARS] * 4 + [ANYWHERE] * 7,
        out_specs=[ANYWHERE] * (4 + shares),
        out_shape=[
            shape((2, height, tile_cols), F32),
            shape((2, height, margin), F32),
            shape((2, height, margin), F32),
            shape(slab_shape, F32),
        ]
        + [shape((part_rows, side), F32)] * shares,
        scratch_shapes=[
            VMEM(probe.shape, F32),
            VMEM(amplitudes.shape, BF16),
            VMEM(table.shape, BF16),
            VMEM((2 * side, 2 * side), BF16),
            VMEM((2 * side, 2 * side), BF16),
            VMEM(dual.shape, F32),
            VMEM((2, height, tile_cols), F32),
            VMEM((2, height, margin), F32),
            VMEM((2, height, margin), F32),
            VMEM(slab_shape, F32),
            VMEM((shares, part_rows, side), F32),
            VMEM((2, height + SUBLANES, extent), F32),
            VMEM((2, height + SUBLANES, extent), F32),
            VMEM((2 * side, side), F32),
            VMEM((SUBLANES, side), F32),
            *chain,
            *chain,
            pltpu.SemaphoreType.DMA((6,)),
            pltpu.SemaphoreType.DMA((slots,)),
            pltpu.SemaphoreType.DMA((shares,)),
            pltpu.SemaphoreType.DMA((4,)),
        ],
        compiler_params=pltpu.CompilerParams(vmem_limit_bytes=VMEM_LIMIT),
        cost_estimate=pl.CostEstimate(
            flops=slots * 32 * side**3,
            bytes_accessed=8 * height * tile_cols * 4,
            transcendentals=slots * side * side,
        ),
        name="patches",
    )(
        rows,
        cols,
        count,
        place,
        own,
        left,
        right,
        probe,
        amplitudes,
        jnp.asarray(table),
        dual,
    )


def update_kernel(
    ids_ref,
    residual_hbm,
    weights_hbm,
    rays_hbm,
    volume_hbm,
    object_hbm,
    from_left_hbm,
    from_right_hbm,
    out_hbm,
    new_object_hbm,
    residual_ref,
    weights_ref,
    rays_ref,
    volume_ref,
    turned_ref,
    total_ref,
    stack_ref,
    spread_ref,
    done_ref,
    cells_ref,
    left_ref,
    right_ref,
    small_sem,
    weights_sem,
    volume_sem,
    out_sem,
    object_sem,
):
    depth = volume_ref.shape[0]
    slots = done_ref.shape[0]
    margin = left_ref.shape[2]
    tile_cols = cells_ref.shape[2]
    width = rays_ref.shape[1]
    parts, projections, _, share = residual_ref.shape
    both = projections * depth

    def weights_copy(a):
        return pltpu.make_async_copy(
            weights_hbm.at[ids_ref[a]], weights_ref.at[a], weights_sem.at[a]
        )

    def volume_copy(z):
        return pltpu.make_async_copy(volume_hbm.at[z], volume_ref.at[z], volume_sem.at[z])

    def out_copy(z):
        slot = lax.rem(z, slots)
        return pltpu.make_async_copy(done_ref.at[slot], out_hbm.at[z], out_sem.at[slot])

    residual_copy = pltpu.make_async_copy(residual_hbm, residual_ref, small_sem.at[0])
    residual_copy.start()
    rays_copy = pltpu.make_async_copy(rays_hbm, rays_ref, small_sem.at[1])
    rays_copy.start()
    for a in range(min(WEIGHTS_AHEAD, projections)):
        weights_copy(a).start()
    copies = [
        pltpu.make_async_copy(source, target, object_sem.at[k])
        for k, (source, target) in enumerate(
            ((object_hbm, cells_ref), (from_left_hbm, left_ref), (from_right_hbm, right_ref))
        )
    ]

    residual_copy.wait()
    for part in range(parts):
        block = residual_ref[part].astype(F32).reshape(both, share)
        turned_ref[part * share : (part + 1) * share, :] = block.T
    total_ref[...] = jnp.zeros(total_ref.shape, F32)
    rays_copy.wait()
    rows = [
        jnp.broadcast_to(rays_ref[pl.ds(ids_ref[a], 1), :], (depth, width))
        for a in range(projections)
    ]
    high, low = split_bf16(jnp.concatenate(rows, axis=0))
    for place, block in enumerate((high, high, low, low)):
        spread_ref[place * both : (place + 1) * both, :] = block.astype(BF16)

    @pl.loop(0, projections)
    def _(a):
        @pl.when(a + WEIGHTS_AHEAD < projections)
        def _():
            weights_copy(a + WEIGHTS_AHEAD).start()

        z = a + WEIGHTS_AHEAD - projections

        @pl.when(jnp.logical_and(z >= 0, z < depth))
        def _():
            volume_copy(z).start()

        weights_copy(a).wait()
        lane = lax.broadcasted_iota(jnp.int32, turned_ref.shape, 1)
        begin = a * depth
        kept = jnp.logical_and(lane >= begin, lane < begin + depth)
        chosen = jnp.where(kept, turned_ref[...], 0.0).astype(BF16)
        total_ref[...] += dot(weights_ref[a], chosen)

    for z in range(min(WEIGHTS_AHEAD, depth), depth):
        volume_copy(z).start()
    for copy in copies:
        copy.start()
    high, low = split_bf16(total_ref[...])
    stack_ref[...] = jnp.concatenate([high, low, high, low], axis=1)

    @pl.loop(0, depth)
    def _(z):
        volume_copy(z).wait()

        @pl.when(z >= slots)
        def _():
            out_copy(z - slots).wait()

        lane = lax.broadcasted_iota(jnp.int32, stack_ref.shape, 1)
        kept = lax.rem(lane, depth) == z
        chosen = jnp.where(kept, stack_ref[...], 0.0).astype(BF16)
        done_ref[lax.rem(z, slots)] = volume_ref[z] - tomo_step * dot(chosen, spread_ref[...])
        out_copy(z).start()

    for copy in copies:
        copy.wait()
    cells_ref[:, :, :margin] += left_ref[...]
    cells_ref[:, :, tile_cols - margin :] += right_ref[...]
    object_copy = pltpu.make_async_copy(cells_ref, new_object_hbm, object_sem.at[0])
    object_copy.start()
    for z in range(max(depth - slots, 0), depth):
        out_copy(z).wait()
    object_copy.wait()


def volume_update(
    angle_ids, residual, proj_weights, rays, volume, partial_object, from_left, from_right
):
    depth, rows, width = volume.shape
    projections = angle_ids.shape[0]
    both = projections * depth
    slots = min(4, depth)
    return pl.pallas_call(
        update_kernel,
        in_specs=[SCALARS] + [ANYWHERE] * 7,
        out_specs=[ANYWHERE] * 2,
        out_shape=[
            jax.ShapeDtypeStruct(volume.shape, F32),
            jax.ShapeDtypeStruct(partial_object.shape, F32),
        ],
        scratch_shapes=[
            VMEM(residual.shape, BF16),
            VMEM((projections, rows, width), BF16),
            VMEM(rays.shape, F32),
            VMEM(volume.shape, F32),
            VMEM((width, both), F32),
            VMEM((rows, both), F32),
            VMEM((rows, 4 * both), F32),
            VMEM((4 * both, width), BF16),
            VMEM((slots, rows, width), F32),
            VMEM(partial_object.shape, F32),
            VMEM(from_left.shape, F32),
            VMEM(from_right.shape, F32),
            pltpu.SemaphoreType.DMA((2,)),
            pltpu.SemaphoreType.DMA((projections,)),
            pltpu.SemaphoreType.DMA((depth,)),
            pltpu.SemaphoreType.DMA((slots,)),
            pltpu.SemaphoreType.DMA((3,)),
        ],
        compiler_params=pltpu.CompilerParams(vmem_limit_bytes=VMEM_LIMIT),
        cost_estimate=pl.CostEstimate(
            flops=2 * rows * width * both * (projections + 4 * depth),
            bytes_accessed=2 * depth * rows * width * 4 + projections * rows * width * 2,
            transcendentals=0,
        ),
        name="update",
    )(angle_ids, residual, proj_weights, rays, volume, partial_object, from_left, from_right)


def gather_parts_kernel(group, *refs):
    *given, out_hbm, out_ref, sem = refs
    total = given[0][...]
    for ref in given[1:]:
        total = total + ref[...]
    _, rows, _ = out_ref.shape
    rows -= SUBLANES
    for k in range(group):
        out_ref[k, :rows, :] = total[k * rows : (k + 1) * rows]
        out_ref[k, rows:, :] = total[group * rows :]
    copy = pltpu.make_async_copy(out_ref, out_hbm, sem)
    copy.start()
    copy.wait()


def gather_parts(given, group):
    total_rows, side = given[0].shape
    rows = (total_rows - SUBLANES) // group + SUBLANES
    return pl.pallas_call(
        functools.partial(gather_parts_kernel, group),
        in_specs=[WHOLE] * len(given),
        out_specs=ANYWHERE,
        out_shape=jax.ShapeDtypeStruct((group, rows, side), F32),
        scratch_shapes=[VMEM((group, rows, side), F32), DMA],
        compiler_params=pltpu.CompilerParams(vmem_limit_bytes=VMEM_LIMIT),
        name="probe_parts",
    )(*given)


def probe_rows_kernel(given_ref, out_hbm, out_ref, sem):
    group, rows, side = given_ref.shape
    rows -= SUBLANES
    total = given_ref[0]
    for k in range(1, group):
        total = total + given_ref[k]
    energy = jnp.sum(total[rows:], keepdims=True) / (side * side)
    steps = total[:rows] / (energy + 1e-05)
    for k in range(group):
        out_ref[k] = steps
    copy = pltpu.make_async_copy(out_ref, out_hbm, sem)
    copy.start()
    copy.wait()


def probe_rows(given):
    group, rows, side = given.shape
    shape = (group, rows - SUBLANES, side)
    return pl.pallas_call(
        probe_rows_kernel,
        in_specs=[WHOLE],
        out_specs=ANYWHERE,
        out_shape=jax.ShapeDtypeStruct(shape, F32),
        scratch_shapes=[VMEM(shape, F32), DMA],
        compiler_params=pltpu.CompilerParams(vmem_limit_bytes=VMEM_LIMIT),
        name="probe_rows",
    )(given)


def turned(value, axis, steps):
    count = lax.axis_size(axis)
    return lax.ppermute(value, axis, [(k, (k + steps) % count) for k in range(count)])


def on_device(
    object_field,
    probe_field,
    amplitudes,
    pos_rows,
    pos_cols,
    counts,
    admm_dual,
    volume,
    proj_weights,
    ray_weights,
    angle_ids,
):
    margin = probe_field.shape[1] // 2
    own = object_field[0]
    tile_cols = own.shape[2]
    flat_axes = ("tile", "proj")
    plane = lax.axis_size("tile") * lax.axis_size("proj")
    proj_count = lax.axis_size("proj")
    layers = lax.axis_size("cuts")
    from_left = shifted(own[:, :, tile_cols - margin :], "tile", 1)
    from_right = shifted(own[:, :, :margin], "tile", -1)
    forward = forward_parts(angle_ids, volume, proj_weights, ray_weights, plane)
    forward, from_left, from_right = lax.optimization_barrier((forward, from_left, from_right))
    arrived = lax.all_to_all(forward, flat_axes, 0, 0, tiled=True)
    place = lax.axis_index("proj")
    partial_object, edge_left, edge_right, slab, *grad_parts = patch_updates(
        pos_rows[0, 0],
        pos_cols[0, 0],
        counts[0],
        place[None],
        own,
        from_left,
        from_right,
        probe_field,
        amplitudes[0, 0],
        admm_dual[0],
        proj_count,
        layers,
    )

    share = tile_cols // proj_count
    edge = slab.shape[3] - share
    holders = margin // edge
    slab, arrived = lax.optimization_barrier((slab, arrived))
    pieces = slab.reshape(proj_count * layers, *slab.shape[2:])
    pieces = lax.all_to_all(pieces, ("proj", "cuts"), 0, 0, tiled=True)
    pairs = []
    for tile in range(lax.axis_size("tile") - 1):
        for k in range(holders):
            lower = tile * proj_count + proj_count - holders + k
            upper = (tile + 1) * proj_count + k
            pairs += [(lower, upper), (upper, lower)]
    grads_in = lax.ppermute(pieces[:, :, share:], flat_axes, pairs)
    at_start = jnp.pad(grads_in, ((0, 0), (0, 0), (0, share - edge)))
    at_end = jnp.pad(grads_in, ((0, 0), (0, 0), (share - edge, 0)))
    target = pieces[:, :, :share] + jnp.where(place < holders, at_start, at_end)
    residual = (jnp.sum(arrived, axis=0) - target).astype(BF16)
    copies = jnp.broadcast_to(residual[None], (plane, *residual.shape))

    group_axes = ("tile", "cuts")
    group = lax.axis_size("tile") * layers
    given = [grad_parts[0]]
    for step in range(1, proj_count):
        given.append(turned(grad_parts[step], "proj", step))
    copies, given, edge_left, edge_right = lax.optimization_barrier(
        (copies, given, edge_left, edge_right)
    )
    residual = lax.all_to_all(copies, flat_axes, 0, 0, tiled=True)
    received = lax.all_to_all(gather_parts(given, group), group_axes, 0, 0, tiled=True)
    edge_from_right = shifted(edge_left, "tile", -1)
    edge_from_left = shifted(edge_right, "tile", 1)
    steps = probe_rows(received)
    steps, residual = lax.optimization_barrier((steps, residual))
    steps = lax.all_to_all(steps, group_axes, 0, 0, tiled=True)
    new_volume, new_object = volume_update(
        angle_ids,
        residual,
        proj_weights,
        ray_weights,
        volume,
        partial_object,
        edge_from_left,
        edge_from_right,
    )
    steps = steps.reshape(-1, probe_field.shape[1])
    if proj_count == 2:
        other = turned(steps, "proj", 1)
        first = place == 0
        steps = jnp.stack([jnp.where(first, steps, other), jnp.where(first, other, steps)])
    else:
        steps = lax.all_gather(steps, "proj", axis=0, tiled=True)
    new_probe = probe_field + steps.reshape(probe_field.shape)
    return (new_object[None], new_probe, new_volume)


def solution(mesh):
    in_specs = (
        P(("proj", "cuts"), None, None, "tile"),
        P(),
        P(("proj", "cuts"), "tile", None, None, None),
        P(("proj", "cuts"), "tile", None),
        P(("proj", "cuts"), "tile", None),
        P(("proj", "cuts"), "tile"),
        P(("proj", "cuts"), None, "tile"),
        P("cuts", ("tile", "proj"), None),
        P(None, ("tile", "proj"), None),
        P(),
        P(),
    )
    out_specs = (P(("proj", "cuts"), None, None, "tile"), P(), P("cuts", ("tile", "proj"), None))
    return jax.shard_map(
        on_device, mesh=mesh, in_specs=in_specs, out_specs=out_specs, check_vma=False
    )
```

```python
import functools
import math

import jax
import jax.numpy as jnp
import numpy as np
from jax import lax
from jax.experimental import pallas as pl
from jax.experimental.pallas import tpu as pltpu
from jax.sharding import PartitionSpec as P

VMEM_LIMIT = 60 * 1024 * 1024
VMEM = pltpu.VMEM
F32 = jnp.float32
BF16 = jnp.bfloat16
LANES = 128
SUBLANES = 8
AHEAD = 3
ANYWHERE = pl.BlockSpec(memory_space=pl.ANY)
WHOLE = pl.BlockSpec(memory_space=pltpu.VMEM)
SCALARS = pl.BlockSpec(memory_space=pltpu.SMEM)
DMA = pltpu.SemaphoreType.DMA

tomo_step = 1.0


def shifted(value, axis, steps):
    count = lax.axis_size(axis)
    leading, last = (max(0, -steps), min(count, count - steps))
    return lax.ppermute(value, axis, [(source, source + steps) for source in range(leading, last)])


def dft_table(side):
    indices = np.arange(side)
    products = (indices[:, None] * indices[None, :]) % side
    phase = products.astype(np.float32) * np.float32(2.0 * math.pi / side)
    norm = np.float32(1.0 / math.sqrt(side))
    real = np.cos(phase).astype(np.float32) * norm
    imag = -np.sin(phase).astype(np.float32) * norm
    return np.stack([real, imag]).astype(jnp.bfloat16)


def dot(left, right):
    return jnp.dot(left, right, preferred_element_type=F32)


def split_bf16(values):
    high = values.astype(BF16).astype(F32)
    low = (values - high).astype(BF16).astype(F32)
    return high, low


def forward_kernel(
    ids_ref,
    rays_hbm,
    volume_hbm,
    weights_hbm,
    out_hbm,
    rays_ref,
    volume_ref,
    weights_ref,
    out_ref,
    table_ref,
    sums_ref,
    rays_sem,
    volume_sem,
    weights_sem,
    out_sem,
):
    depth, projections, _ = sums_ref.shape
    width, lanes = table_ref.shape
    parts, _, _, share = out_ref.shape

    def volume_copy(z):
        return pltpu.make_async_copy(volume_hbm.at[z], volume_ref.at[z], volume_sem.at[z])

    def weights_copy(a):
        return pltpu.make_async_copy(
            weights_hbm.at[ids_ref[a]], weights_ref.at[a], weights_sem.at[a]
        )

    def out_copy(a):
        return pltpu.make_async_copy(out_ref.at[:, a], out_hbm.at[:, a], out_sem.at[a])

    rays_copy = pltpu.make_async_copy(rays_hbm, rays_ref, rays_sem)
    rays_copy.start()
    for z in range(min(AHEAD, depth)):
        volume_copy(z).start()
    for a in range(min(max(AHEAD - depth, 0), projections)):
        weights_copy(a).start()

    rays_copy.wait()
    rows = jnp.concatenate([rays_ref[pl.ds(ids_ref[a], 1), :] for a in range(projections)], axis=0)
    high, low = split_bf16(rows)
    stacked = [high, low]
    if lanes > 2 * projections:
        stacked.append(jnp.zeros((lanes - 2 * projections, width), F32))
    table_ref[...] = jnp.concatenate(stacked, axis=0).T.astype(BF16)

    @pl.loop(0, depth)
    def _(z):
        volume_copy(z).wait()

        @pl.when(z + AHEAD < depth)
        def _():
            volume_copy(z + AHEAD).start()

        @pl.when(jnp.logical_and(z + AHEAD >= depth, z + AHEAD - depth < projections))
        def _():
            weights_copy(z + AHEAD - depth).start()

        piece = min(512, width)
        first = second = None
        for k in range(0, width, piece):
            block = volume_ref[z, :, k : k + piece]
            high = block.astype(BF16)
            low = (block - high.astype(F32)).astype(BF16)
            of_high = dot(high, table_ref[k : k + piece, :])
            of_low = dot(low, table_ref[k : k + piece, :])
            first = of_high if first is None else first + of_high
            second = of_low if second is None else second + of_low
        first = first.T
        second = second.T
        sums_ref[z] = first[:projections] + (
            first[projections : 2 * projections] + second[:projections]
        )

    @pl.loop(0, projections)
    def _(a):
        weights_copy(a).wait()

        @pl.when(a + AHEAD < projections)
        def _():
            weights_copy(a + AHEAD).start()

        rows = sums_ref[:, pl.ds(a, 1), :].reshape(depth, sums_ref.shape[2])
        result = dot(rows.astype(BF16), weights_ref[a])
        for part in range(parts):
            out_ref[part, a] = result[:, part * share : (part + 1) * share]
        out_copy(a).start()

    @pl.loop(0, projections)
    def _(a):
        out_copy(a).wait()


def forward_parts(angle_ids, volume, proj_weights, ray_weights, parts):
    depth, rows, width = volume.shape
    projections = angle_ids.shape[0]
    lanes = -(-2 * projections // LANES) * LANES
    share = width // parts
    return pl.pallas_call(
        forward_kernel,
        in_specs=[SCALARS] + [ANYWHERE] * 3,
        out_specs=ANYWHERE,
        out_shape=jax.ShapeDtypeStruct((parts, projections, depth, share), F32),
        scratch_shapes=[
            VMEM(ray_weights.shape, F32),
            VMEM(volume.shape, F32),
            VMEM((projections, rows, width), BF16),
            VMEM((parts, projections, depth, share), F32),
            VMEM((width, lanes), BF16),
            VMEM((depth, projections, rows), F32),
            DMA,
            pltpu.SemaphoreType.DMA((depth,)),
            pltpu.SemaphoreType.DMA((projections,)),
            pltpu.SemaphoreType.DMA((projections,)),
        ],
        compiler_params=pltpu.CompilerParams(vmem_limit_bytes=VMEM_LIMIT),
        cost_estimate=pl.CostEstimate(
            flops=4 * depth * rows * width * lanes,
            bytes_accessed=depth * rows * width * 4 + projections * rows * width * 2,
            transcendentals=0,
        ),
        name="forward",
    )(angle_ids, ray_weights, volume, proj_weights)


def placed(values, down, across):
    rows, cols = values.shape
    tall = jnp.concatenate([values, jnp.zeros((SUBLANES, cols), F32)], axis=0)
    tall = pltpu.roll(tall, down, axis=0)
    wide = jnp.concatenate([tall, jnp.zeros((rows + SUBLANES, LANES), F32)], axis=1)
    return pltpu.roll(wide, across, axis=1)


def patch_kernel(
    rows_ref,
    cols_ref,
    count_ref,
    place_ref,
    own_hbm,
    left_hbm,
    right_hbm,
    probe_hbm,
    amp_hbm,
    table_hbm,
    dual_hbm,
    new_hbm,
    edge_left_hbm,
    edge_right_hbm,
    slab_hbm,
    *rest,
):
    shares = len(rest) - 27
    parts_hbm = rest[:shares]
    (
        probe_ref,
        amp_ref,
        table_ref,
        dft_a_ref,
        dft_b_ref,
        dual_ref,
        new_ref,
        edge_left_ref,
        edge_right_ref,
        slab_ref,
        parts_ref,
        ext_ref,
        sum_ref,
        grad_ref,
        energy_ref,
        *chain_refs,
        in_sem,
        amp_sem,
        parts_sem,
        out_sem,
    ) = rest[shares:]
    chain_refs = [chain_refs[k : k + 4] for k in range(0, len(chain_refs), 4)]
    side = probe_ref.shape[1]
    _, height, margin = edge_left_ref.shape
    tile_cols = new_ref.shape[2]
    window = side + LANES
    chunk = 32
    tall = chunk + SUBLANES
    inner = pl.ds(0, height)

    copies = [
        pltpu.make_async_copy(source, target, in_sem.at[k])
        for k, (source, target) in enumerate(
            (
                (left_hbm, ext_ref.at[:, inner, pl.ds(0, margin)]),
                (own_hbm, ext_ref.at[:, inner, pl.ds(margin, tile_cols)]),
                (right_hbm, ext_ref.at[:, inner, pl.ds(margin + tile_cols, margin)]),
                (probe_hbm, probe_ref),
                (table_hbm, table_ref),
                (dual_hbm, dual_ref),
            )
        )
    ]
    for copy in copies:
        copy.start()
    live_count = count_ref[0]

    def amp_copy(k):
        return pltpu.make_async_copy(amp_hbm.at[k], amp_ref.at[k], amp_sem.at[k])

    @pl.loop(0, live_count)
    def _(k):
        amp_copy(k).start()

    sum_ref[...] = jnp.zeros(sum_ref.shape, F32)
    grad_ref[...] = jnp.zeros(grad_ref.shape, F32)
    energy_ref[...] = jnp.zeros(energy_ref.shape, F32)
    for copy in copies:
        copy.wait()
    real = table_ref[0]
    imag = table_ref[1]
    for ref, sign in ((dft_a_ref, -1), (dft_b_ref, 1)):
        ref[:side, :side] = real
        ref[side:, side:] = real
        ref[:side, side:] = sign * imag
        ref[side:, :side] = -sign * imag

    @pl.loop(0, live_count)
    def _(k):
        amp_copy(k).wait()

    def pair_step(pair, carry):
        chains = []
        for k, refs in enumerate(chain_refs):
            slot = jnp.minimum(2 * pair + k, live_count - 1)
            live = (2 * pair + k < live_count).astype(F32)
            row = rows_ref[slot]
            col = cols_ref[slot]
            lane = lax.rem(col, LANES)
            notch = lax.rem(row, SUBLANES)
            base = pl.multiple_of(col - lane, LANES)
            top = pl.multiple_of(row - notch, SUBLANES)
            chains.append((slot, live, lane, notch, base, top, *refs))
        for slot, live, lane, notch, base, top, patch_ref, wave_ref, half_ref, far_ref in chains:
            back_shift = lax.rem(window - lane, window)
            up_shift = lax.rem(tall - notch, tall)
            for r in range(0, side, chunk):
                cells = pl.ds(top + r, tall)
                here = slice(r, r + chunk)
                below = slice(side + r, side + r + chunk)
                x_re = pltpu.roll(ext_ref[0, cells, pl.ds(base, window)], back_shift, axis=1)
                x_im = pltpu.roll(ext_ref[1, cells, pl.ds(base, window)], back_shift, axis=1)
                x_re = pltpu.roll(x_re[:, :side], up_shift, axis=0)[:chunk]
                x_im = pltpu.roll(x_im[:, :side], up_shift, axis=0)[:chunk]
                p_re = probe_ref[0, here, :]
                p_im = probe_ref[1, here, :]
                patch_ref[here, :] = x_re
                patch_ref[below, :] = x_im
                wave_ref[here, :] = (p_re * x_re - p_im * x_im).astype(BF16)
                wave_ref[below, :] = (p_re * x_im + p_im * x_re).astype(BF16)
                power = x_re * x_re + x_im * x_im
                energy_ref[...] += live * jnp.sum(
                    power.reshape(chunk // SUBLANES, SUBLANES, side), axis=0
                )
        for *_, wave_ref, half_ref, far_ref in chains:
            half_ref[:, :side] = dot(dft_a_ref[:side, :], wave_ref[...]).astype(BF16)
            half_ref[:, side:] = dot(dft_a_ref[side:, :], wave_ref[...]).astype(BF16)
        for *_, half_ref, far_ref in chains:
            far_ref[...] = dot(half_ref[...], dft_b_ref[...])
        for slot, live, *_, wave_ref, half_ref, far_ref in chains:
            for r in range(0, side, chunk):
                here = slice(r, r + chunk)
                below = slice(side + r, side + r + chunk)
                f_re = far_ref[here, :side]
                f_im = far_ref[here, side:]
                inverse = lax.rsqrt(f_re * f_re + f_im * f_im + 0.25)
                factor = amp_ref[slot, here, :].astype(F32) * inverse - 1.0
                wave_ref[here, :] = (f_re * factor).astype(BF16)
                wave_ref[below, :] = (f_im * factor).astype(BF16)
        for *_, wave_ref, half_ref, far_ref in chains:
            half_ref[:, :side] = dot(dft_b_ref[:side, :], wave_ref[...]).astype(BF16)
            half_ref[:, side:] = dot(dft_b_ref[side:, :], wave_ref[...]).astype(BF16)
        for *_, half_ref, far_ref in chains:
            far_ref[...] = dot(half_ref[...], dft_a_ref[...])
        for slot, live, lane, notch, base, top, patch_ref, wave_ref, half_ref, far_ref in chains:
            for r in range(0, side, chunk):
                cells = pl.ds(top + r, tall)
                here = slice(r, r + chunk)
                below = slice(side + r, side + r + chunk)
                b_re = live * far_ref[here, :side]
                b_im = live * far_ref[here, side:]
                p_re = probe_ref[0, here, :]
                p_im = probe_ref[1, here, :]
                x_re = patch_ref[here, :]
                x_im = patch_ref[below, :]
                o_re = p_re * b_re + p_im * b_im
                o_im = p_re * b_im - p_im * b_re
                sum_ref[0, cells, pl.ds(base, window)] += placed(o_re, notch, lane)
                sum_ref[1, cells, pl.ds(base, window)] += placed(o_im, notch, lane)
                grad_ref[here, :] += x_re * b_re + x_im * b_im
                grad_ref[below, :] += x_re * b_im - x_im * b_re
        return carry

    lax.fori_loop(0, lax.div(live_count + 1, 2), pair_step, 0)

    p_re = probe_ref[0]
    p_im = probe_ref[1]
    peak = jnp.max(p_re * p_re + p_im * p_im)
    scale = 1.0 / (jnp.full((1, LANES), peak, F32) + 1e-05)
    wide = jnp.tile(scale, (1, tile_cols // LANES))
    shares, layers, depth, share = slab_ref.shape
    edge = min(share - tile_cols // shares, margin)
    share -= edge
    holders = margin // edge
    first = (height - layers * depth) // 2
    band = pl.ds(first, layers * depth)
    mid = slice(margin, margin + tile_cols)
    far_side = slice(margin + tile_cols, 2 * margin + tile_cols)
    own_band = ext_ref[1, band, mid] + sum_ref[1, band, mid] * wide + dual_ref[...]
    left_band = sum_ref[1, band, :margin] * scale
    right_band = sum_ref[1, band, far_side] * scale
    for layer in range(layers):
        rows = slice(layer * depth, (layer + 1) * depth)
        for p in range(shares):
            slab_ref[p, layer, :, :share] = own_band[rows, p * share : (p + 1) * share]
            begin = (p - shares + holders) * edge
            if p < holders:
                outgoing = left_band[rows, p * edge : (p + 1) * edge]
            elif p >= shares - holders:
                outgoing = right_band[rows, begin : begin + edge]
            else:
                outgoing = jnp.zeros((depth, edge), F32)
            slab_ref[p, layer, :, share:] = outgoing
    slab_copy = pltpu.make_async_copy(slab_ref, slab_hbm, out_sem.at[3])
    slab_copy.start()
    part_rows = parts_ref.shape[1] - SUBLANES
    last_copies = [slab_copy]
    for step in range(shares):
        begin = pl.multiple_of(lax.rem(place_ref[0] + step, shares) * part_rows, SUBLANES)
        parts_ref[step, :part_rows, :] = grad_ref[pl.ds(begin, part_rows), :]
        parts_ref[step, part_rows:, :] = energy_ref[...]
        copy = pltpu.make_async_copy(parts_ref.at[step], parts_hbm[step], parts_sem.at[step])
        copy.start()
        last_copies.append(copy)
    for c in range(2):
        new_ref[c] = ext_ref[c, inner, mid] + sum_ref[c, inner, mid] * wide
        edge_left_ref[c] = sum_ref[c, inner, :margin] * scale
        edge_right_ref[c] = sum_ref[c, inner, far_side] * scale
    for k, (source, target) in enumerate(
        ((new_ref, new_hbm), (edge_left_ref, edge_left_hbm), (edge_right_ref, edge_right_hbm))
    ):
        copy = pltpu.make_async_copy(source, target, out_sem.at[k])
        copy.start()
        last_copies.append(copy)
    for copy in last_copies:
        copy.wait()


def patch_updates(
    rows, cols, count, place, own, left, right, probe, amplitudes, dual, shares, layers
):
    side = probe.shape[1]
    _, height, tile_cols = own.shape
    margin = left.shape[2]
    slots = amplitudes.shape[0]
    slab_rows = dual.shape[0]
    share = tile_cols // shares
    edge = min(share, margin)
    table = dft_table(side)
    extent = tile_cols + 2 * margin + LANES
    shape = jax.ShapeDtypeStruct
    slab_shape = (shares, layers, slab_rows // layers, share + edge)
    part_rows = 2 * side // shares + SUBLANES
    chain = [
        VMEM((2 * side, side), F32),
        VMEM((2 * side, side), BF16),
        VMEM((side, 2 * side), BF16),
        VMEM((side, 2 * side), F32),
    ]
    return pl.pallas_call(
        patch_kernel,
        in_specs=[SCALARS] * 4 + [ANYWHERE] * 7,
        out_specs=[ANYWHERE] * (4 + shares),
        out_shape=[
            shape((2, height, tile_cols), F32),
            shape((2, height, margin), F32),
            shape((2, height, margin), F32),
            shape(slab_shape, F32),
        ]
        + [shape((part_rows, side), F32)] * shares,
        scratch_shapes=[
            VMEM(probe.shape, F32),
            VMEM(amplitudes.shape, BF16),
            VMEM(table.shape, BF16),
            VMEM((2 * side, 2 * side), BF16),
            VMEM((2 * side, 2 * side), BF16),
            VMEM(dual.shape, F32),
            VMEM((2, height, tile_cols), F32),
            VMEM((2, height, margin), F32),
            VMEM((2, height, margin), F32),
            VMEM(slab_shape, F32),
            VMEM((shares, part_rows, side), F32),
            VMEM((2, height + SUBLANES, extent), F32),
            VMEM((2, height + SUBLANES, extent), F32),
            VMEM((2 * side, side), F32),
            VMEM((SUBLANES, side), F32),
            *chain,
            *chain,
            pltpu.SemaphoreType.DMA((6,)),
            pltpu.SemaphoreType.DMA((slots,)),
            pltpu.SemaphoreType.DMA((shares,)),
            pltpu.SemaphoreType.DMA((4,)),
        ],
        compiler_params=pltpu.CompilerParams(vmem_limit_bytes=VMEM_LIMIT),
        cost_estimate=pl.CostEstimate(
            flops=slots * 32 * side**3,
            bytes_accessed=8 * height * tile_cols * 4,
            transcendentals=slots * side * side,
        ),
        name="patches",
    )(
        rows,
        cols,
        count,
        place,
        own,
        left,
        right,
        probe,
        amplitudes,
        jnp.asarray(table),
        dual,
    )


def backward_kernel(
    ids_ref, residual_hbm, weights_hbm, out_ref, residual_ref, weights_ref, turned_ref, sem, weights_sem
):
    parts, projections, depth, share = residual_ref.shape
    both = projections * depth

    def weights_copy(a):
        return pltpu.make_async_copy(
            weights_hbm.at[ids_ref[a]], weights_ref.at[a], weights_sem.at[a]
        )

    residual_copy = pltpu.make_async_copy(residual_hbm, residual_ref, sem)
    residual_copy.start()
    for a in range(min(AHEAD, projections)):
        weights_copy(a).start()
    residual_copy.wait()
    for part in range(parts):
        block = residual_ref[part].astype(F32).reshape(both, share)
        turned_ref[part * share : (part + 1) * share, :] = block.T
    out_ref[...] = jnp.zeros(out_ref.shape, F32)

    @pl.loop(0, projections)
    def _(a):
        weights_copy(a).wait()

        @pl.when(a + AHEAD < projections)
        def _():
            weights_copy(a + AHEAD).start()

        lane = lax.broadcasted_iota(jnp.int32, turned_ref.shape, 1)
        begin = a * depth
        kept = jnp.logical_and(lane >= begin, lane < begin + depth)
        chosen = jnp.where(kept, turned_ref[...], 0.0).astype(BF16)
        out_ref[...] += dot(weights_ref[a], chosen)


def backward_sums(angle_ids, residual, proj_weights):
    _, rows, width = proj_weights.shape
    _, projections, depth, _ = residual.shape
    return pl.pallas_call(
        backward_kernel,
        in_specs=[SCALARS, ANYWHERE, ANYWHERE],
        out_specs=WHOLE,
        out_shape=jax.ShapeDtypeStruct((rows, projections * depth), F32),
        scratch_shapes=[
            VMEM(residual.shape, BF16),
            VMEM((projections, rows, width), BF16),
            VMEM((width, projections * depth), F32),
            DMA,
            pltpu.SemaphoreType.DMA((projections,)),
        ],
        compiler_params=pltpu.CompilerParams(vmem_limit_bytes=VMEM_LIMIT),
        cost_estimate=pl.CostEstimate(
            flops=2 * rows * width * projections * projections * depth,
            bytes_accessed=projections * rows * width * 2,
            transcendentals=0,
        ),
        name="backward",
    )(angle_ids, residual, proj_weights)


def update_kernel(
    ids_ref,
    sums_ref,
    rays_hbm,
    volume_hbm,
    out_hbm,
    rays_ref,
    stack_ref,
    spread_ref,
    volume_ref,
    done_ref,
    rays_sem,
    volume_sem,
    out_sem,
):
    depth = volume_ref.shape[0]
    slots = done_ref.shape[0]
    width = rays_ref.shape[1]
    projections = sums_ref.shape[1] // depth
    both = sums_ref.shape[1]

    def volume_copy(z):
        return pltpu.make_async_copy(volume_hbm.at[z], volume_ref.at[z], volume_sem.at[z])

    def out_copy(z):
        slot = lax.rem(z, slots)
        return pltpu.make_async_copy(done_ref.at[slot], out_hbm.at[z], out_sem.at[slot])

    rays_copy = pltpu.make_async_copy(rays_hbm, rays_ref, rays_sem)
    rays_copy.start()
    for z in range(min(AHEAD, depth)):
        volume_copy(z).start()
    high, low = split_bf16(sums_ref[...])
    stack_ref[...] = jnp.concatenate([high, low, high, low], axis=1)
    rays_copy.wait()
    rows = [
        jnp.broadcast_to(rays_ref[pl.ds(ids_ref[a], 1), :], (depth, width))
        for a in range(projections)
    ]
    high, low = split_bf16(jnp.concatenate(rows, axis=0))
    for place, block in enumerate((high, high, low, low)):
        spread_ref[place * both : (place + 1) * both, :] = block.astype(BF16)

    @pl.loop(0, depth)
    def _(z):
        volume_copy(z).wait()

        @pl.when(z + AHEAD < depth)
        def _():
            volume_copy(z + AHEAD).start()

        @pl.when(z >= slots)
        def _():
            out_copy(z - slots).wait()

        lane = lax.broadcasted_iota(jnp.int32, stack_ref.shape, 1)
        kept = lax.rem(lane, depth) == z
        chosen = jnp.where(kept, stack_ref[...], 0.0).astype(BF16)
        done_ref[lax.rem(z, slots)] = volume_ref[z] - tomo_step * dot(chosen, spread_ref[...])
        out_copy(z).start()

    for z in range(max(depth - slots, 0), depth):
        out_copy(z).wait()


def volume_update(angle_ids, sums, rays, volume):
    depth, rows, width = volume.shape
    slots = min(4, depth)
    return pl.pallas_call(
        update_kernel,
        in_specs=[SCALARS, WHOLE] + [ANYWHERE] * 2,
        out_specs=ANYWHERE,
        out_shape=jax.ShapeDtypeStruct(volume.shape, F32),
        scratch_shapes=[
            VMEM(rays.shape, F32),
            VMEM((rows, 4 * sums.shape[1]), F32),
            VMEM((4 * sums.shape[1], width), BF16),
            VMEM(volume.shape, F32),
            VMEM((slots, rows, width), F32),
            DMA,
            pltpu.SemaphoreType.DMA((depth,)),
            pltpu.SemaphoreType.DMA((slots,)),
        ],
        compiler_params=pltpu.CompilerParams(vmem_limit_bytes=VMEM_LIMIT),
        cost_estimate=pl.CostEstimate(
            flops=8 * rows * width * sums.shape[1] * depth,
            bytes_accessed=2 * depth * rows * width * 4,
            transcendentals=0,
        ),
        name="update",
    )(angle_ids, sums, rays, volume)


def gather_parts_kernel(group, *refs):
    *given, out_hbm, out_ref, sem = refs
    total = given[0][...]
    for ref in given[1:]:
        total = total + ref[...]
    blocks = total.shape[1] // LANES
    rows = (out_ref.shape[1] - SUBLANES) // blocks
    columns = [total[:, k * LANES : (k + 1) * LANES] for k in range(blocks)]
    energy = columns[0][group * rows :]
    for block in columns[1:]:
        energy = energy + block[group * rows :]
    for k in range(group):
        for place, block in enumerate(columns):
            out_ref[k, place * rows : (place + 1) * rows, :] = block[k * rows : (k + 1) * rows]
        out_ref[k, blocks * rows :, :] = energy
    copy = pltpu.make_async_copy(out_ref, out_hbm, sem)
    copy.start()
    copy.wait()


def gather_parts(given, group):
    total_rows, side = given[0].shape
    rows = (total_rows - SUBLANES) // group * (side // LANES) + SUBLANES
    shape = (group, rows, LANES)
    return pl.pallas_call(
        functools.partial(gather_parts_kernel, group),
        in_specs=[WHOLE] * len(given),
        out_specs=ANYWHERE,
        out_shape=jax.ShapeDtypeStruct(shape, F32),
        scratch_shapes=[VMEM(shape, F32), DMA],
        compiler_params=pltpu.CompilerParams(vmem_limit_bytes=VMEM_LIMIT),
        name="probe_parts",
    )(*given)


def probe_rows_kernel(given_ref, out_hbm, out_ref, sem):
    group, rows, _ = given_ref.shape
    receivers, taken, side = out_ref.shape
    total = given_ref[0]
    for k in range(1, group):
        total = total + given_ref[k]
    energy = jnp.sum(total[rows - SUBLANES :], keepdims=True) / (side * side)
    steps = total[: rows - SUBLANES] / (energy + 1e-05)
    steps = jnp.concatenate(
        [steps[k * taken : (k + 1) * taken] for k in range(side // LANES)], axis=1
    )
    for k in range(receivers):
        out_ref[k] = steps
    copy = pltpu.make_async_copy(out_ref, out_hbm, sem)
    copy.start()
    copy.wait()


def probe_rows(given, side, receivers):
    _, rows, _ = given.shape
    shape = (receivers, (rows - SUBLANES) * LANES // side, side)
    return pl.pallas_call(
        probe_rows_kernel,
        in_specs=[WHOLE],
        out_specs=ANYWHERE,
        out_shape=jax.ShapeDtypeStruct(shape, F32),
        scratch_shapes=[VMEM(shape, F32), DMA],
        compiler_params=pltpu.CompilerParams(vmem_limit_bytes=VMEM_LIMIT),
        name="probe_rows",
    )(given)


def turned(value, axis, steps):
    count = lax.axis_size(axis)
    return lax.ppermute(value, axis, [(k, (k + steps) % count) for k in range(count)])


def on_device(
    object_field,
    probe_field,
    amplitudes,
    pos_rows,
    pos_cols,
    counts,
    admm_dual,
    volume,
    proj_weights,
    ray_weights,
    angle_ids,
):
    margin = probe_field.shape[1] // 2
    own = object_field[0]
    tile_cols = own.shape[2]
    flat_axes = ("tile", "proj")
    plane = lax.axis_size("tile") * lax.axis_size("proj")
    proj_count = lax.axis_size("proj")
    layers = lax.axis_size("cuts")
    from_left = shifted(own[:, :, tile_cols - margin :], "tile", 1)
    from_right = shifted(own[:, :, :margin], "tile", -1)
    forward = forward_parts(angle_ids, volume, proj_weights, ray_weights, plane)
    _, from_left, from_right = lax.optimization_barrier((forward, from_left, from_right))
    arrived = lax.all_to_all(forward, flat_axes, 0, 0, tiled=True)
    place = lax.axis_index("proj")
    partial_object, edge_left, edge_right, slab, *grad_parts = patch_updates(
        pos_rows[0, 0],
        pos_cols[0, 0],
        counts[0],
        place[None],
        own,
        from_left,
        from_right,
        probe_field,
        amplitudes[0, 0],
        admm_dual[0],
        proj_count,
        layers,
    )

    share = tile_cols // proj_count
    edge = slab.shape[3] - share
    holders = margin // edge
    slab, arrived = lax.optimization_barrier((slab, arrived))
    pieces = slab.reshape(proj_count * layers, *slab.shape[2:])
    pieces = lax.all_to_all(pieces, ("proj", "cuts"), 0, 0, tiled=True)
    pieces, grad_parts = lax.optimization_barrier((pieces, grad_parts))
    pairs = []
    for tile in range(lax.axis_size("tile") - 1):
        for k in range(holders):
            lower = tile * proj_count + proj_count - holders + k
            upper = (tile + 1) * proj_count + k
            pairs += [(lower, upper), (upper, lower)]
    grads_in = lax.ppermute(pieces[:, :, share:], flat_axes, pairs)
    at_start = jnp.pad(grads_in, ((0, 0), (0, 0), (0, share - edge)))
    at_end = jnp.pad(grads_in, ((0, 0), (0, 0), (share - edge, 0)))
    target = pieces[:, :, :share] + jnp.where(place < holders, at_start, at_end)
    residual = (jnp.sum(arrived, axis=0) - target).astype(BF16)
    copies = jnp.broadcast_to(residual[None], (plane, *residual.shape))

    group_axes = ("tile", "cuts")
    group = lax.axis_size("tile") * layers
    given = [grad_parts[0]]
    for step in range(1, proj_count):
        given.append(turned(grad_parts[step], "proj", step))
    copies, given = lax.optimization_barrier((copies, given))
    residual = lax.all_to_all(copies, flat_axes, 0, 0, tiled=True)
    by_receiver = gather_parts(given, group)
    residual, by_receiver, edge_left, edge_right = lax.optimization_barrier(
        (residual, by_receiver, edge_left, edge_right)
    )
    received = lax.all_to_all(by_receiver, group_axes, 0, 0, tiled=True)
    edge_from_left = shifted(edge_right, "tile", 1)
    back_sums = backward_sums(angle_ids, residual, proj_weights)
    back_sums, received, edge_from_left, edge_left = lax.optimization_barrier(
        (back_sums, received, edge_from_left, edge_left)
    )
    edge_from_right = shifted(edge_left, "tile", -1)
    steps = probe_rows(received, probe_field.shape[1], plane * layers)
    back_sums, steps = lax.optimization_barrier((back_sums, steps))
    steps = lax.all_to_all(steps, ("proj", "tile", "cuts"), 0, 0, tiled=True)
    new_volume = volume_update(angle_ids, back_sums, ray_weights, volume)
    new_volume, steps = lax.optimization_barrier((new_volume, steps))
    new_probe = probe_field + steps.reshape(probe_field.shape)
    rest = tile_cols - margin
    new_object = (
        partial_object
        + jnp.pad(edge_from_left, ((0, 0), (0, 0), (0, rest)))
        + jnp.pad(edge_from_right, ((0, 0), (0, 0), (rest, 0)))
    )
    return (new_object[None], new_probe, new_volume)


def solution(mesh):
    in_specs = (
        P(("proj", "cuts"), None, None, "tile"),
        P(),
        P(("proj", "cuts"), "tile", None, None, None),
        P(("proj", "cuts"), "tile", None),
        P(("proj", "cuts"), "tile", None),
        P(("proj", "cuts"), "tile"),
        P(("proj", "cuts"), None, "tile"),
        P("cuts", ("tile", "proj"), None),
        P(None, ("tile", "proj"), None),
        P(),
        P(),
    )
    out_specs = (P(("proj", "cuts"), None, None, "tile"), P(), P("cuts", ("tile", "proj"), None))
    return jax.shard_map(
        on_device, mesh=mesh, in_specs=in_specs, out_specs=out_specs, check_vma=False
    )
```

```python
import functools
import math

import jax
import jax.numpy as jnp
import numpy as np
from jax import lax
from jax.experimental import pallas as pl
from jax.experimental.pallas import tpu as pltpu
from jax.sharding import PartitionSpec as P

VMEM_LIMIT = 60 * 1024 * 1024
VMEM = pltpu.VMEM
F32 = jnp.float32
BF16 = jnp.bfloat16
LANES = 128
SUBLANES = 8
AHEAD = 3
UPDATE_AHEAD = 6
SMALL_LIMIT = 16 * 1024 * 1024
ANYWHERE = pl.BlockSpec(memory_space=pl.ANY)
WHOLE = pl.BlockSpec(memory_space=pltpu.VMEM)
SCALARS = pl.BlockSpec(memory_space=pltpu.SMEM)
DMA = pltpu.SemaphoreType.DMA

tomo_step = 1.0


def shifted(value, axis, steps):
    count = lax.axis_size(axis)
    leading, last = (max(0, -steps), min(count, count - steps))
    return lax.ppermute(value, axis, [(source, source + steps) for source in range(leading, last)])


def dft_table(side):
    indices = np.arange(side)
    products = (indices[:, None] * indices[None, :]) % side
    phase = products.astype(np.float32) * np.float32(2.0 * math.pi / side)
    norm = np.float32(1.0 / math.sqrt(side))
    real = np.cos(phase).astype(np.float32) * norm
    imag = -np.sin(phase).astype(np.float32) * norm
    return np.stack([real, imag]).astype(jnp.bfloat16)


def dot(left, right):
    return jnp.dot(left, right, preferred_element_type=F32)


def split_bf16(values):
    high = values.astype(BF16).astype(F32)
    low = (values - high).astype(BF16).astype(F32)
    return high, low


def forward_kernel(
    ids_ref,
    rays_hbm,
    volume_hbm,
    weights_hbm,
    out_hbm,
    rays_ref,
    volume_ref,
    weights_ref,
    out_ref,
    table_ref,
    sums_ref,
    rays_sem,
    volume_sem,
    weights_sem,
    out_sem,
):
    depth, projections, _ = sums_ref.shape
    width, lanes = table_ref.shape
    parts, _, _, share = out_ref.shape

    def volume_copy(z):
        return pltpu.make_async_copy(volume_hbm.at[z], volume_ref.at[z], volume_sem.at[z])

    def weights_copy(a):
        return pltpu.make_async_copy(
            weights_hbm.at[ids_ref[a]], weights_ref.at[a], weights_sem.at[a]
        )

    def out_copy(a):
        return pltpu.make_async_copy(out_ref.at[:, a], out_hbm.at[:, a], out_sem.at[a])

    rays_copy = pltpu.make_async_copy(rays_hbm, rays_ref, rays_sem)
    rays_copy.start()
    for z in range(min(AHEAD, depth)):
        volume_copy(z).start()
    for a in range(min(max(AHEAD - depth, 0), projections)):
        weights_copy(a).start()

    rays_copy.wait()
    rows = jnp.concatenate([rays_ref[pl.ds(ids_ref[a], 1), :] for a in range(projections)], axis=0)
    high, low = split_bf16(rows)
    stacked = [high, low]
    if lanes > 2 * projections:
        stacked.append(jnp.zeros((lanes - 2 * projections, width), F32))
    table_ref[...] = jnp.concatenate(stacked, axis=0).T.astype(BF16)

    @pl.loop(0, depth)
    def _(z):
        volume_copy(z).wait()

        @pl.when(z + AHEAD < depth)
        def _():
            volume_copy(z + AHEAD).start()

        @pl.when(jnp.logical_and(z + AHEAD >= depth, z + AHEAD - depth < projections))
        def _():
            weights_copy(z + AHEAD - depth).start()

        piece = min(512, width)
        total = None
        for k in range(0, width, piece):
            block = volume_ref[z, :, k : k + piece]
            high = block.astype(BF16)
            low = (block - high.astype(F32)).astype(BF16)
            stacked = jnp.concatenate([high, low], axis=0)
            part = dot(stacked, table_ref[k : k + piece, :])
            total = part if total is None else total + part
        rows = volume_ref.shape[1]
        total = (total[:rows] + total[rows:]).T
        sums_ref[z] = total[:projections] + total[projections : 2 * projections]

    @pl.loop(0, projections)
    def _(a):
        weights_copy(a).wait()

        @pl.when(a + AHEAD < projections)
        def _():
            weights_copy(a + AHEAD).start()

        rows = sums_ref[:, pl.ds(a, 1), :].reshape(depth, sums_ref.shape[2])
        result = dot(rows.astype(BF16), weights_ref[a])
        for part in range(parts):
            out_ref[part, a] = result[:, part * share : (part + 1) * share]
        out_copy(a).start()

    @pl.loop(0, projections)
    def _(a):
        out_copy(a).wait()


def forward_parts(angle_ids, volume, proj_weights, ray_weights, parts):
    depth, rows, width = volume.shape
    projections = angle_ids.shape[0]
    lanes = -(-2 * projections // LANES) * LANES
    share = width // parts
    return pl.pallas_call(
        forward_kernel,
        in_specs=[SCALARS] + [ANYWHERE] * 3,
        out_specs=ANYWHERE,
        out_shape=jax.ShapeDtypeStruct((parts, projections, depth, share), F32),
        scratch_shapes=[
            VMEM(ray_weights.shape, F32),
            VMEM(volume.shape, F32),
            VMEM((projections, rows, width), BF16),
            VMEM((parts, projections, depth, share), F32),
            VMEM((width, lanes), BF16),
            VMEM((depth, projections, rows), F32),
            DMA,
            pltpu.SemaphoreType.DMA((depth,)),
            pltpu.SemaphoreType.DMA((projections,)),
            pltpu.SemaphoreType.DMA((projections,)),
        ],
        compiler_params=pltpu.CompilerParams(vmem_limit_bytes=VMEM_LIMIT),
        cost_estimate=pl.CostEstimate(
            flops=4 * depth * rows * width * lanes,
            bytes_accessed=depth * rows * width * 4 + projections * rows * width * 2,
            transcendentals=0,
        ),
        name="forward",
    )(angle_ids, ray_weights, volume, proj_weights)


def placed(values, down, across):
    rows, cols = values.shape
    tall = jnp.concatenate([values, jnp.zeros((SUBLANES, cols), F32)], axis=0)
    tall = pltpu.roll(tall, down, axis=0)
    wide = jnp.concatenate([tall, jnp.zeros((rows + SUBLANES, LANES), F32)], axis=1)
    return pltpu.roll(wide, across, axis=1)


def patch_kernel(
    rows_ref,
    cols_ref,
    count_ref,
    place_ref,
    own_hbm,
    left_hbm,
    right_hbm,
    probe_hbm,
    amp_hbm,
    table_hbm,
    dual_hbm,
    new_hbm,
    edge_left_hbm,
    edge_right_hbm,
    slab_hbm,
    *rest,
):
    shares = len(rest) - 27
    parts_hbm = rest[:shares]
    (
        probe_ref,
        amp_ref,
        table_ref,
        dft_a_ref,
        dft_b_ref,
        dual_ref,
        new_ref,
        edge_left_ref,
        edge_right_ref,
        slab_ref,
        parts_ref,
        ext_ref,
        sum_ref,
        grad_ref,
        energy_ref,
        *chain_refs,
        in_sem,
        amp_sem,
        parts_sem,
        out_sem,
    ) = rest[shares:]
    chain_refs = [chain_refs[k : k + 4] for k in range(0, len(chain_refs), 4)]
    side = probe_ref.shape[1]
    _, height, margin = edge_left_ref.shape
    tile_cols = new_ref.shape[2]
    window = side + LANES
    chunk = 32
    tall = chunk + SUBLANES
    inner = pl.ds(0, height)

    copies = [
        pltpu.make_async_copy(source, target, in_sem.at[k])
        for k, (source, target) in enumerate(
            (
                (left_hbm, ext_ref.at[:, inner, pl.ds(0, margin)]),
                (own_hbm, ext_ref.at[:, inner, pl.ds(margin, tile_cols)]),
                (right_hbm, ext_ref.at[:, inner, pl.ds(margin + tile_cols, margin)]),
                (probe_hbm, probe_ref),
                (table_hbm, table_ref),
                (dual_hbm, dual_ref),
            )
        )
    ]
    for copy in copies:
        copy.start()
    live_count = count_ref[0]

    def amp_copy(k):
        return pltpu.make_async_copy(amp_hbm.at[k], amp_ref.at[k], amp_sem.at[k])

    @pl.loop(0, live_count)
    def _(k):
        amp_copy(k).start()

    sum_ref[...] = jnp.zeros(sum_ref.shape, F32)
    grad_ref[...] = jnp.zeros(grad_ref.shape, F32)
    energy_ref[...] = jnp.zeros(energy_ref.shape, F32)
    for copy in copies:
        copy.wait()
    real = table_ref[0]
    imag = table_ref[1]
    for ref, sign in ((dft_a_ref, -1), (dft_b_ref, 1)):
        ref[:side, :side] = real
        ref[side:, side:] = real
        ref[:side, side:] = sign * imag
        ref[side:, :side] = -sign * imag

    @pl.loop(0, live_count)
    def _(k):
        amp_copy(k).wait()

    def pair_step(pair, carry):
        chains = []
        for k, refs in enumerate(chain_refs):
            slot = jnp.minimum(2 * pair + k, live_count - 1)
            live = (2 * pair + k < live_count).astype(F32)
            row = rows_ref[slot]
            col = cols_ref[slot]
            lane = lax.rem(col, LANES)
            notch = lax.rem(row, SUBLANES)
            base = pl.multiple_of(col - lane, LANES)
            top = pl.multiple_of(row - notch, SUBLANES)
            chains.append((slot, live, lane, notch, base, top, *refs))
        for slot, live, lane, notch, base, top, patch_ref, wave_ref, half_ref, far_ref in chains:
            back_shift = lax.rem(window - lane, window)
            up_shift = lax.rem(tall - notch, tall)
            for r in range(0, side, chunk):
                cells = pl.ds(top + r, tall)
                here = slice(r, r + chunk)
                below = slice(side + r, side + r + chunk)
                x_re = pltpu.roll(ext_ref[0, cells, pl.ds(base, window)], back_shift, axis=1)
                x_im = pltpu.roll(ext_ref[1, cells, pl.ds(base, window)], back_shift, axis=1)
                x_re = pltpu.roll(x_re[:, :side], up_shift, axis=0)[:chunk]
                x_im = pltpu.roll(x_im[:, :side], up_shift, axis=0)[:chunk]
                p_re = probe_ref[0, here, :]
                p_im = probe_ref[1, here, :]
                patch_ref[here, :] = x_re
                patch_ref[below, :] = x_im
                wave_ref[here, :] = (p_re * x_re - p_im * x_im).astype(BF16)
                wave_ref[below, :] = (p_re * x_im + p_im * x_re).astype(BF16)
                power = x_re * x_re + x_im * x_im
                energy_ref[...] += live * jnp.sum(
                    power.reshape(chunk // SUBLANES, SUBLANES, side), axis=0
                )
        for *_, wave_ref, half_ref, far_ref in chains:
            half_ref[:, :side] = dot(dft_a_ref[:side, :], wave_ref[...]).astype(BF16)
            half_ref[:, side:] = dot(dft_a_ref[side:, :], wave_ref[...]).astype(BF16)
        for *_, half_ref, far_ref in chains:
            far_ref[...] = dot(half_ref[...], dft_b_ref[...])
        for slot, live, *_, wave_ref, half_ref, far_ref in chains:
            for r in range(0, side, chunk):
                here = slice(r, r + chunk)
                below = slice(side + r, side + r + chunk)
                f_re = far_ref[here, :side]
                f_im = far_ref[here, side:]
                inverse = lax.rsqrt(f_re * f_re + f_im * f_im + 0.25)
                factor = amp_ref[slot, here, :].astype(F32) * inverse - 1.0
                wave_ref[here, :] = (f_re * factor).astype(BF16)
                wave_ref[below, :] = (f_im * factor).astype(BF16)
        for *_, wave_ref, half_ref, far_ref in chains:
            half_ref[:, :side] = dot(dft_b_ref[:side, :], wave_ref[...]).astype(BF16)
            half_ref[:, side:] = dot(dft_b_ref[side:, :], wave_ref[...]).astype(BF16)
        for *_, half_ref, far_ref in chains:
            far_ref[...] = dot(half_ref[...], dft_a_ref[...])
        for slot, live, lane, notch, base, top, patch_ref, wave_ref, half_ref, far_ref in chains:
            for r in range(0, side, chunk):
                cells = pl.ds(top + r, tall)
                here = slice(r, r + chunk)
                below = slice(side + r, side + r + chunk)
                b_re = live * far_ref[here, :side]
                b_im = live * far_ref[here, side:]
                p_re = probe_ref[0, here, :]
                p_im = probe_ref[1, here, :]
                x_re = patch_ref[here, :]
                x_im = patch_ref[below, :]
                o_re = p_re * b_re + p_im * b_im
                o_im = p_re * b_im - p_im * b_re
                sum_ref[0, cells, pl.ds(base, window)] += placed(o_re, notch, lane)
                sum_ref[1, cells, pl.ds(base, window)] += placed(o_im, notch, lane)
                grad_ref[here, :] += x_re * b_re + x_im * b_im
                grad_ref[below, :] += x_re * b_im - x_im * b_re
        return carry

    lax.fori_loop(0, lax.div(live_count + 1, 2), pair_step, 0)

    p_re = probe_ref[0]
    p_im = probe_ref[1]
    peak = jnp.max(p_re * p_re + p_im * p_im)
    scale = 1.0 / (jnp.full((1, LANES), peak, F32) + 1e-05)
    wide = jnp.tile(scale, (1, tile_cols // LANES))
    shares, layers, depth, share = slab_ref.shape
    edge = min(share - tile_cols // shares, margin)
    share -= edge
    holders = margin // edge
    first = (height - layers * depth) // 2
    band = pl.ds(first, layers * depth)
    mid = slice(margin, margin + tile_cols)
    far_side = slice(margin + tile_cols, 2 * margin + tile_cols)
    own_band = ext_ref[1, band, mid] + sum_ref[1, band, mid] * wide + dual_ref[...]
    left_band = sum_ref[1, band, :margin] * scale
    right_band = sum_ref[1, band, far_side] * scale
    for layer in range(layers):
        rows = slice(layer * depth, (layer + 1) * depth)
        for p in range(shares):
            slab_ref[p, layer, :, :share] = own_band[rows, p * share : (p + 1) * share]
            begin = (p - shares + holders) * edge
            if p < holders:
                outgoing = left_band[rows, p * edge : (p + 1) * edge]
            elif p >= shares - holders:
                outgoing = right_band[rows, begin : begin + edge]
            else:
                outgoing = jnp.zeros((depth, edge), F32)
            slab_ref[p, layer, :, share:] = outgoing
    slab_copy = pltpu.make_async_copy(slab_ref, slab_hbm, out_sem.at[3])
    slab_copy.start()
    part_rows = parts_ref.shape[1] - SUBLANES
    last_copies = [slab_copy]
    for step in range(shares):
        begin = pl.multiple_of(lax.rem(place_ref[0] + step, shares) * part_rows, SUBLANES)
        parts_ref[step, :part_rows, :] = grad_ref[pl.ds(begin, part_rows), :]
        parts_ref[step, part_rows:, :] = energy_ref[...]
        copy = pltpu.make_async_copy(parts_ref.at[step], parts_hbm[step], parts_sem.at[step])
        copy.start()
        last_copies.append(copy)
    for c in range(2):
        new_ref[c] = ext_ref[c, inner, mid] + sum_ref[c, inner, mid] * wide
        edge_left_ref[c] = sum_ref[c, inner, :margin] * scale
        edge_right_ref[c] = sum_ref[c, inner, far_side] * scale
    for k, (source, target) in enumerate(
        ((new_ref, new_hbm), (edge_left_ref, edge_left_hbm), (edge_right_ref, edge_right_hbm))
    ):
        copy = pltpu.make_async_copy(source, target, out_sem.at[k])
        copy.start()
        last_copies.append(copy)
    for copy in last_copies:
        copy.wait()


def patch_updates(
    rows, cols, count, place, own, left, right, probe, amplitudes, dual, shares, layers
):
    side = probe.shape[1]
    _, height, tile_cols = own.shape
    margin = left.shape[2]
    slots = amplitudes.shape[0]
    slab_rows = dual.shape[0]
    share = tile_cols // shares
    edge = min(share, margin)
    table = dft_table(side)
    extent = tile_cols + 2 * margin + LANES
    shape = jax.ShapeDtypeStruct
    slab_shape = (shares, layers, slab_rows // layers, share + edge)
    part_rows = 2 * side // shares + SUBLANES
    chain = [
        VMEM((2 * side, side), F32),
        VMEM((2 * side, side), BF16),
        VMEM((side, 2 * side), BF16),
        VMEM((side, 2 * side), F32),
    ]
    return pl.pallas_call(
        patch_kernel,
        in_specs=[SCALARS] * 4 + [ANYWHERE] * 7,
        out_specs=[ANYWHERE] * (4 + shares),
        out_shape=[
            shape((2, height, tile_cols), F32),
            shape((2, height, margin), F32),
            shape((2, height, margin), F32),
            shape(slab_shape, F32),
        ]
        + [shape((part_rows, side), F32)] * shares,
        scratch_shapes=[
            VMEM(probe.shape, F32),
            VMEM(amplitudes.shape, BF16),
            VMEM(table.shape, BF16),
            VMEM((2 * side, 2 * side), BF16),
            VMEM((2 * side, 2 * side), BF16),
            VMEM(dual.shape, F32),
            VMEM((2, height, tile_cols), F32),
            VMEM((2, height, margin), F32),
            VMEM((2, height, margin), F32),
            VMEM(slab_shape, F32),
            VMEM((shares, part_rows, side), F32),
            VMEM((2, height + SUBLANES, extent), F32),
            VMEM((2, height + SUBLANES, extent), F32),
            VMEM((2 * side, side), F32),
            VMEM((SUBLANES, side), F32),
            *chain,
            *chain,
            pltpu.SemaphoreType.DMA((6,)),
            pltpu.SemaphoreType.DMA((slots,)),
            pltpu.SemaphoreType.DMA((shares,)),
            pltpu.SemaphoreType.DMA((4,)),
        ],
        compiler_params=pltpu.CompilerParams(vmem_limit_bytes=VMEM_LIMIT),
        cost_estimate=pl.CostEstimate(
            flops=slots * 32 * side**3,
            bytes_accessed=8 * height * tile_cols * 4,
            transcendentals=slots * side * side,
        ),
        name="patches",
    )(
        rows,
        cols,
        count,
        place,
        own,
        left,
        right,
        probe,
        amplitudes,
        jnp.asarray(table),
        dual,
    )


def backward_kernel(
    ids_ref, residual_hbm, weights_hbm, out_ref, residual_ref, weights_ref, turned_ref, sem, weights_sem
):
    parts, projections, depth, share = residual_ref.shape
    both = projections * depth

    def weights_copy(a):
        return pltpu.make_async_copy(
            weights_hbm.at[ids_ref[a]], weights_ref.at[a], weights_sem.at[a]
        )

    residual_copy = pltpu.make_async_copy(residual_hbm, residual_ref, sem)
    residual_copy.start()
    for a in range(min(AHEAD, projections)):
        weights_copy(a).start()
    residual_copy.wait()
    for part in range(parts):
        block = residual_ref[part].astype(F32).reshape(both, share)
        turned_ref[part * share : (part + 1) * share, :] = block.T
    out_ref[...] = jnp.zeros(out_ref.shape, F32)

    @pl.loop(0, projections)
    def _(a):
        weights_copy(a).wait()

        @pl.when(a + AHEAD < projections)
        def _():
            weights_copy(a + AHEAD).start()

        lane = lax.broadcasted_iota(jnp.int32, turned_ref.shape, 1)
        begin = a * depth
        kept = jnp.logical_and(lane >= begin, lane < begin + depth)
        chosen = jnp.where(kept, turned_ref[...], 0.0).astype(BF16)
        out_ref[...] += dot(weights_ref[a], chosen)


def backward_sums(angle_ids, residual, proj_weights):
    _, rows, width = proj_weights.shape
    _, projections, depth, _ = residual.shape
    return pl.pallas_call(
        backward_kernel,
        in_specs=[SCALARS, ANYWHERE, ANYWHERE],
        out_specs=WHOLE,
        out_shape=jax.ShapeDtypeStruct((rows, projections * depth), F32),
        scratch_shapes=[
            VMEM(residual.shape, BF16),
            VMEM((projections, rows, width), BF16),
            VMEM((width, projections * depth), F32),
            DMA,
            pltpu.SemaphoreType.DMA((projections,)),
        ],
        compiler_params=pltpu.CompilerParams(vmem_limit_bytes=VMEM_LIMIT),
        cost_estimate=pl.CostEstimate(
            flops=2 * rows * width * projections * projections * depth,
            bytes_accessed=projections * rows * width * 2,
            transcendentals=0,
        ),
        name="backward",
    )(angle_ids, residual, proj_weights)


def update_kernel(
    ids_ref,
    sums_ref,
    rays_hbm,
    volume_hbm,
    out_hbm,
    rays_ref,
    stack_ref,
    spread_ref,
    volume_ref,
    done_ref,
    rays_sem,
    volume_sem,
    out_sem,
):
    depth = volume_ref.shape[0]
    slots = done_ref.shape[0]
    width = rays_ref.shape[1]
    projections = sums_ref.shape[1] // depth
    both = sums_ref.shape[1]

    def volume_copy(z):
        return pltpu.make_async_copy(volume_hbm.at[z], volume_ref.at[z], volume_sem.at[z])

    def out_copy(z):
        slot = lax.rem(z, slots)
        return pltpu.make_async_copy(done_ref.at[slot], out_hbm.at[z], out_sem.at[slot])

    rays_copy = pltpu.make_async_copy(rays_hbm, rays_ref, rays_sem)
    rays_copy.start()
    for z in range(min(UPDATE_AHEAD, depth)):
        volume_copy(z).start()
    high, low = split_bf16(sums_ref[...])
    stack_ref[...] = jnp.concatenate([high, low, high, low], axis=1)
    rays_copy.wait()
    rows = [
        jnp.broadcast_to(rays_ref[pl.ds(ids_ref[a], 1), :], (depth, width))
        for a in range(projections)
    ]
    high, low = split_bf16(jnp.concatenate(rows, axis=0))
    for place, block in enumerate((high, high, low, low)):
        spread_ref[place * both : (place + 1) * both, :] = block.astype(BF16)

    @pl.loop(0, depth)
    def _(z):
        volume_copy(z).wait()

        @pl.when(z + UPDATE_AHEAD < depth)
        def _():
            volume_copy(z + UPDATE_AHEAD).start()

        @pl.when(z >= slots)
        def _():
            out_copy(z - slots).wait()

        lane = lax.broadcasted_iota(jnp.int32, stack_ref.shape, 1)
        kept = lax.rem(lane, depth) == z
        chosen = jnp.where(kept, stack_ref[...], 0.0).astype(BF16)
        done_ref[lax.rem(z, slots)] = volume_ref[z] - tomo_step * dot(chosen, spread_ref[...])
        out_copy(z).start()

    for z in range(max(depth - slots, 0), depth):
        out_copy(z).wait()


def volume_update(angle_ids, sums, rays, volume):
    depth, rows, width = volume.shape
    slots = min(4, depth)
    return pl.pallas_call(
        update_kernel,
        in_specs=[SCALARS, WHOLE] + [ANYWHERE] * 2,
        out_specs=ANYWHERE,
        out_shape=jax.ShapeDtypeStruct(volume.shape, F32),
        scratch_shapes=[
            VMEM(rays.shape, F32),
            VMEM((rows, 4 * sums.shape[1]), F32),
            VMEM((4 * sums.shape[1], width), BF16),
            VMEM(volume.shape, F32),
            VMEM((slots, rows, width), F32),
            DMA,
            pltpu.SemaphoreType.DMA((depth,)),
            pltpu.SemaphoreType.DMA((slots,)),
        ],
        compiler_params=pltpu.CompilerParams(vmem_limit_bytes=VMEM_LIMIT),
        cost_estimate=pl.CostEstimate(
            flops=8 * rows * width * sums.shape[1] * depth,
            bytes_accessed=2 * depth * rows * width * 4,
            transcendentals=0,
        ),
        name="update",
    )(angle_ids, sums, rays, volume)


def gather_parts_kernel(group, *refs):
    *given, out_hbm, out_ref, sem = refs
    total = given[0][...]
    for ref in given[1:]:
        total = total + ref[...]
    blocks = total.shape[1] // LANES
    rows = (out_ref.shape[1] - SUBLANES) // blocks
    columns = [total[:, k * LANES : (k + 1) * LANES] for k in range(blocks)]
    energy = columns[0][group * rows :]
    for block in columns[1:]:
        energy = energy + block[group * rows :]
    for k in range(group):
        for place, block in enumerate(columns):
            out_ref[k, place * rows : (place + 1) * rows, :] = block[k * rows : (k + 1) * rows]
        out_ref[k, blocks * rows :, :] = energy
    copy = pltpu.make_async_copy(out_ref, out_hbm, sem)
    copy.start()
    copy.wait()


def gather_parts(given, group):
    total_rows, side = given[0].shape
    rows = (total_rows - SUBLANES) // group * (side // LANES) + SUBLANES
    shape = (group, rows, LANES)
    return pl.pallas_call(
        functools.partial(gather_parts_kernel, group),
        in_specs=[WHOLE] * len(given),
        out_specs=ANYWHERE,
        out_shape=jax.ShapeDtypeStruct(shape, F32),
        scratch_shapes=[VMEM(shape, F32), DMA],
        compiler_params=pltpu.CompilerParams(vmem_limit_bytes=SMALL_LIMIT),
        name="probe_parts",
    )(*given)


def probe_rows_kernel(given_ref, out_hbm, out_ref, sem):
    group, rows, _ = given_ref.shape
    receivers, taken, side = out_ref.shape
    total = given_ref[0]
    for k in range(1, group):
        total = total + given_ref[k]
    energy = jnp.sum(total[rows - SUBLANES :], keepdims=True) / (side * side)
    steps = total[: rows - SUBLANES] / (energy + 1e-05)
    steps = jnp.concatenate(
        [steps[k * taken : (k + 1) * taken] for k in range(side // LANES)], axis=1
    )
    for k in range(receivers):
        out_ref[k] = steps
    copy = pltpu.make_async_copy(out_ref, out_hbm, sem)
    copy.start()
    copy.wait()


def probe_rows(given, side, receivers):
    _, rows, _ = given.shape
    shape = (receivers, (rows - SUBLANES) * LANES // side, side)
    return pl.pallas_call(
        probe_rows_kernel,
        in_specs=[WHOLE],
        out_specs=ANYWHERE,
        out_shape=jax.ShapeDtypeStruct(shape, F32),
        scratch_shapes=[VMEM(shape, F32), DMA],
        compiler_params=pltpu.CompilerParams(vmem_limit_bytes=SMALL_LIMIT),
        name="probe_rows",
    )(given)


def turned(value, axis, steps):
    count = lax.axis_size(axis)
    return lax.ppermute(value, axis, [(k, (k + steps) % count) for k in range(count)])


def on_device(
    object_field,
    probe_field,
    amplitudes,
    pos_rows,
    pos_cols,
    counts,
    admm_dual,
    volume,
    proj_weights,
    ray_weights,
    angle_ids,
):
    margin = probe_field.shape[1] // 2
    own = object_field[0]
    tile_cols = own.shape[2]
    flat_axes = ("tile", "proj")
    plane = lax.axis_size("tile") * lax.axis_size("proj")
    proj_count = lax.axis_size("proj")
    layers = lax.axis_size("cuts")
    from_left = shifted(own[:, :, tile_cols - margin :], "tile", 1)
    from_right = shifted(own[:, :, :margin], "tile", -1)
    forward = forward_parts(angle_ids, volume, proj_weights, ray_weights, plane)
    _, from_left, from_right = lax.optimization_barrier((forward, from_left, from_right))
    arrived = lax.all_to_all(forward, flat_axes, 0, 0, tiled=True)
    place = lax.axis_index("proj")
    partial_object, edge_left, edge_right, slab, *grad_parts = patch_updates(
        pos_rows[0, 0],
        pos_cols[0, 0],
        counts[0],
        place[None],
        own,
        from_left,
        from_right,
        probe_field,
        amplitudes[0, 0],
        admm_dual[0],
        proj_count,
        layers,
    )

    share = tile_cols // proj_count
    edge = slab.shape[3] - share
    holders = margin // edge
    slab, arrived = lax.optimization_barrier((slab, arrived))
    pieces = slab.reshape(proj_count * layers, *slab.shape[2:])
    pieces = lax.all_to_all(pieces, ("proj", "cuts"), 0, 0, tiled=True)
    pieces, grad_parts = lax.optimization_barrier((pieces, grad_parts))
    pairs = []
    for tile in range(lax.axis_size("tile") - 1):
        for k in range(holders):
            lower = tile * proj_count + proj_count - holders + k
            upper = (tile + 1) * proj_count + k
            pairs += [(lower, upper), (upper, lower)]
    grads_in = lax.ppermute(pieces[:, :, share:], flat_axes, pairs)
    at_start = jnp.pad(grads_in, ((0, 0), (0, 0), (0, share - edge)))
    at_end = jnp.pad(grads_in, ((0, 0), (0, 0), (share - edge, 0)))
    target = pieces[:, :, :share] + jnp.where(place < holders, at_start, at_end)
    residual = (jnp.sum(arrived, axis=0) - target).astype(BF16)
    copies = jnp.broadcast_to(residual[None], (plane, *residual.shape))

    group_axes = ("tile", "cuts")
    group = lax.axis_size("tile") * layers
    given = [grad_parts[0]]
    for step in range(1, proj_count):
        given.append(turned(grad_parts[step], "proj", step))
    copies, given = lax.optimization_barrier((copies, given))
    residual = lax.all_to_all(copies, flat_axes, 0, 0, tiled=True)
    by_receiver = gather_parts(given, group)
    residual, by_receiver, edge_left, edge_right = lax.optimization_barrier(
        (residual, by_receiver, edge_left, edge_right)
    )
    received = lax.all_to_all(by_receiver, group_axes, 0, 0, tiled=True)
    edge_from_left = shifted(edge_right, "tile", 1)
    back_sums = backward_sums(angle_ids, residual, proj_weights)
    back_sums, received, edge_left = lax.optimization_barrier((back_sums, received, edge_left))
    edge_from_right = shifted(edge_left, "tile", -1)
    steps = probe_rows(received, probe_field.shape[1], plane * layers)
    back_sums, steps, edge_from_left = lax.optimization_barrier(
        (back_sums, steps, edge_from_left)
    )
    steps = lax.all_to_all(steps, ("proj", "tile", "cuts"), 0, 0, tiled=True)
    new_volume = volume_update(angle_ids, back_sums, ray_weights, volume)
    new_volume, steps = lax.optimization_barrier((new_volume, steps))
    new_probe = probe_field + steps.reshape(probe_field.shape)
    rest = tile_cols - margin
    new_object = (
        partial_object
        + jnp.pad(edge_from_left, ((0, 0), (0, 0), (0, rest)))
        + jnp.pad(edge_from_right, ((0, 0), (0, 0), (rest, 0)))
    )
    return (new_object[None], new_probe, new_volume)


def solution(mesh):
    in_specs = (
        P(("proj", "cuts"), None, None, "tile"),
        P(),
        P(("proj", "cuts"), "tile", None, None, None),
        P(("proj", "cuts"), "tile", None),
        P(("proj", "cuts"), "tile", None),
        P(("proj", "cuts"), "tile"),
        P(("proj", "cuts"), None, "tile"),
        P("cuts", ("tile", "proj"), None),
        P(None, ("tile", "proj"), None),
        P(),
        P(),
    )
    out_specs = (P(("proj", "cuts"), None, None, "tile"), P(), P("cuts", ("tile", "proj"), None))
    return jax.shard_map(
        on_device, mesh=mesh, in_specs=in_specs, out_specs=out_specs, check_vma=False
    )
```

```python
import functools
import math

import jax
import jax.numpy as jnp
import numpy as np
from jax import lax
from jax.experimental import pallas as pl
from jax.experimental.pallas import tpu as pltpu
from jax.sharding import PartitionSpec as P

VMEM_LIMIT = 60 * 1024 * 1024
VMEM = pltpu.VMEM
F32 = jnp.float32
BF16 = jnp.bfloat16
LANES = 128
SUBLANES = 8
AHEAD = 4
UPDATE_AHEAD = 6
SMALL_LIMIT = 16 * 1024 * 1024
ANYWHERE = pl.BlockSpec(memory_space=pl.ANY)
WHOLE = pl.BlockSpec(memory_space=pltpu.VMEM)
SCALARS = pl.BlockSpec(memory_space=pltpu.SMEM)
DMA = pltpu.SemaphoreType.DMA

tomo_step = 1.0


def shifted(value, axis, steps):
    count = lax.axis_size(axis)
    leading, last = (max(0, -steps), min(count, count - steps))
    return lax.ppermute(value, axis, [(source, source + steps) for source in range(leading, last)])


def dft_table(side):
    indices = np.arange(side)
    products = (indices[:, None] * indices[None, :]) % side
    phase = products.astype(np.float32) * np.float32(2.0 * math.pi / side)
    norm = np.float32(1.0 / math.sqrt(side))
    real = np.cos(phase).astype(np.float32) * norm
    imag = -np.sin(phase).astype(np.float32) * norm
    return np.stack([real, imag]).astype(jnp.bfloat16)


def dot(left, right):
    return jnp.dot(left, right, preferred_element_type=F32)


def split_bf16(values):
    high = values.astype(BF16).astype(F32)
    low = (values - high).astype(BF16).astype(F32)
    return high, low


def forward_kernel(
    ids_ref,
    rays_hbm,
    volume_hbm,
    weights_hbm,
    out_hbm,
    rays_ref,
    volume_ref,
    weights_ref,
    out_ref,
    table_ref,
    sums_ref,
    rays_sem,
    volume_sem,
    weights_sem,
    out_sem,
):
    depth, projections, _ = sums_ref.shape
    width, lanes = table_ref.shape
    parts, _, _, share = out_ref.shape

    def volume_copy(z):
        return pltpu.make_async_copy(volume_hbm.at[z], volume_ref.at[z], volume_sem.at[z])

    def weights_copy(a):
        return pltpu.make_async_copy(
            weights_hbm.at[ids_ref[a]], weights_ref.at[a], weights_sem.at[a]
        )

    def out_copy(a):
        return pltpu.make_async_copy(out_ref.at[:, a], out_hbm.at[:, a], out_sem.at[a])

    rays_copy = pltpu.make_async_copy(rays_hbm, rays_ref, rays_sem)
    rays_copy.start()
    for z in range(min(AHEAD, depth)):
        volume_copy(z).start()
    for a in range(min(max(AHEAD - depth, 0), projections)):
        weights_copy(a).start()

    rays_copy.wait()
    rows = jnp.concatenate([rays_ref[pl.ds(ids_ref[a], 1), :] for a in range(projections)], axis=0)
    high, low = split_bf16(rows)
    stacked = [high, low]
    if lanes > 2 * projections:
        stacked.append(jnp.zeros((lanes - 2 * projections, width), F32))
    table_ref[...] = jnp.concatenate(stacked, axis=0).T.astype(BF16)

    rows = volume_ref.shape[1]
    piece = min(512, width)
    group = math.gcd(depth, 2)

    @pl.loop(0, depth, step=group)
    def _(first):
        for z in range(group):
            volume_copy(first + z).wait()
        for z in range(group):
            item = first + z + AHEAD

            @pl.when(item < depth)
            def _():
                volume_copy(item).start()

            @pl.when(jnp.logical_and(item >= depth, item - depth < projections))
            def _():
                weights_copy(item - depth).start()

        for z in range(group):
            total = None
            for k in range(0, width, piece):
                block = volume_ref[first + z, :, k : k + piece]
                high = block.astype(BF16)
                low = (block - high.astype(F32)).astype(BF16)
                stacked = jnp.concatenate([high, low], axis=0)
                part = dot(stacked, table_ref[k : k + piece, :])
                total = part if total is None else total + part
            total = (total[:rows] + total[rows:]).T
            sums_ref[first + z] = total[:projections] + total[projections : 2 * projections]

    members = math.gcd(projections, AHEAD)

    @pl.loop(0, projections, step=members)
    def _(first):
        for a in range(members):
            weights_copy(first + a).wait()
        for a in range(members):
            item = first + a + AHEAD

            @pl.when(item < projections)
            def _():
                weights_copy(item).start()

        for a in range(members):
            sums = sums_ref[:, pl.ds(first + a, 1), :].reshape(depth, rows)
            result = dot(sums.astype(BF16), weights_ref[first + a])
            for part in range(parts):
                out_ref[part, first + a] = result[:, part * share : (part + 1) * share]
        for a in range(members):
            out_copy(first + a).start()

    @pl.loop(0, projections)
    def _(a):
        out_copy(a).wait()


def forward_parts(angle_ids, volume, proj_weights, ray_weights, parts):
    depth, rows, width = volume.shape
    projections = angle_ids.shape[0]
    lanes = -(-2 * projections // LANES) * LANES
    share = width // parts
    return pl.pallas_call(
        forward_kernel,
        in_specs=[SCALARS] + [ANYWHERE] * 3,
        out_specs=ANYWHERE,
        out_shape=jax.ShapeDtypeStruct((parts, projections, depth, share), F32),
        scratch_shapes=[
            VMEM(ray_weights.shape, F32),
            VMEM(volume.shape, F32),
            VMEM((projections, rows, width), BF16),
            VMEM((parts, projections, depth, share), F32),
            VMEM((width, lanes), BF16),
            VMEM((depth, projections, rows), F32),
            DMA,
            pltpu.SemaphoreType.DMA((depth,)),
            pltpu.SemaphoreType.DMA((projections,)),
            pltpu.SemaphoreType.DMA((projections,)),
        ],
        compiler_params=pltpu.CompilerParams(vmem_limit_bytes=VMEM_LIMIT),
        cost_estimate=pl.CostEstimate(
            flops=4 * depth * rows * width * lanes,
            bytes_accessed=depth * rows * width * 4 + projections * rows * width * 2,
            transcendentals=0,
        ),
        name="forward",
    )(angle_ids, ray_weights, volume, proj_weights)


def placed(values, down, across):
    rows, cols = values.shape
    tall = jnp.concatenate([values, jnp.zeros((SUBLANES, cols), F32)], axis=0)
    tall = pltpu.roll(tall, down, axis=0)
    wide = jnp.concatenate([tall, jnp.zeros((rows + SUBLANES, LANES), F32)], axis=1)
    return pltpu.roll(wide, across, axis=1)


def patch_kernel(
    rows_ref,
    cols_ref,
    count_ref,
    place_ref,
    own_hbm,
    left_hbm,
    right_hbm,
    probe_hbm,
    amp_hbm,
    table_hbm,
    dual_hbm,
    new_hbm,
    edge_left_hbm,
    edge_right_hbm,
    slab_hbm,
    *rest,
):
    shares = len(rest) - 27
    parts_hbm = rest[:shares]
    (
        probe_ref,
        amp_ref,
        table_ref,
        dft_a_ref,
        dft_b_ref,
        dual_ref,
        new_ref,
        edge_left_ref,
        edge_right_ref,
        slab_ref,
        parts_ref,
        ext_ref,
        sum_ref,
        grad_ref,
        energy_ref,
        *chain_refs,
        in_sem,
        amp_sem,
        parts_sem,
        out_sem,
    ) = rest[shares:]
    chain_refs = [chain_refs[k : k + 4] for k in range(0, len(chain_refs), 4)]
    side = probe_ref.shape[1]
    _, height, margin = edge_left_ref.shape
    tile_cols = new_ref.shape[2]
    window = side + LANES
    chunk = 32
    tall = chunk + SUBLANES
    inner = pl.ds(0, height)

    copies = [
        pltpu.make_async_copy(source, target, in_sem.at[k])
        for k, (source, target) in enumerate(
            (
                (left_hbm, ext_ref.at[:, inner, pl.ds(0, margin)]),
                (own_hbm, ext_ref.at[:, inner, pl.ds(margin, tile_cols)]),
                (right_hbm, ext_ref.at[:, inner, pl.ds(margin + tile_cols, margin)]),
                (probe_hbm, probe_ref),
                (table_hbm, table_ref),
                (dual_hbm, dual_ref),
            )
        )
    ]
    for copy in copies:
        copy.start()
    live_count = count_ref[0]

    def amp_copy(k):
        return pltpu.make_async_copy(amp_hbm.at[k], amp_ref.at[k], amp_sem.at[k])

    @pl.loop(0, live_count)
    def _(k):
        amp_copy(k).start()

    sum_ref[...] = jnp.zeros(sum_ref.shape, F32)
    grad_ref[...] = jnp.zeros(grad_ref.shape, F32)
    energy_ref[...] = jnp.zeros(energy_ref.shape, F32)
    for copy in copies:
        copy.wait()
    real = table_ref[0]
    imag = table_ref[1]
    for ref, sign in ((dft_a_ref, -1), (dft_b_ref, 1)):
        ref[:side, :side] = real
        ref[side:, side:] = real
        ref[:side, side:] = sign * imag
        ref[side:, :side] = -sign * imag

    @pl.loop(0, live_count)
    def _(k):
        amp_copy(k).wait()

    def pair_step(pair, carry):
        chains = []
        for k, refs in enumerate(chain_refs):
            slot = jnp.minimum(2 * pair + k, live_count - 1)
            live = (2 * pair + k < live_count).astype(F32)
            row = rows_ref[slot]
            col = cols_ref[slot]
            lane = lax.rem(col, LANES)
            notch = lax.rem(row, SUBLANES)
            base = pl.multiple_of(col - lane, LANES)
            top = pl.multiple_of(row - notch, SUBLANES)
            chains.append((slot, live, lane, notch, base, top, *refs))
        for slot, live, lane, notch, base, top, patch_ref, wave_ref, half_ref, far_ref in chains:
            back_shift = lax.rem(window - lane, window)
            up_shift = lax.rem(tall - notch, tall)
            for r in range(0, side, chunk):
                cells = pl.ds(top + r, tall)
                here = slice(r, r + chunk)
                below = slice(side + r, side + r + chunk)
                x_re = pltpu.roll(ext_ref[0, cells, pl.ds(base, window)], back_shift, axis=1)
                x_im = pltpu.roll(ext_ref[1, cells, pl.ds(base, window)], back_shift, axis=1)
                x_re = pltpu.roll(x_re[:, :side], up_shift, axis=0)[:chunk]
                x_im = pltpu.roll(x_im[:, :side], up_shift, axis=0)[:chunk]
                p_re = probe_ref[0, here, :]
                p_im = probe_ref[1, here, :]
                patch_ref[here, :] = x_re
                patch_ref[below, :] = x_im
                wave_ref[here, :] = (p_re * x_re - p_im * x_im).astype(BF16)
                wave_ref[below, :] = (p_re * x_im + p_im * x_re).astype(BF16)
                power = x_re * x_re + x_im * x_im
                energy_ref[...] += live * jnp.sum(
                    power.reshape(chunk // SUBLANES, SUBLANES, side), axis=0
                )
        for *_, wave_ref, half_ref, far_ref in chains:
            half_ref[:, :side] = dot(dft_a_ref[:side, :], wave_ref[...]).astype(BF16)
            half_ref[:, side:] = dot(dft_a_ref[side:, :], wave_ref[...]).astype(BF16)
        for *_, half_ref, far_ref in chains:
            far_ref[...] = dot(half_ref[...], dft_b_ref[...])
        for slot, live, *_, wave_ref, half_ref, far_ref in chains:
            for r in range(0, side, chunk):
                here = slice(r, r + chunk)
                below = slice(side + r, side + r + chunk)
                f_re = far_ref[here, :side]
                f_im = far_ref[here, side:]
                inverse = lax.rsqrt(f_re * f_re + f_im * f_im + 0.25)
                factor = amp_ref[slot, here, :].astype(F32) * inverse - 1.0
                wave_ref[here, :] = (f_re * factor).astype(BF16)
                wave_ref[below, :] = (f_im * factor).astype(BF16)
        for *_, wave_ref, half_ref, far_ref in chains:
            half_ref[:, :side] = dot(dft_b_ref[:side, :], wave_ref[...]).astype(BF16)
            half_ref[:, side:] = dot(dft_b_ref[side:, :], wave_ref[...]).astype(BF16)
        for *_, half_ref, far_ref in chains:
            far_ref[...] = dot(half_ref[...], dft_a_ref[...])
        for slot, live, lane, notch, base, top, patch_ref, wave_ref, half_ref, far_ref in chains:
            for r in range(0, side, chunk):
                cells = pl.ds(top + r, tall)
                here = slice(r, r + chunk)
                below = slice(side + r, side + r + chunk)
                b_re = live * far_ref[here, :side]
                b_im = live * far_ref[here, side:]
                p_re = probe_ref[0, here, :]
                p_im = probe_ref[1, here, :]
                x_re = patch_ref[here, :]
                x_im = patch_ref[below, :]
                o_re = p_re * b_re + p_im * b_im
                o_im = p_re * b_im - p_im * b_re
                sum_ref[0, cells, pl.ds(base, window)] += placed(o_re, notch, lane)
                sum_ref[1, cells, pl.ds(base, window)] += placed(o_im, notch, lane)
                grad_ref[here, :] += x_re * b_re + x_im * b_im
                grad_ref[below, :] += x_re * b_im - x_im * b_re
        return carry

    lax.fori_loop(0, lax.div(live_count + 1, 2), pair_step, 0)

    p_re = probe_ref[0]
    p_im = probe_ref[1]
    peak = jnp.max(p_re * p_re + p_im * p_im)
    scale = 1.0 / (jnp.full((1, LANES), peak, F32) + 1e-05)
    wide = jnp.tile(scale, (1, tile_cols // LANES))
    shares, layers, depth, share = slab_ref.shape
    edge = min(share - tile_cols // shares, margin)
    share -= edge
    holders = margin // edge
    first = (height - layers * depth) // 2
    band = pl.ds(first, layers * depth)
    mid = slice(margin, margin + tile_cols)
    far_side = slice(margin + tile_cols, 2 * margin + tile_cols)
    own_band = ext_ref[1, band, mid] + sum_ref[1, band, mid] * wide + dual_ref[...]
    left_band = sum_ref[1, band, :margin] * scale
    right_band = sum_ref[1, band, far_side] * scale
    for layer in range(layers):
        rows = slice(layer * depth, (layer + 1) * depth)
        for p in range(shares):
            slab_ref[p, layer, :, :share] = own_band[rows, p * share : (p + 1) * share]
            begin = (p - shares + holders) * edge
            if p < holders:
                outgoing = left_band[rows, p * edge : (p + 1) * edge]
            elif p >= shares - holders:
                outgoing = right_band[rows, begin : begin + edge]
            else:
                outgoing = jnp.zeros((depth, edge), F32)
            slab_ref[p, layer, :, share:] = outgoing
    slab_copy = pltpu.make_async_copy(slab_ref, slab_hbm, out_sem.at[3])
    slab_copy.start()
    part_rows = parts_ref.shape[1] - SUBLANES
    last_copies = [slab_copy]
    for step in range(shares):
        begin = pl.multiple_of(lax.rem(place_ref[0] + step, shares) * part_rows, SUBLANES)
        parts_ref[step, :part_rows, :] = grad_ref[pl.ds(begin, part_rows), :]
        parts_ref[step, part_rows:, :] = energy_ref[...]
        copy = pltpu.make_async_copy(parts_ref.at[step], parts_hbm[step], parts_sem.at[step])
        copy.start()
        last_copies.append(copy)
    for c in range(2):
        new_ref[c] = ext_ref[c, inner, mid] + sum_ref[c, inner, mid] * wide
        edge_left_ref[c] = sum_ref[c, inner, :margin] * scale
        edge_right_ref[c] = sum_ref[c, inner, far_side] * scale
    for k, (source, target) in enumerate(
        ((new_ref, new_hbm), (edge_left_ref, edge_left_hbm), (edge_right_ref, edge_right_hbm))
    ):
        copy = pltpu.make_async_copy(source, target, out_sem.at[k])
        copy.start()
        last_copies.append(copy)
    for copy in last_copies:
        copy.wait()


def patch_updates(
    rows, cols, count, place, own, left, right, probe, amplitudes, dual, shares, layers
):
    side = probe.shape[1]
    _, height, tile_cols = own.shape
    margin = left.shape[2]
    slots = amplitudes.shape[0]
    slab_rows = dual.shape[0]
    share = tile_cols // shares
    edge = min(share, margin)
    table = dft_table(side)
    extent = tile_cols + 2 * margin + LANES
    shape = jax.ShapeDtypeStruct
    slab_shape = (shares, layers, slab_rows // layers, share + edge)
    part_rows = 2 * side // shares + SUBLANES
    chain = [
        VMEM((2 * side, side), F32),
        VMEM((2 * side, side), BF16),
        VMEM((side, 2 * side), BF16),
        VMEM((side, 2 * side), F32),
    ]
    return pl.pallas_call(
        patch_kernel,
        in_specs=[SCALARS] * 4 + [ANYWHERE] * 7,
        out_specs=[ANYWHERE] * (4 + shares),
        out_shape=[
            shape((2, height, tile_cols), F32),
            shape((2, height, margin), F32),
            shape((2, height, margin), F32),
            shape(slab_shape, F32),
        ]
        + [shape((part_rows, side), F32)] * shares,
        scratch_shapes=[
            VMEM(probe.shape, F32),
            VMEM(amplitudes.shape, BF16),
            VMEM(table.shape, BF16),
            VMEM((2 * side, 2 * side), BF16),
            VMEM((2 * side, 2 * side), BF16),
            VMEM(dual.shape, F32),
            VMEM((2, height, tile_cols), F32),
            VMEM((2, height, margin), F32),
            VMEM((2, height, margin), F32),
            VMEM(slab_shape, F32),
            VMEM((shares, part_rows, side), F32),
            VMEM((2, height + SUBLANES, extent), F32),
            VMEM((2, height + SUBLANES, extent), F32),
            VMEM((2 * side, side), F32),
            VMEM((SUBLANES, side), F32),
            *chain,
            *chain,
            pltpu.SemaphoreType.DMA((6,)),
            pltpu.SemaphoreType.DMA((slots,)),
            pltpu.SemaphoreType.DMA((shares,)),
            pltpu.SemaphoreType.DMA((4,)),
        ],
        compiler_params=pltpu.CompilerParams(vmem_limit_bytes=VMEM_LIMIT),
        cost_estimate=pl.CostEstimate(
            flops=slots * 32 * side**3,
            bytes_accessed=8 * height * tile_cols * 4,
            transcendentals=slots * side * side,
        ),
        name="patches",
    )(
        rows,
        cols,
        count,
        place,
        own,
        left,
        right,
        probe,
        amplitudes,
        jnp.asarray(table),
        dual,
    )


def backward_kernel(
    ids_ref, residual_hbm, weights_hbm, out_ref, residual_ref, weights_ref, turned_ref, sem, weights_sem
):
    parts, projections, depth, share = residual_ref.shape
    both = projections * depth

    def weights_copy(a):
        return pltpu.make_async_copy(
            weights_hbm.at[ids_ref[a]], weights_ref.at[a], weights_sem.at[a]
        )

    residual_copy = pltpu.make_async_copy(residual_hbm, residual_ref, sem)
    residual_copy.start()
    for a in range(min(AHEAD, projections)):
        weights_copy(a).start()
    residual_copy.wait()
    for part in range(parts):
        block = residual_ref[part].astype(F32).reshape(both, share)
        turned_ref[part * share : (part + 1) * share, :] = block.T
    out_ref[...] = jnp.zeros(out_ref.shape, F32)

    members = math.gcd(projections, 2)

    @pl.loop(0, projections, step=members)
    def _(first):
        for a in range(members):
            weights_copy(first + a).wait()
        for a in range(members):
            item = first + a + AHEAD

            @pl.when(item < projections)
            def _():
                weights_copy(item).start()

        lane = lax.broadcasted_iota(jnp.int32, turned_ref.shape, 1)
        total = out_ref[...]
        for a in range(members):
            begin = (first + a) * depth
            kept = jnp.logical_and(lane >= begin, lane < begin + depth)
            chosen = jnp.where(kept, turned_ref[...], 0.0).astype(BF16)
            total += dot(weights_ref[first + a], chosen)
        out_ref[...] = total


def backward_sums(angle_ids, residual, proj_weights):
    _, rows, width = proj_weights.shape
    _, projections, depth, _ = residual.shape
    return pl.pallas_call(
        backward_kernel,
        in_specs=[SCALARS, ANYWHERE, ANYWHERE],
        out_specs=WHOLE,
        out_shape=jax.ShapeDtypeStruct((rows, projections * depth), F32),
        scratch_shapes=[
            VMEM(residual.shape, BF16),
            VMEM((projections, rows, width), BF16),
            VMEM((width, projections * depth), F32),
            DMA,
            pltpu.SemaphoreType.DMA((projections,)),
        ],
        compiler_params=pltpu.CompilerParams(vmem_limit_bytes=VMEM_LIMIT),
        cost_estimate=pl.CostEstimate(
            flops=2 * rows * width * projections * projections * depth,
            bytes_accessed=projections * rows * width * 2,
            transcendentals=0,
        ),
        name="backward",
    )(angle_ids, residual, proj_weights)


def update_kernel(
    ids_ref,
    sums_ref,
    rays_hbm,
    volume_hbm,
    out_hbm,
    rays_ref,
    stack_ref,
    spread_ref,
    volume_ref,
    done_ref,
    rays_sem,
    volume_sem,
    out_sem,
):
    depth = volume_ref.shape[0]
    slots = done_ref.shape[0]
    width = rays_ref.shape[1]
    projections = sums_ref.shape[1] // depth
    both = sums_ref.shape[1]

    def volume_copy(z):
        return pltpu.make_async_copy(volume_hbm.at[z], volume_ref.at[z], volume_sem.at[z])

    def out_copy(z):
        slot = lax.rem(z, slots)
        return pltpu.make_async_copy(done_ref.at[slot], out_hbm.at[z], out_sem.at[slot])

    rays_copy = pltpu.make_async_copy(rays_hbm, rays_ref, rays_sem)
    rays_copy.start()
    for z in range(min(UPDATE_AHEAD, depth)):
        volume_copy(z).start()
    high, low = split_bf16(sums_ref[...])
    stack_ref[...] = jnp.concatenate([high, low, high, low], axis=1)
    rays_copy.wait()
    rows = [
        jnp.broadcast_to(rays_ref[pl.ds(ids_ref[a], 1), :], (depth, width))
        for a in range(projections)
    ]
    high, low = split_bf16(jnp.concatenate(rows, axis=0))
    for place, block in enumerate((high, high, low, low)):
        spread_ref[place * both : (place + 1) * both, :] = block.astype(BF16)

    @pl.loop(0, depth)
    def _(z):
        volume_copy(z).wait()

        @pl.when(z + UPDATE_AHEAD < depth)
        def _():
            volume_copy(z + UPDATE_AHEAD).start()

        @pl.when(z >= slots)
        def _():
            out_copy(z - slots).wait()

        lane = lax.broadcasted_iota(jnp.int32, stack_ref.shape, 1)
        kept = lax.rem(lane, depth) == z
        chosen = jnp.where(kept, stack_ref[...], 0.0).astype(BF16)
        done_ref[lax.rem(z, slots)] = volume_ref[z] - tomo_step * dot(chosen, spread_ref[...])
        out_copy(z).start()

    for z in range(max(depth - slots, 0), depth):
        out_copy(z).wait()


def volume_update(angle_ids, sums, rays, volume):
    depth, rows, width = volume.shape
    slots = min(4, depth)
    return pl.pallas_call(
        update_kernel,
        in_specs=[SCALARS, WHOLE] + [ANYWHERE] * 2,
        out_specs=ANYWHERE,
        out_shape=jax.ShapeDtypeStruct(volume.shape, F32),
        scratch_shapes=[
            VMEM(rays.shape, F32),
            VMEM((rows, 4 * sums.shape[1]), F32),
            VMEM((4 * sums.shape[1], width), BF16),
            VMEM(volume.shape, F32),
            VMEM((slots, rows, width), F32),
            DMA,
            pltpu.SemaphoreType.DMA((depth,)),
            pltpu.SemaphoreType.DMA((slots,)),
        ],
        compiler_params=pltpu.CompilerParams(vmem_limit_bytes=VMEM_LIMIT),
        cost_estimate=pl.CostEstimate(
            flops=8 * rows * width * sums.shape[1] * depth,
            bytes_accessed=2 * depth * rows * width * 4,
            transcendentals=0,
        ),
        name="update",
    )(angle_ids, sums, rays, volume)


def gather_parts_kernel(group, *refs):
    *given, out_hbm, out_ref, sem = refs
    total = given[0][...]
    for ref in given[1:]:
        total = total + ref[...]
    blocks = total.shape[1] // LANES
    rows = (out_ref.shape[1] - SUBLANES) // blocks
    columns = [total[:, k * LANES : (k + 1) * LANES] for k in range(blocks)]
    energy = columns[0][group * rows :]
    for block in columns[1:]:
        energy = energy + block[group * rows :]
    for k in range(group):
        for place, block in enumerate(columns):
            out_ref[k, place * rows : (place + 1) * rows, :] = block[k * rows : (k + 1) * rows]
        out_ref[k, blocks * rows :, :] = energy
    copy = pltpu.make_async_copy(out_ref, out_hbm, sem)
    copy.start()
    copy.wait()


def gather_parts(given, group):
    total_rows, side = given[0].shape
    rows = (total_rows - SUBLANES) // group * (side // LANES) + SUBLANES
    shape = (group, rows, LANES)
    return pl.pallas_call(
        functools.partial(gather_parts_kernel, group),
        in_specs=[WHOLE] * len(given),
        out_specs=ANYWHERE,
        out_shape=jax.ShapeDtypeStruct(shape, F32),
        scratch_shapes=[VMEM(shape, F32), DMA],
        compiler_params=pltpu.CompilerParams(vmem_limit_bytes=SMALL_LIMIT),
        name="probe_parts",
    )(*given)


def probe_rows_kernel(given_ref, out_hbm, out_ref, sem):
    group, rows, _ = given_ref.shape
    receivers, taken, side = out_ref.shape
    total = given_ref[0]
    for k in range(1, group):
        total = total + given_ref[k]
    energy = jnp.sum(total[rows - SUBLANES :], keepdims=True) / (side * side)
    steps = total[: rows - SUBLANES] / (energy + 1e-05)
    steps = jnp.concatenate(
        [steps[k * taken : (k + 1) * taken] for k in range(side // LANES)], axis=1
    )
    for k in range(receivers):
        out_ref[k] = steps
    copy = pltpu.make_async_copy(out_ref, out_hbm, sem)
    copy.start()
    copy.wait()


def probe_rows(given, side, receivers):
    _, rows, _ = given.shape
    shape = (receivers, (rows - SUBLANES) * LANES // side, side)
    return pl.pallas_call(
        probe_rows_kernel,
        in_specs=[WHOLE],
        out_specs=ANYWHERE,
        out_shape=jax.ShapeDtypeStruct(shape, F32),
        scratch_shapes=[VMEM(shape, F32), DMA],
        compiler_params=pltpu.CompilerParams(vmem_limit_bytes=SMALL_LIMIT),
        name="probe_rows",
    )(given)


def turned(value, axis, steps):
    count = lax.axis_size(axis)
    return lax.ppermute(value, axis, [(k, (k + steps) % count) for k in range(count)])


def on_device(
    object_field,
    probe_field,
    amplitudes,
    pos_rows,
    pos_cols,
    counts,
    admm_dual,
    volume,
    proj_weights,
    ray_weights,
    angle_ids,
):
    margin = probe_field.shape[1] // 2
    own = object_field[0]
    tile_cols = own.shape[2]
    flat_axes = ("tile", "proj")
    plane = lax.axis_size("tile") * lax.axis_size("proj")
    proj_count = lax.axis_size("proj")
    layers = lax.axis_size("cuts")
    from_left = shifted(own[:, :, tile_cols - margin :], "tile", 1)
    from_right = shifted(own[:, :, :margin], "tile", -1)
    forward = forward_parts(angle_ids, volume, proj_weights, ray_weights, plane)
    _, from_left, from_right = lax.optimization_barrier((forward, from_left, from_right))
    arrived = lax.all_to_all(forward, flat_axes, 0, 0, tiled=True)
    place = lax.axis_index("proj")
    partial_object, edge_left, edge_right, slab, *grad_parts = patch_updates(
        pos_rows[0, 0],
        pos_cols[0, 0],
        counts[0],
        place[None],
        own,
        from_left,
        from_right,
        probe_field,
        amplitudes[0, 0],
        admm_dual[0],
        proj_count,
        layers,
    )

    share = tile_cols // proj_count
    edge = slab.shape[3] - share
    holders = margin // edge
    slab, arrived = lax.optimization_barrier((slab, arrived))
    pieces = slab.reshape(proj_count * layers, *slab.shape[2:])
    pieces = lax.all_to_all(pieces, ("proj", "cuts"), 0, 0, tiled=True)
    pieces, grad_parts = lax.optimization_barrier((pieces, grad_parts))
    pairs = []
    for tile in range(lax.axis_size("tile") - 1):
        for k in range(holders):
            lower = tile * proj_count + proj_count - holders + k
            upper = (tile + 1) * proj_count + k
            pairs += [(lower, upper), (upper, lower)]
    grads_in = lax.ppermute(pieces[:, :, share:], flat_axes, pairs)
    at_start = jnp.pad(grads_in, ((0, 0), (0, 0), (0, share - edge)))
    at_end = jnp.pad(grads_in, ((0, 0), (0, 0), (share - edge, 0)))
    target = pieces[:, :, :share] + jnp.where(place < holders, at_start, at_end)
    residual = (jnp.sum(arrived, axis=0) - target).astype(BF16)
    copies = jnp.broadcast_to(residual[None], (plane, *residual.shape))

    group_axes = ("tile", "cuts")
    group = lax.axis_size("tile") * layers
    given = [grad_parts[0]]
    for step in range(1, proj_count):
        given.append(turned(grad_parts[step], "proj", step))
    copies, given = lax.optimization_barrier((copies, given))
    residual = lax.all_to_all(copies, flat_axes, 0, 0, tiled=True)
    by_receiver = gather_parts(given, group)
    residual, by_receiver, edge_left, edge_right = lax.optimization_barrier(
        (residual, by_receiver, edge_left, edge_right)
    )
    received = lax.all_to_all(by_receiver, group_axes, 0, 0, tiled=True)
    edge_from_left = shifted(edge_right, "tile", 1)
    back_sums = backward_sums(angle_ids, residual, proj_weights)
    back_sums, received, edge_left = lax.optimization_barrier((back_sums, received, edge_left))
    edge_from_right = shifted(edge_left, "tile", -1)
    steps = probe_rows(received, probe_field.shape[1], plane * layers)
    back_sums, steps, edge_from_left = lax.optimization_barrier(
        (back_sums, steps, edge_from_left)
    )
    steps = lax.all_to_all(steps, ("proj", "tile", "cuts"), 0, 0, tiled=True)
    new_volume = volume_update(angle_ids, back_sums, ray_weights, volume)
    new_volume, steps = lax.optimization_barrier((new_volume, steps))
    new_probe = probe_field + steps.reshape(probe_field.shape)
    rest = tile_cols - margin
    new_object = (
        partial_object
        + jnp.pad(edge_from_left, ((0, 0), (0, 0), (0, rest)))
        + jnp.pad(edge_from_right, ((0, 0), (0, 0), (rest, 0)))
    )
    return (new_object[None], new_probe, new_volume)


def solution(mesh):
    in_specs = (
        P(("proj", "cuts"), None, None, "tile"),
        P(),
        P(("proj", "cuts"), "tile", None, None, None),
        P(("proj", "cuts"), "tile", None),
        P(("proj", "cuts"), "tile", None),
        P(("proj", "cuts"), "tile"),
        P(("proj", "cuts"), None, "tile"),
        P("cuts", ("tile", "proj"), None),
        P(None, ("tile", "proj"), None),
        P(),
        P(),
    )
    out_specs = (P(("proj", "cuts"), None, None, "tile"), P(), P("cuts", ("tile", "proj"), None))
    return jax.shard_map(
        on_device, mesh=mesh, in_specs=in_specs, out_specs=out_specs, check_vma=False
    )
```

```python
import functools
import math

import jax
import jax.numpy as jnp
import numpy as np
from jax import lax
from jax.experimental import pallas as pl
from jax.experimental.pallas import tpu as pltpu
from jax.sharding import PartitionSpec as P

VMEM_LIMIT = 60 * 1024 * 1024
VMEM = pltpu.VMEM
F32 = jnp.float32
BF16 = jnp.bfloat16
LANES = 128
SUBLANES = 8
AHEAD = 4
UPDATE_AHEAD = 6
FORWARD_LIMIT = 44 * 1024 * 1024
SMALL_LIMIT = 16 * 1024 * 1024
ANYWHERE = pl.BlockSpec(memory_space=pl.ANY)
WHOLE = pl.BlockSpec(memory_space=pltpu.VMEM)
SCALARS = pl.BlockSpec(memory_space=pltpu.SMEM)
DMA = pltpu.SemaphoreType.DMA

tomo_step = 1.0


def shifted(value, axis, steps):
    count = lax.axis_size(axis)
    leading, last = (max(0, -steps), min(count, count - steps))
    return lax.ppermute(value, axis, [(source, source + steps) for source in range(leading, last)])


def dft_table(side):
    indices = np.arange(side)
    products = (indices[:, None] * indices[None, :]) % side
    phase = products.astype(np.float32) * np.float32(2.0 * math.pi / side)
    norm = np.float32(1.0 / math.sqrt(side))
    real = np.cos(phase).astype(np.float32) * norm
    imag = -np.sin(phase).astype(np.float32) * norm
    return np.stack([real, imag]).astype(jnp.bfloat16)


def dot(left, right):
    return jnp.dot(left, right, preferred_element_type=F32)


def split_bf16(values):
    high = values.astype(BF16).astype(F32)
    low = (values - high).astype(BF16).astype(F32)
    return high, low


def forward_kernel(
    ids_ref,
    rays_hbm,
    volume_hbm,
    weights_hbm,
    out_hbm,
    rays_ref,
    volume_ref,
    weights_ref,
    out_ref,
    table_ref,
    sums_ref,
    rays_sem,
    volume_sem,
    weights_sem,
    out_sem,
):
    depth, projections, _ = sums_ref.shape
    width, lanes = table_ref.shape
    parts, _, _, share = out_ref.shape

    def volume_copy(z):
        return pltpu.make_async_copy(volume_hbm.at[z], volume_ref.at[z], volume_sem.at[z])

    def weights_copy(a):
        return pltpu.make_async_copy(
            weights_hbm.at[ids_ref[a]], weights_ref.at[a], weights_sem.at[a]
        )

    def out_copy(a):
        return pltpu.make_async_copy(out_ref.at[:, a], out_hbm.at[:, a], out_sem.at[a])

    rays_copy = pltpu.make_async_copy(rays_hbm, rays_ref, rays_sem)
    rays_copy.start()
    for z in range(min(AHEAD, depth)):
        volume_copy(z).start()
    for a in range(min(max(AHEAD - depth, 0), projections)):
        weights_copy(a).start()

    rays_copy.wait()
    rows = jnp.concatenate([rays_ref[pl.ds(ids_ref[a], 1), :] for a in range(projections)], axis=0)
    high, low = split_bf16(rows)
    stacked = [high, low]
    if lanes > 2 * projections:
        stacked.append(jnp.zeros((lanes - 2 * projections, width), F32))
    table_ref[...] = jnp.concatenate(stacked, axis=0).T.astype(BF16)

    @pl.loop(0, depth)
    def _(z):
        volume_copy(z).wait()

        @pl.when(z + AHEAD < depth)
        def _():
            volume_copy(z + AHEAD).start()

        @pl.when(jnp.logical_and(z + AHEAD >= depth, z + AHEAD - depth < projections))
        def _():
            weights_copy(z + AHEAD - depth).start()

        piece = min(512, width)
        total = None
        for k in range(0, width, piece):
            block = volume_ref[z, :, k : k + piece]
            high = block.astype(BF16)
            low = (block - high.astype(F32)).astype(BF16)
            stacked = jnp.concatenate([high, low], axis=0)
            part = dot(stacked, table_ref[k : k + piece, :])
            total = part if total is None else total + part
        rows = volume_ref.shape[1]
        total = (total[:rows] + total[rows:]).T
        sums_ref[z] = total[:projections] + total[projections : 2 * projections]

    @pl.loop(0, projections)
    def _(a):
        weights_copy(a).wait()

        @pl.when(a + AHEAD < projections)
        def _():
            weights_copy(a + AHEAD).start()

        rows = sums_ref[:, pl.ds(a, 1), :].reshape(depth, sums_ref.shape[2])
        result = dot(rows.astype(BF16), weights_ref[a])
        for part in range(parts):
            out_ref[part, a] = result[:, part * share : (part + 1) * share]
        out_copy(a).start()

    @pl.loop(0, projections)
    def _(a):
        out_copy(a).wait()


def forward_parts(angle_ids, volume, proj_weights, ray_weights, parts):
    depth, rows, width = volume.shape
    projections = angle_ids.shape[0]
    lanes = -(-2 * projections // LANES) * LANES
    share = width // parts
    return pl.pallas_call(
        forward_kernel,
        in_specs=[SCALARS] + [ANYWHERE] * 3,
        out_specs=ANYWHERE,
        out_shape=jax.ShapeDtypeStruct((parts, projections, depth, share), F32),
        scratch_shapes=[
            VMEM(ray_weights.shape, F32),
            VMEM(volume.shape, F32),
            VMEM((projections, rows, width), BF16),
            VMEM((parts, projections, depth, share), F32),
            VMEM((width, lanes), BF16),
            VMEM((depth, projections, rows), F32),
            DMA,
            pltpu.SemaphoreType.DMA((depth,)),
            pltpu.SemaphoreType.DMA((projections,)),
            pltpu.SemaphoreType.DMA((projections,)),
        ],
        compiler_params=pltpu.CompilerParams(vmem_limit_bytes=FORWARD_LIMIT),
        cost_estimate=pl.CostEstimate(
            flops=4 * depth * rows * width * lanes,
            bytes_accessed=depth * rows * width * 4 + projections * rows * width * 2,
            transcendentals=0,
        ),
        name="forward",
    )(angle_ids, ray_weights, volume, proj_weights)


def placed(values, down, across):
    rows, cols = values.shape
    tall = jnp.concatenate([values, jnp.zeros((SUBLANES, cols), F32)], axis=0)
    tall = pltpu.roll(tall, down, axis=0)
    wide = jnp.concatenate([tall, jnp.zeros((rows + SUBLANES, LANES), F32)], axis=1)
    return pltpu.roll(wide, across, axis=1)


def patch_kernel(
    rows_ref,
    cols_ref,
    count_ref,
    place_ref,
    own_hbm,
    left_hbm,
    right_hbm,
    probe_hbm,
    amp_hbm,
    table_hbm,
    dual_hbm,
    new_hbm,
    edge_left_hbm,
    edge_right_hbm,
    slab_hbm,
    *rest,
):
    shares = len(rest) - 27
    parts_hbm = rest[:shares]
    (
        probe_ref,
        amp_ref,
        table_ref,
        dft_a_ref,
        dft_b_ref,
        dual_ref,
        new_ref,
        edge_left_ref,
        edge_right_ref,
        slab_ref,
        parts_ref,
        ext_ref,
        sum_ref,
        grad_ref,
        energy_ref,
        *chain_refs,
        in_sem,
        amp_sem,
        parts_sem,
        out_sem,
    ) = rest[shares:]
    chain_refs = [chain_refs[k : k + 4] for k in range(0, len(chain_refs), 4)]
    side = probe_ref.shape[1]
    _, height, margin = edge_left_ref.shape
    tile_cols = new_ref.shape[2]
    window = side + LANES
    chunk = 32
    tall = chunk + SUBLANES
    inner = pl.ds(0, height)

    copies = [
        pltpu.make_async_copy(source, target, in_sem.at[k])
        for k, (source, target) in enumerate(
            (
                (left_hbm, ext_ref.at[:, inner, pl.ds(0, margin)]),
                (own_hbm, ext_ref.at[:, inner, pl.ds(margin, tile_cols)]),
                (right_hbm, ext_ref.at[:, inner, pl.ds(margin + tile_cols, margin)]),
                (probe_hbm, probe_ref),
                (table_hbm, table_ref),
                (dual_hbm, dual_ref),
            )
        )
    ]
    for copy in copies:
        copy.start()
    live_count = count_ref[0]

    def amp_copy(k):
        return pltpu.make_async_copy(amp_hbm.at[k], amp_ref.at[k], amp_sem.at[k])

    @pl.loop(0, live_count)
    def _(k):
        amp_copy(k).start()

    sum_ref[...] = jnp.zeros(sum_ref.shape, F32)
    grad_ref[...] = jnp.zeros(grad_ref.shape, F32)
    energy_ref[...] = jnp.zeros(energy_ref.shape, F32)
    for copy in copies:
        copy.wait()
    real = table_ref[0]
    imag = table_ref[1]
    for ref, sign in ((dft_a_ref, -1), (dft_b_ref, 1)):
        ref[:side, :side] = real
        ref[side:, side:] = real
        ref[:side, side:] = sign * imag
        ref[side:, :side] = -sign * imag

    @pl.loop(0, live_count)
    def _(k):
        amp_copy(k).wait()

    def pair_step(pair, carry):
        chains = []
        for k, refs in enumerate(chain_refs):
            slot = jnp.minimum(2 * pair + k, live_count - 1)
            live = (2 * pair + k < live_count).astype(F32)
            row = rows_ref[slot]
            col = cols_ref[slot]
            lane = lax.rem(col, LANES)
            notch = lax.rem(row, SUBLANES)
            base = pl.multiple_of(col - lane, LANES)
            top = pl.multiple_of(row - notch, SUBLANES)
            chains.append((slot, live, lane, notch, base, top, *refs))
        for slot, live, lane, notch, base, top, patch_ref, wave_ref, half_ref, far_ref in chains:
            back_shift = lax.rem(window - lane, window)
            up_shift = lax.rem(tall - notch, tall)
            for r in range(0, side, chunk):
                cells = pl.ds(top + r, tall)
                here = slice(r, r + chunk)
                below = slice(side + r, side + r + chunk)
                x_re = pltpu.roll(ext_ref[0, cells, pl.ds(base, window)], back_shift, axis=1)
                x_im = pltpu.roll(ext_ref[1, cells, pl.ds(base, window)], back_shift, axis=1)
                x_re = pltpu.roll(x_re[:, :side], up_shift, axis=0)[:chunk]
                x_im = pltpu.roll(x_im[:, :side], up_shift, axis=0)[:chunk]
                p_re = probe_ref[0, here, :]
                p_im = probe_ref[1, here, :]
                patch_ref[here, :] = x_re
                patch_ref[below, :] = x_im
                wave_ref[here, :] = (p_re * x_re - p_im * x_im).astype(BF16)
                wave_ref[below, :] = (p_re * x_im + p_im * x_re).astype(BF16)
                power = x_re * x_re + x_im * x_im
                energy_ref[...] += live * jnp.sum(
                    power.reshape(chunk // SUBLANES, SUBLANES, side), axis=0
                )
        for *_, wave_ref, half_ref, far_ref in chains:
            half_ref[:, :side] = dot(dft_a_ref[:side, :], wave_ref[...]).astype(BF16)
            half_ref[:, side:] = dot(dft_a_ref[side:, :], wave_ref[...]).astype(BF16)
        for *_, half_ref, far_ref in chains:
            far_ref[...] = dot(half_ref[...], dft_b_ref[...])
        for slot, live, *_, wave_ref, half_ref, far_ref in chains:
            for r in range(0, side, chunk):
                here = slice(r, r + chunk)
                below = slice(side + r, side + r + chunk)
                f_re = far_ref[here, :side]
                f_im = far_ref[here, side:]
                inverse = lax.rsqrt(f_re * f_re + f_im * f_im + 0.25)
                factor = amp_ref[slot, here, :].astype(F32) * inverse - 1.0
                wave_ref[here, :] = (f_re * factor).astype(BF16)
                wave_ref[below, :] = (f_im * factor).astype(BF16)
        for *_, wave_ref, half_ref, far_ref in chains:
            half_ref[:, :side] = dot(dft_b_ref[:side, :], wave_ref[...]).astype(BF16)
            half_ref[:, side:] = dot(dft_b_ref[side:, :], wave_ref[...]).astype(BF16)
        for *_, half_ref, far_ref in chains:
            far_ref[...] = dot(half_ref[...], dft_a_ref[...])
        for slot, live, lane, notch, base, top, patch_ref, wave_ref, half_ref, far_ref in chains:
            for r in range(0, side, chunk):
                cells = pl.ds(top + r, tall)
                here = slice(r, r + chunk)
                below = slice(side + r, side + r + chunk)
                b_re = live * far_ref[here, :side]
                b_im = live * far_ref[here, side:]
                p_re = probe_ref[0, here, :]
                p_im = probe_ref[1, here, :]
                x_re = patch_ref[here, :]
                x_im = patch_ref[below, :]
                o_re = p_re * b_re + p_im * b_im
                o_im = p_re * b_im - p_im * b_re
                sum_ref[0, cells, pl.ds(base, window)] += placed(o_re, notch, lane)
                sum_ref[1, cells, pl.ds(base, window)] += placed(o_im, notch, lane)
                grad_ref[here, :] += x_re * b_re + x_im * b_im
                grad_ref[below, :] += x_re * b_im - x_im * b_re
        return carry

    lax.fori_loop(0, lax.div(live_count + 1, 2), pair_step, 0)

    p_re = probe_ref[0]
    p_im = probe_ref[1]
    peak = jnp.max(p_re * p_re + p_im * p_im)
    scale = 1.0 / (jnp.full((1, LANES), peak, F32) + 1e-05)
    wide = jnp.tile(scale, (1, tile_cols // LANES))
    shares, layers, depth, share = slab_ref.shape
    edge = min(share - tile_cols // shares, margin)
    share -= edge
    holders = margin // edge
    first = (height - layers * depth) // 2
    band = pl.ds(first, layers * depth)
    mid = slice(margin, margin + tile_cols)
    far_side = slice(margin + tile_cols, 2 * margin + tile_cols)
    own_band = ext_ref[1, band, mid] + sum_ref[1, band, mid] * wide + dual_ref[...]
    left_band = sum_ref[1, band, :margin] * scale
    right_band = sum_ref[1, band, far_side] * scale
    for layer in range(layers):
        rows = slice(layer * depth, (layer + 1) * depth)
        for p in range(shares):
            slab_ref[p, layer, :, :share] = own_band[rows, p * share : (p + 1) * share]
            begin = (p - shares + holders) * edge
            if p < holders:
                outgoing = left_band[rows, p * edge : (p + 1) * edge]
            elif p >= shares - holders:
                outgoing = right_band[rows, begin : begin + edge]
            else:
                outgoing = jnp.zeros((depth, edge), F32)
            slab_ref[p, layer, :, share:] = outgoing
    slab_copy = pltpu.make_async_copy(slab_ref, slab_hbm, out_sem.at[3])
    slab_copy.start()
    part_rows = parts_ref.shape[1] - SUBLANES
    last_copies = [slab_copy]
    for step in range(shares):
        begin = pl.multiple_of(lax.rem(place_ref[0] + step, shares) * part_rows, SUBLANES)
        parts_ref[step, :part_rows, :] = grad_ref[pl.ds(begin, part_rows), :]
        parts_ref[step, part_rows:, :] = energy_ref[...]
        copy = pltpu.make_async_copy(parts_ref.at[step], parts_hbm[step], parts_sem.at[step])
        copy.start()
        last_copies.append(copy)
    for c in range(2):
        new_ref[c] = ext_ref[c, inner, mid] + sum_ref[c, inner, mid] * wide
        edge_left_ref[c] = (sum_ref[c, inner, :margin] * scale).astype(BF16)
        edge_right_ref[c] = (sum_ref[c, inner, far_side] * scale).astype(BF16)
    for k, (source, target) in enumerate(
        ((new_ref, new_hbm), (edge_left_ref, edge_left_hbm), (edge_right_ref, edge_right_hbm))
    ):
        copy = pltpu.make_async_copy(source, target, out_sem.at[k])
        copy.start()
        last_copies.append(copy)
    for copy in last_copies:
        copy.wait()


def patch_updates(
    rows, cols, count, place, own, left, right, probe, amplitudes, dual, shares, layers
):
    side = probe.shape[1]
    _, height, tile_cols = own.shape
    margin = left.shape[2]
    slots = amplitudes.shape[0]
    slab_rows = dual.shape[0]
    share = tile_cols // shares
    edge = min(share, margin)
    table = dft_table(side)
    extent = tile_cols + 2 * margin + LANES
    shape = jax.ShapeDtypeStruct
    slab_shape = (shares, layers, slab_rows // layers, share + edge)
    part_rows = 2 * side // shares + SUBLANES
    chain = [
        VMEM((2 * side, side), F32),
        VMEM((2 * side, side), BF16),
        VMEM((side, 2 * side), BF16),
        VMEM((side, 2 * side), F32),
    ]
    return pl.pallas_call(
        patch_kernel,
        in_specs=[SCALARS] * 4 + [ANYWHERE] * 7,
        out_specs=[ANYWHERE] * (4 + shares),
        out_shape=[
            shape((2, height, tile_cols), F32),
            shape((2, height, margin), BF16),
            shape((2, height, margin), BF16),
            shape(slab_shape, F32),
        ]
        + [shape((part_rows, side), F32)] * shares,
        scratch_shapes=[
            VMEM(probe.shape, F32),
            VMEM(amplitudes.shape, BF16),
            VMEM(table.shape, BF16),
            VMEM((2 * side, 2 * side), BF16),
            VMEM((2 * side, 2 * side), BF16),
            VMEM(dual.shape, F32),
            VMEM((2, height, tile_cols), F32),
            VMEM((2, height, margin), BF16),
            VMEM((2, height, margin), BF16),
            VMEM(slab_shape, F32),
            VMEM((shares, part_rows, side), F32),
            VMEM((2, height + SUBLANES, extent), F32),
            VMEM((2, height + SUBLANES, extent), F32),
            VMEM((2 * side, side), F32),
            VMEM((SUBLANES, side), F32),
            *chain,
            *chain,
            pltpu.SemaphoreType.DMA((6,)),
            pltpu.SemaphoreType.DMA((slots,)),
            pltpu.SemaphoreType.DMA((shares,)),
            pltpu.SemaphoreType.DMA((4,)),
        ],
        compiler_params=pltpu.CompilerParams(vmem_limit_bytes=VMEM_LIMIT),
        cost_estimate=pl.CostEstimate(
            flops=slots * 32 * side**3,
            bytes_accessed=8 * height * tile_cols * 4,
            transcendentals=slots * side * side,
        ),
        name="patches",
    )(
        rows,
        cols,
        count,
        place,
        own,
        left,
        right,
        probe,
        amplitudes,
        jnp.asarray(table),
        dual,
    )


def backward_kernel(
    ids_ref, residual_hbm, weights_hbm, out_ref, residual_ref, weights_ref, turned_ref, sem, weights_sem
):
    parts, projections, depth, share = residual_ref.shape
    both = projections * depth

    def weights_copy(a):
        return pltpu.make_async_copy(
            weights_hbm.at[ids_ref[a]], weights_ref.at[a], weights_sem.at[a]
        )

    residual_copy = pltpu.make_async_copy(residual_hbm, residual_ref, sem)
    residual_copy.start()
    for a in range(min(AHEAD, projections)):
        weights_copy(a).start()
    residual_copy.wait()
    for part in range(parts):
        block = residual_ref[part].astype(F32).reshape(both, share)
        turned_ref[part * share : (part + 1) * share, :] = block.T
    out_ref[...] = jnp.zeros(out_ref.shape, F32)

    members = math.gcd(projections, 2)

    @pl.loop(0, projections, step=members)
    def _(first):
        for a in range(members):
            weights_copy(first + a).wait()
        for a in range(members):
            item = first + a + AHEAD

            @pl.when(item < projections)
            def _():
                weights_copy(item).start()

        lane = lax.broadcasted_iota(jnp.int32, turned_ref.shape, 1)
        total = out_ref[...]
        for a in range(members):
            begin = (first + a) * depth
            kept = jnp.logical_and(lane >= begin, lane < begin + depth)
            chosen = jnp.where(kept, turned_ref[...], 0.0).astype(BF16)
            total += dot(weights_ref[first + a], chosen)
        out_ref[...] = total


def backward_sums(angle_ids, residual, proj_weights):
    _, rows, width = proj_weights.shape
    _, projections, depth, _ = residual.shape
    return pl.pallas_call(
        backward_kernel,
        in_specs=[SCALARS, ANYWHERE, ANYWHERE],
        out_specs=WHOLE,
        out_shape=jax.ShapeDtypeStruct((rows, projections * depth), F32),
        scratch_shapes=[
            VMEM(residual.shape, BF16),
            VMEM((projections, rows, width), BF16),
            VMEM((width, projections * depth), F32),
            DMA,
            pltpu.SemaphoreType.DMA((projections,)),
        ],
        compiler_params=pltpu.CompilerParams(vmem_limit_bytes=VMEM_LIMIT),
        cost_estimate=pl.CostEstimate(
            flops=2 * rows * width * projections * projections * depth,
            bytes_accessed=projections * rows * width * 2,
            transcendentals=0,
        ),
        name="backward",
    )(angle_ids, residual, proj_weights)


def update_kernel(
    ids_ref,
    sums_ref,
    rays_hbm,
    volume_hbm,
    out_hbm,
    rays_ref,
    stack_ref,
    spread_ref,
    volume_ref,
    done_ref,
    rays_sem,
    volume_sem,
    out_sem,
):
    depth = volume_ref.shape[0]
    slots = done_ref.shape[0]
    width = rays_ref.shape[1]
    projections = sums_ref.shape[1] // depth
    both = sums_ref.shape[1]

    def volume_copy(z):
        return pltpu.make_async_copy(volume_hbm.at[z], volume_ref.at[z], volume_sem.at[z])

    def out_copy(z):
        slot = lax.rem(z, slots)
        return pltpu.make_async_copy(done_ref.at[slot], out_hbm.at[z], out_sem.at[slot])

    rays_copy = pltpu.make_async_copy(rays_hbm, rays_ref, rays_sem)
    rays_copy.start()
    for z in range(min(UPDATE_AHEAD, depth)):
        volume_copy(z).start()
    high, low = split_bf16(sums_ref[...])
    stack_ref[...] = jnp.concatenate([high, low, high, low], axis=1)
    rays_copy.wait()
    rows = [
        jnp.broadcast_to(rays_ref[pl.ds(ids_ref[a], 1), :], (depth, width))
        for a in range(projections)
    ]
    high, low = split_bf16(jnp.concatenate(rows, axis=0))
    for place, block in enumerate((high, high, low, low)):
        spread_ref[place * both : (place + 1) * both, :] = block.astype(BF16)

    @pl.loop(0, depth)
    def _(z):
        volume_copy(z).wait()

        @pl.when(z + UPDATE_AHEAD < depth)
        def _():
            volume_copy(z + UPDATE_AHEAD).start()

        @pl.when(z >= slots)
        def _():
            out_copy(z - slots).wait()

        lane = lax.broadcasted_iota(jnp.int32, stack_ref.shape, 1)
        kept = lax.rem(lane, depth) == z
        chosen = jnp.where(kept, stack_ref[...], 0.0).astype(BF16)
        done_ref[lax.rem(z, slots)] = volume_ref[z] - tomo_step * dot(chosen, spread_ref[...])
        out_copy(z).start()

    for z in range(max(depth - slots, 0), depth):
        out_copy(z).wait()


def volume_update(angle_ids, sums, rays, volume):
    depth, rows, width = volume.shape
    slots = min(4, depth)
    return pl.pallas_call(
        update_kernel,
        in_specs=[SCALARS, WHOLE] + [ANYWHERE] * 2,
        out_specs=ANYWHERE,
        out_shape=jax.ShapeDtypeStruct(volume.shape, F32),
        scratch_shapes=[
            VMEM(rays.shape, F32),
            VMEM((rows, 4 * sums.shape[1]), F32),
            VMEM((4 * sums.shape[1], width), BF16),
            VMEM(volume.shape, F32),
            VMEM((slots, rows, width), F32),
            DMA,
            pltpu.SemaphoreType.DMA((depth,)),
            pltpu.SemaphoreType.DMA((slots,)),
        ],
        compiler_params=pltpu.CompilerParams(vmem_limit_bytes=VMEM_LIMIT),
        cost_estimate=pl.CostEstimate(
            flops=8 * rows * width * sums.shape[1] * depth,
            bytes_accessed=2 * depth * rows * width * 4,
            transcendentals=0,
        ),
        name="update",
    )(angle_ids, sums, rays, volume)


def gather_parts_kernel(group, *refs):
    *given, out_hbm, out_ref, sem = refs
    total = given[0][...]
    for ref in given[1:]:
        total = total + ref[...]
    blocks = total.shape[1] // LANES
    rows = (out_ref.shape[1] - SUBLANES) // blocks
    columns = [total[:, k * LANES : (k + 1) * LANES] for k in range(blocks)]
    energy = columns[0][group * rows :]
    for block in columns[1:]:
        energy = energy + block[group * rows :]
    for k in range(group):
        for place, block in enumerate(columns):
            out_ref[k, place * rows : (place + 1) * rows, :] = block[k * rows : (k + 1) * rows]
        out_ref[k, blocks * rows :, :] = energy
    copy = pltpu.make_async_copy(out_ref, out_hbm, sem)
    copy.start()
    copy.wait()


def gather_parts(given, group):
    total_rows, side = given[0].shape
    rows = (total_rows - SUBLANES) // group * (side // LANES) + SUBLANES
    shape = (group, rows, LANES)
    return pl.pallas_call(
        functools.partial(gather_parts_kernel, group),
        in_specs=[WHOLE] * len(given),
        out_specs=ANYWHERE,
        out_shape=jax.ShapeDtypeStruct(shape, F32),
        scratch_shapes=[VMEM(shape, F32), DMA],
        compiler_params=pltpu.CompilerParams(vmem_limit_bytes=SMALL_LIMIT),
        name="probe_parts",
    )(*given)


def probe_rows_kernel(given_ref, out_hbm, out_ref, sem):
    group, rows, _ = given_ref.shape
    receivers, taken, side = out_ref.shape
    total = given_ref[0]
    for k in range(1, group):
        total = total + given_ref[k]
    energy = jnp.sum(total[rows - SUBLANES :], keepdims=True) / (side * side)
    steps = total[: rows - SUBLANES] / (energy + 1e-05)
    steps = jnp.concatenate(
        [steps[k * taken : (k + 1) * taken] for k in range(side // LANES)], axis=1
    )
    for k in range(receivers):
        out_ref[k] = steps
    copy = pltpu.make_async_copy(out_ref, out_hbm, sem)
    copy.start()
    copy.wait()


def probe_rows(given, side, receivers):
    _, rows, _ = given.shape
    shape = (receivers, (rows - SUBLANES) * LANES // side, side)
    return pl.pallas_call(
        probe_rows_kernel,
        in_specs=[WHOLE],
        out_specs=ANYWHERE,
        out_shape=jax.ShapeDtypeStruct(shape, F32),
        scratch_shapes=[VMEM(shape, F32), DMA],
        compiler_params=pltpu.CompilerParams(vmem_limit_bytes=SMALL_LIMIT),
        name="probe_rows",
    )(given)


def turned(value, axis, steps):
    count = lax.axis_size(axis)
    return lax.ppermute(value, axis, [(k, (k + steps) % count) for k in range(count)])


def on_device(
    object_field,
    probe_field,
    amplitudes,
    pos_rows,
    pos_cols,
    counts,
    admm_dual,
    volume,
    proj_weights,
    ray_weights,
    angle_ids,
):
    margin = probe_field.shape[1] // 2
    own = object_field[0]
    tile_cols = own.shape[2]
    flat_axes = ("tile", "proj")
    plane = lax.axis_size("tile") * lax.axis_size("proj")
    proj_count = lax.axis_size("proj")
    layers = lax.axis_size("cuts")
    from_left = shifted(own[:, :, tile_cols - margin :], "tile", 1)
    from_right = shifted(own[:, :, :margin], "tile", -1)
    forward = forward_parts(angle_ids, volume, proj_weights, ray_weights, plane)
    _, from_left, from_right = lax.optimization_barrier((forward, from_left, from_right))
    arrived = lax.all_to_all(forward, flat_axes, 0, 0, tiled=True)
    place = lax.axis_index("proj")
    partial_object, edge_left, edge_right, slab, *grad_parts = patch_updates(
        pos_rows[0, 0],
        pos_cols[0, 0],
        counts[0],
        place[None],
        own,
        from_left,
        from_right,
        probe_field,
        amplitudes[0, 0],
        admm_dual[0],
        proj_count,
        layers,
    )

    share = tile_cols // proj_count
    edge = slab.shape[3] - share
    holders = margin // edge
    slab, arrived = lax.optimization_barrier((slab, arrived))
    pieces = slab.reshape(proj_count * layers, *slab.shape[2:])
    pieces = lax.all_to_all(pieces, ("proj", "cuts"), 0, 0, tiled=True)
    pieces, grad_parts = lax.optimization_barrier((pieces, grad_parts))
    pairs = []
    for tile in range(lax.axis_size("tile") - 1):
        for k in range(holders):
            lower = tile * proj_count + proj_count - holders + k
            upper = (tile + 1) * proj_count + k
            pairs += [(lower, upper), (upper, lower)]
    grads_in = lax.ppermute(pieces[:, :, share:], flat_axes, pairs)
    at_start = jnp.pad(grads_in, ((0, 0), (0, 0), (0, share - edge)))
    at_end = jnp.pad(grads_in, ((0, 0), (0, 0), (share - edge, 0)))
    target = pieces[:, :, :share] + jnp.where(place < holders, at_start, at_end)
    residual = (jnp.sum(arrived, axis=0) - target).astype(BF16)
    copies = jnp.broadcast_to(residual[None], (plane, *residual.shape))

    group_axes = ("tile", "cuts")
    group = lax.axis_size("tile") * layers
    given = [grad_parts[0]]
    for step in range(1, proj_count):
        given.append(turned(grad_parts[step], "proj", step))
    copies, given = lax.optimization_barrier((copies, given))
    residual = lax.all_to_all(copies, flat_axes, 0, 0, tiled=True)
    by_receiver = gather_parts(given, group)
    residual, by_receiver, edge_left, edge_right = lax.optimization_barrier(
        (residual, by_receiver, edge_left, edge_right)
    )
    received = lax.all_to_all(by_receiver, group_axes, 0, 0, tiled=True)
    edge_from_left = shifted(edge_right, "tile", 1)
    back_sums = backward_sums(angle_ids, residual, proj_weights)
    back_sums, received, edge_left = lax.optimization_barrier((back_sums, received, edge_left))
    edge_from_right = shifted(edge_left, "tile", -1)
    steps = probe_rows(received, probe_field.shape[1], plane * layers)
    back_sums, steps, edge_from_left = lax.optimization_barrier(
        (back_sums, steps, edge_from_left)
    )
    steps = lax.all_to_all(steps, ("proj", "tile", "cuts"), 0, 0, tiled=True)
    new_volume = volume_update(angle_ids, back_sums, ray_weights, volume)
    new_volume, steps = lax.optimization_barrier((new_volume, steps))
    new_probe = probe_field + steps.reshape(probe_field.shape)
    rest = tile_cols - margin
    new_object = (
        partial_object
        + jnp.pad(edge_from_left.astype(F32), ((0, 0), (0, 0), (0, rest)))
        + jnp.pad(edge_from_right.astype(F32), ((0, 0), (0, 0), (rest, 0)))
    )
    return (new_object[None], new_probe, new_volume)


def solution(mesh):
    in_specs = (
        P(("proj", "cuts"), None, None, "tile"),
        P(),
        P(("proj", "cuts"), "tile", None, None, None),
        P(("proj", "cuts"), "tile", None),
        P(("proj", "cuts"), "tile", None),
        P(("proj", "cuts"), "tile"),
        P(("proj", "cuts"), None, "tile"),
        P("cuts", ("tile", "proj"), None),
        P(None, ("tile", "proj"), None),
        P(),
        P(),
    )
    out_specs = (P(("proj", "cuts"), None, None, "tile"), P(), P("cuts", ("tile", "proj"), None))
    return jax.shard_map(
        on_device, mesh=mesh, in_specs=in_specs, out_specs=out_specs, check_vma=False
    )
```

```python
import functools
import math

import jax
import jax.numpy as jnp
import numpy as np
from jax import lax
from jax.experimental import pallas as pl
from jax.experimental.pallas import tpu as pltpu
from jax.sharding import PartitionSpec as P

VMEM_LIMIT = 60 * 1024 * 1024
VMEM = pltpu.VMEM
F32 = jnp.float32
BF16 = jnp.bfloat16
LANES = 128
SUBLANES = 8
AHEAD = 4
UPDATE_AHEAD = 6
TOMO_LIMIT = 50 * 1024 * 1024
FORWARD_LIMIT = 44 * 1024 * 1024
SMALL_LIMIT = 16 * 1024 * 1024
ANYWHERE = pl.BlockSpec(memory_space=pl.ANY)
WHOLE = pl.BlockSpec(memory_space=pltpu.VMEM)
SCALARS = pl.BlockSpec(memory_space=pltpu.SMEM)
DMA = pltpu.SemaphoreType.DMA

tomo_step = 1.0


def shifted(value, axis, steps):
    count = lax.axis_size(axis)
    leading, last = (max(0, -steps), min(count, count - steps))
    return lax.ppermute(value, axis, [(source, source + steps) for source in range(leading, last)])


def dft_table(side):
    indices = np.arange(side)
    products = (indices[:, None] * indices[None, :]) % side
    phase = products.astype(np.float32) * np.float32(2.0 * math.pi / side)
    norm = np.float32(1.0 / math.sqrt(side))
    real = np.cos(phase).astype(np.float32) * norm
    imag = -np.sin(phase).astype(np.float32) * norm
    return np.stack([real, imag]).astype(jnp.bfloat16)


def dot(left, right):
    return jnp.dot(left, right, preferred_element_type=F32)


def split_bf16(values):
    high = values.astype(BF16).astype(F32)
    low = (values - high).astype(BF16).astype(F32)
    return high, low


def forward_kernel(
    ids_ref,
    rays_hbm,
    volume_hbm,
    weights_hbm,
    out_hbm,
    rays_ref,
    volume_ref,
    weights_ref,
    out_ref,
    table_ref,
    sums_ref,
    rays_sem,
    volume_sem,
    weights_sem,
    out_sem,
):
    depth, projections, _ = sums_ref.shape
    width, lanes = table_ref.shape
    parts, _, _, share = out_ref.shape

    def volume_copy(z):
        return pltpu.make_async_copy(volume_hbm.at[z], volume_ref.at[z], volume_sem.at[z])

    def weights_copy(a):
        return pltpu.make_async_copy(
            weights_hbm.at[ids_ref[a]], weights_ref.at[a], weights_sem.at[a]
        )

    def out_copy(a):
        return pltpu.make_async_copy(out_ref.at[:, a], out_hbm.at[:, a], out_sem.at[a])

    rays_copy = pltpu.make_async_copy(rays_hbm, rays_ref, rays_sem)
    rays_copy.start()
    for z in range(min(AHEAD, depth)):
        volume_copy(z).start()
    for a in range(min(max(AHEAD - depth, 0), projections)):
        weights_copy(a).start()

    rays_copy.wait()
    rows = jnp.concatenate([rays_ref[pl.ds(ids_ref[a], 1), :] for a in range(projections)], axis=0)
    high, low = split_bf16(rows)
    stacked = [high, low]
    if lanes > 2 * projections:
        stacked.append(jnp.zeros((lanes - 2 * projections, width), F32))
    table_ref[...] = jnp.concatenate(stacked, axis=0).T.astype(BF16)

    @pl.loop(0, depth)
    def _(z):
        volume_copy(z).wait()

        @pl.when(z + AHEAD < depth)
        def _():
            volume_copy(z + AHEAD).start()

        @pl.when(jnp.logical_and(z + AHEAD >= depth, z + AHEAD - depth < projections))
        def _():
            weights_copy(z + AHEAD - depth).start()

        piece = min(512, width)
        total = None
        for k in range(0, width, piece):
            block = volume_ref[z, :, k : k + piece]
            high = block.astype(BF16)
            low = (block - high.astype(F32)).astype(BF16)
            stacked = jnp.concatenate([high, low], axis=0)
            part = dot(stacked, table_ref[k : k + piece, :])
            total = part if total is None else total + part
        rows = volume_ref.shape[1]
        total = (total[:rows] + total[rows:]).T
        sums_ref[z] = total[:projections] + total[projections : 2 * projections]

    @pl.loop(0, projections)
    def _(a):
        weights_copy(a).wait()

        @pl.when(a + AHEAD < projections)
        def _():
            weights_copy(a + AHEAD).start()

        rows = sums_ref[:, pl.ds(a, 1), :].reshape(depth, sums_ref.shape[2])
        result = dot(rows.astype(BF16), weights_ref[a])
        for part in range(parts):
            out_ref[part, a] = result[:, part * share : (part + 1) * share]
        out_copy(a).start()

    @pl.loop(0, projections)
    def _(a):
        out_copy(a).wait()


def forward_parts(angle_ids, volume, proj_weights, ray_weights, parts):
    depth, rows, width = volume.shape
    projections = angle_ids.shape[0]
    lanes = -(-2 * projections // LANES) * LANES
    share = width // parts
    return pl.pallas_call(
        forward_kernel,
        in_specs=[SCALARS] + [ANYWHERE] * 3,
        out_specs=ANYWHERE,
        out_shape=jax.ShapeDtypeStruct((parts, projections, depth, share), F32),
        scratch_shapes=[
            VMEM(ray_weights.shape, F32),
            VMEM(volume.shape, F32),
            VMEM((projections, rows, width), BF16),
            VMEM((parts, projections, depth, share), F32),
            VMEM((width, lanes), BF16),
            VMEM((depth, projections, rows), F32),
            DMA,
            pltpu.SemaphoreType.DMA((depth,)),
            pltpu.SemaphoreType.DMA((projections,)),
            pltpu.SemaphoreType.DMA((projections,)),
        ],
        compiler_params=pltpu.CompilerParams(vmem_limit_bytes=FORWARD_LIMIT),
        cost_estimate=pl.CostEstimate(
            flops=4 * depth * rows * width * lanes,
            bytes_accessed=depth * rows * width * 4 + projections * rows * width * 2,
            transcendentals=0,
        ),
        name="forward",
    )(angle_ids, ray_weights, volume, proj_weights)


def placed(values, down, across):
    rows, cols = values.shape
    tall = jnp.concatenate([values, jnp.zeros((SUBLANES, cols), F32)], axis=0)
    tall = pltpu.roll(tall, down, axis=0)
    wide = jnp.concatenate([tall, jnp.zeros((rows + SUBLANES, LANES), F32)], axis=1)
    return pltpu.roll(wide, across, axis=1)


def patch_kernel(
    rows_ref,
    cols_ref,
    count_ref,
    place_ref,
    own_hbm,
    left_hbm,
    right_hbm,
    probe_hbm,
    amp_hbm,
    table_hbm,
    dual_hbm,
    new_hbm,
    edge_left_hbm,
    edge_right_hbm,
    slab_hbm,
    *rest,
):
    shares = len(rest) - 27
    parts_hbm = rest[:shares]
    (
        probe_ref,
        amp_ref,
        table_ref,
        dft_a_ref,
        dft_b_ref,
        dual_ref,
        new_ref,
        edge_left_ref,
        edge_right_ref,
        slab_ref,
        parts_ref,
        ext_ref,
        sum_ref,
        grad_ref,
        energy_ref,
        *chain_refs,
        in_sem,
        amp_sem,
        parts_sem,
        out_sem,
    ) = rest[shares:]
    chain_refs = [chain_refs[k : k + 4] for k in range(0, len(chain_refs), 4)]
    side = probe_ref.shape[1]
    _, height, margin = edge_left_ref.shape
    tile_cols = new_ref.shape[2]
    window = side + LANES
    chunk = 32
    tall = chunk + SUBLANES
    inner = pl.ds(0, height)

    copies = [
        pltpu.make_async_copy(source, target, in_sem.at[k])
        for k, (source, target) in enumerate(
            (
                (left_hbm, ext_ref.at[:, inner, pl.ds(0, margin)]),
                (own_hbm, ext_ref.at[:, inner, pl.ds(margin, tile_cols)]),
                (right_hbm, ext_ref.at[:, inner, pl.ds(margin + tile_cols, margin)]),
                (probe_hbm, probe_ref),
                (table_hbm, table_ref),
                (dual_hbm, dual_ref),
            )
        )
    ]
    for copy in copies:
        copy.start()
    live_count = count_ref[0]

    def amp_copy(k):
        return pltpu.make_async_copy(amp_hbm.at[k], amp_ref.at[k], amp_sem.at[k])

    @pl.loop(0, live_count)
    def _(k):
        amp_copy(k).start()

    sum_ref[...] = jnp.zeros(sum_ref.shape, F32)
    grad_ref[...] = jnp.zeros(grad_ref.shape, F32)
    energy_ref[...] = jnp.zeros(energy_ref.shape, F32)
    for copy in copies:
        copy.wait()
    real = table_ref[0]
    imag = table_ref[1]
    for ref, sign in ((dft_a_ref, -1), (dft_b_ref, 1)):
        ref[:side, :side] = real
        ref[side:, side:] = real
        ref[:side, side:] = sign * imag
        ref[side:, :side] = -sign * imag

    @pl.loop(0, live_count)
    def _(k):
        amp_copy(k).wait()

    def pair_step(pair, carry):
        chains = []
        for k, refs in enumerate(chain_refs):
            slot = jnp.minimum(2 * pair + k, live_count - 1)
            live = (2 * pair + k < live_count).astype(F32)
            row = rows_ref[slot]
            col = cols_ref[slot]
            lane = lax.rem(col, LANES)
            notch = lax.rem(row, SUBLANES)
            base = pl.multiple_of(col - lane, LANES)
            top = pl.multiple_of(row - notch, SUBLANES)
            chains.append((slot, live, lane, notch, base, top, *refs))
        for slot, live, lane, notch, base, top, patch_ref, wave_ref, half_ref, far_ref in chains:
            back_shift = lax.rem(window - lane, window)
            up_shift = lax.rem(tall - notch, tall)
            for r in range(0, side, chunk):
                cells = pl.ds(top + r, tall)
                here = slice(r, r + chunk)
                below = slice(side + r, side + r + chunk)
                x_re = pltpu.roll(ext_ref[0, cells, pl.ds(base, window)], back_shift, axis=1)
                x_im = pltpu.roll(ext_ref[1, cells, pl.ds(base, window)], back_shift, axis=1)
                x_re = pltpu.roll(x_re[:, :side], up_shift, axis=0)[:chunk]
                x_im = pltpu.roll(x_im[:, :side], up_shift, axis=0)[:chunk]
                p_re = probe_ref[0, here, :]
                p_im = probe_ref[1, here, :]
                patch_ref[here, :] = x_re
                patch_ref[below, :] = x_im
                wave_ref[here, :] = (p_re * x_re - p_im * x_im).astype(BF16)
                wave_ref[below, :] = (p_re * x_im + p_im * x_re).astype(BF16)
                power = x_re * x_re + x_im * x_im
                energy_ref[...] += live * jnp.sum(
                    power.reshape(chunk // SUBLANES, SUBLANES, side), axis=0
                )
        for *_, wave_ref, half_ref, far_ref in chains:
            half_ref[:, :side] = dot(dft_a_ref[:side, :], wave_ref[...]).astype(BF16)
            half_ref[:, side:] = dot(dft_a_ref[side:, :], wave_ref[...]).astype(BF16)
        for *_, half_ref, far_ref in chains:
            far_ref[...] = dot(half_ref[...], dft_b_ref[...])
        for slot, live, *_, wave_ref, half_ref, far_ref in chains:
            for r in range(0, side, chunk):
                here = slice(r, r + chunk)
                below = slice(side + r, side + r + chunk)
                f_re = far_ref[here, :side]
                f_im = far_ref[here, side:]
                inverse = lax.rsqrt(f_re * f_re + f_im * f_im + 0.25)
                factor = amp_ref[slot, here, :].astype(F32) * inverse - 1.0
                wave_ref[here, :] = (f_re * factor).astype(BF16)
                wave_ref[below, :] = (f_im * factor).astype(BF16)
        for *_, wave_ref, half_ref, far_ref in chains:
            half_ref[:, :side] = dot(dft_b_ref[:side, :], wave_ref[...]).astype(BF16)
            half_ref[:, side:] = dot(dft_b_ref[side:, :], wave_ref[...]).astype(BF16)
        for *_, half_ref, far_ref in chains:
            far_ref[...] = dot(half_ref[...], dft_a_ref[...])
        for slot, live, lane, notch, base, top, patch_ref, wave_ref, half_ref, far_ref in chains:
            for r in range(0, side, chunk):
                cells = pl.ds(top + r, tall)
                here = slice(r, r + chunk)
                below = slice(side + r, side + r + chunk)
                b_re = live * far_ref[here, :side]
                b_im = live * far_ref[here, side:]
                p_re = probe_ref[0, here, :]
                p_im = probe_ref[1, here, :]
                x_re = patch_ref[here, :]
                x_im = patch_ref[below, :]
                o_re = p_re * b_re + p_im * b_im
                o_im = p_re * b_im - p_im * b_re
                sum_ref[0, cells, pl.ds(base, window)] += placed(o_re, notch, lane)
                sum_ref[1, cells, pl.ds(base, window)] += placed(o_im, notch, lane)
                grad_ref[here, :] += x_re * b_re + x_im * b_im
                grad_ref[below, :] += x_re * b_im - x_im * b_re
        return carry

    lax.fori_loop(0, lax.div(live_count + 1, 2), pair_step, 0)

    p_re = probe_ref[0]
    p_im = probe_ref[1]
    peak = jnp.max(p_re * p_re + p_im * p_im)
    scale = 1.0 / (jnp.full((1, LANES), peak, F32) + 1e-05)
    wide = jnp.tile(scale, (1, tile_cols // LANES))
    shares, layers, depth, share = slab_ref.shape
    edge = min(share - tile_cols // shares, margin)
    share -= edge
    holders = margin // edge
    first = (height - layers * depth) // 2
    band = pl.ds(first, layers * depth)
    mid = slice(margin, margin + tile_cols)
    far_side = slice(margin + tile_cols, 2 * margin + tile_cols)
    own_band = ext_ref[1, band, mid] + sum_ref[1, band, mid] * wide + dual_ref[...]
    left_band = sum_ref[1, band, :margin] * scale
    right_band = sum_ref[1, band, far_side] * scale
    for layer in range(layers):
        rows = slice(layer * depth, (layer + 1) * depth)
        for p in range(shares):
            slab_ref[p, layer, :, :share] = own_band[rows, p * share : (p + 1) * share]
            begin = (p - shares + holders) * edge
            if p < holders:
                outgoing = left_band[rows, p * edge : (p + 1) * edge]
            elif p >= shares - holders:
                outgoing = right_band[rows, begin : begin + edge]
            else:
                outgoing = jnp.zeros((depth, edge), F32)
            slab_ref[p, layer, :, share:] = outgoing
    slab_copy = pltpu.make_async_copy(slab_ref, slab_hbm, out_sem.at[3])
    slab_copy.start()
    part_rows = parts_ref.shape[1] - SUBLANES
    last_copies = [slab_copy]
    for step in range(shares):
        begin = pl.multiple_of(lax.rem(place_ref[0] + step, shares) * part_rows, SUBLANES)
        parts_ref[step, :part_rows, :] = grad_ref[pl.ds(begin, part_rows), :]
        parts_ref[step, part_rows:, :] = energy_ref[...]
        copy = pltpu.make_async_copy(parts_ref.at[step], parts_hbm[step], parts_sem.at[step])
        copy.start()
        last_copies.append(copy)
    for c in range(2):
        new_ref[c] = ext_ref[c, inner, mid] + sum_ref[c, inner, mid] * wide
        edge_left_ref[c] = (sum_ref[c, inner, :margin] * scale).astype(BF16)
        edge_right_ref[c] = (sum_ref[c, inner, far_side] * scale).astype(BF16)
    for k, (source, target) in enumerate(
        ((new_ref, new_hbm), (edge_left_ref, edge_left_hbm), (edge_right_ref, edge_right_hbm))
    ):
        copy = pltpu.make_async_copy(source, target, out_sem.at[k])
        copy.start()
        last_copies.append(copy)
    for copy in last_copies:
        copy.wait()


def patch_updates(
    rows, cols, count, place, own, left, right, probe, amplitudes, dual, shares, layers
):
    side = probe.shape[1]
    _, height, tile_cols = own.shape
    margin = left.shape[2]
    slots = amplitudes.shape[0]
    slab_rows = dual.shape[0]
    share = tile_cols // shares
    edge = min(share, margin)
    table = dft_table(side)
    extent = tile_cols + 2 * margin + LANES
    shape = jax.ShapeDtypeStruct
    slab_shape = (shares, layers, slab_rows // layers, share + edge)
    part_rows = 2 * side // shares + SUBLANES
    chain = [
        VMEM((2 * side, side), F32),
        VMEM((2 * side, side), BF16),
        VMEM((side, 2 * side), BF16),
        VMEM((side, 2 * side), F32),
    ]
    return pl.pallas_call(
        patch_kernel,
        in_specs=[SCALARS] * 4 + [ANYWHERE] * 7,
        out_specs=[ANYWHERE] * (4 + shares),
        out_shape=[
            shape((2, height, tile_cols), F32),
            shape((2, height, margin), BF16),
            shape((2, height, margin), BF16),
            shape(slab_shape, F32),
        ]
        + [shape((part_rows, side), F32)] * shares,
        scratch_shapes=[
            VMEM(probe.shape, F32),
            VMEM(amplitudes.shape, BF16),
            VMEM(table.shape, BF16),
            VMEM((2 * side, 2 * side), BF16),
            VMEM((2 * side, 2 * side), BF16),
            VMEM(dual.shape, F32),
            VMEM((2, height, tile_cols), F32),
            VMEM((2, height, margin), BF16),
            VMEM((2, height, margin), BF16),
            VMEM(slab_shape, F32),
            VMEM((shares, part_rows, side), F32),
            VMEM((2, height + SUBLANES, extent), F32),
            VMEM((2, height + SUBLANES, extent), F32),
            VMEM((2 * side, side), F32),
            VMEM((SUBLANES, side), F32),
            *chain,
            *chain,
            pltpu.SemaphoreType.DMA((6,)),
            pltpu.SemaphoreType.DMA((slots,)),
            pltpu.SemaphoreType.DMA((shares,)),
            pltpu.SemaphoreType.DMA((4,)),
        ],
        compiler_params=pltpu.CompilerParams(vmem_limit_bytes=VMEM_LIMIT),
        cost_estimate=pl.CostEstimate(
            flops=slots * 32 * side**3,
            bytes_accessed=8 * height * tile_cols * 4,
            transcendentals=slots * side * side,
        ),
        name="patches",
    )(
        rows,
        cols,
        count,
        place,
        own,
        left,
        right,
        probe,
        amplitudes,
        jnp.asarray(table),
        dual,
    )


def backward_kernel(
    ids_ref, residual_hbm, weights_hbm, out_ref, residual_ref, weights_ref, turned_ref, sem, weights_sem
):
    parts, projections, depth, share = residual_ref.shape
    both = projections * depth

    def weights_copy(a):
        return pltpu.make_async_copy(
            weights_hbm.at[ids_ref[a]], weights_ref.at[a], weights_sem.at[a]
        )

    residual_copy = pltpu.make_async_copy(residual_hbm, residual_ref, sem)
    residual_copy.start()
    for a in range(min(AHEAD, projections)):
        weights_copy(a).start()
    residual_copy.wait()
    for part in range(parts):
        block = residual_ref[part].astype(F32).reshape(both, share)
        turned_ref[part * share : (part + 1) * share, :] = block.T
    out_ref[...] = jnp.zeros(out_ref.shape, F32)

    members = math.gcd(projections, 2)

    @pl.loop(0, projections, step=members)
    def _(first):
        for a in range(members):
            weights_copy(first + a).wait()
        for a in range(members):
            item = first + a + AHEAD

            @pl.when(item < projections)
            def _():
                weights_copy(item).start()

        lane = lax.broadcasted_iota(jnp.int32, turned_ref.shape, 1)
        total = out_ref[...]
        for a in range(members):
            begin = (first + a) * depth
            kept = jnp.logical_and(lane >= begin, lane < begin + depth)
            chosen = jnp.where(kept, turned_ref[...], 0.0).astype(BF16)
            total += dot(weights_ref[first + a], chosen)
        out_ref[...] = total


def backward_sums(angle_ids, residual, proj_weights):
    _, rows, width = proj_weights.shape
    _, projections, depth, _ = residual.shape
    return pl.pallas_call(
        backward_kernel,
        in_specs=[SCALARS, ANYWHERE, ANYWHERE],
        out_specs=WHOLE,
        out_shape=jax.ShapeDtypeStruct((rows, projections * depth), F32),
        scratch_shapes=[
            VMEM(residual.shape, BF16),
            VMEM((projections, rows, width), BF16),
            VMEM((width, projections * depth), F32),
            DMA,
            pltpu.SemaphoreType.DMA((projections,)),
        ],
        compiler_params=pltpu.CompilerParams(vmem_limit_bytes=TOMO_LIMIT),
        cost_estimate=pl.CostEstimate(
            flops=2 * rows * width * projections * projections * depth,
            bytes_accessed=projections * rows * width * 2,
            transcendentals=0,
        ),
        name="backward",
    )(angle_ids, residual, proj_weights)


def update_kernel(
    ids_ref,
    sums_ref,
    rays_hbm,
    volume_hbm,
    out_hbm,
    rays_ref,
    stack_ref,
    spread_ref,
    volume_ref,
    done_ref,
    rays_sem,
    volume_sem,
    out_sem,
):
    depth = volume_ref.shape[0]
    slots = done_ref.shape[0]
    width = rays_ref.shape[1]
    projections = sums_ref.shape[1] // depth
    both = sums_ref.shape[1]

    def volume_copy(z):
        return pltpu.make_async_copy(volume_hbm.at[z], volume_ref.at[z], volume_sem.at[z])

    def out_copy(z):
        slot = lax.rem(z, slots)
        return pltpu.make_async_copy(done_ref.at[slot], out_hbm.at[z], out_sem.at[slot])

    rays_copy = pltpu.make_async_copy(rays_hbm, rays_ref, rays_sem)
    rays_copy.start()
    for z in range(min(UPDATE_AHEAD, depth)):
        volume_copy(z).start()
    high, low = split_bf16(sums_ref[...])
    stack_ref[...] = jnp.concatenate([high, low, high, low], axis=1)
    rays_copy.wait()
    rows = [
        jnp.broadcast_to(rays_ref[pl.ds(ids_ref[a], 1), :], (depth, width))
        for a in range(projections)
    ]
    high, low = split_bf16(jnp.concatenate(rows, axis=0))
    for place, block in enumerate((high, high, low, low)):
        spread_ref[place * both : (place + 1) * both, :] = block.astype(BF16)

    @pl.loop(0, depth)
    def _(z):
        volume_copy(z).wait()

        @pl.when(z + UPDATE_AHEAD < depth)
        def _():
            volume_copy(z + UPDATE_AHEAD).start()

        @pl.when(z >= slots)
        def _():
            out_copy(z - slots).wait()

        lane = lax.broadcasted_iota(jnp.int32, stack_ref.shape, 1)
        kept = lax.rem(lane, depth) == z
        chosen = jnp.where(kept, stack_ref[...], 0.0).astype(BF16)
        done_ref[lax.rem(z, slots)] = volume_ref[z] - tomo_step * dot(chosen, spread_ref[...])
        out_copy(z).start()

    for z in range(max(depth - slots, 0), depth):
        out_copy(z).wait()


def volume_update(angle_ids, sums, rays, volume):
    depth, rows, width = volume.shape
    slots = min(4, depth)
    return pl.pallas_call(
        update_kernel,
        in_specs=[SCALARS, WHOLE] + [ANYWHERE] * 2,
        out_specs=ANYWHERE,
        out_shape=jax.ShapeDtypeStruct(volume.shape, F32),
        scratch_shapes=[
            VMEM(rays.shape, F32),
            VMEM((rows, 4 * sums.shape[1]), F32),
            VMEM((4 * sums.shape[1], width), BF16),
            VMEM(volume.shape, F32),
            VMEM((slots, rows, width), F32),
            DMA,
            pltpu.SemaphoreType.DMA((depth,)),
            pltpu.SemaphoreType.DMA((slots,)),
        ],
        compiler_params=pltpu.CompilerParams(vmem_limit_bytes=TOMO_LIMIT),
        cost_estimate=pl.CostEstimate(
            flops=8 * rows * width * sums.shape[1] * depth,
            bytes_accessed=2 * depth * rows * width * 4,
            transcendentals=0,
        ),
        name="update",
    )(angle_ids, sums, rays, volume)


def gather_parts_kernel(group, *refs):
    *given, out_hbm, out_ref, sem = refs
    total = given[0][...]
    for ref in given[1:]:
        total = total + ref[...]
    blocks = total.shape[1] // LANES
    rows = (out_ref.shape[1] - SUBLANES) // blocks
    columns = [total[:, k * LANES : (k + 1) * LANES] for k in range(blocks)]
    energy = columns[0][group * rows :]
    for block in columns[1:]:
        energy = energy + block[group * rows :]
    for k in range(group):
        for place, block in enumerate(columns):
            out_ref[k, place * rows : (place + 1) * rows, :] = block[k * rows : (k + 1) * rows]
        out_ref[k, blocks * rows :, :] = energy
    copy = pltpu.make_async_copy(out_ref, out_hbm, sem)
    copy.start()
    copy.wait()


def gather_parts(given, group):
    total_rows, side = given[0].shape
    rows = (total_rows - SUBLANES) // group * (side // LANES) + SUBLANES
    shape = (group, rows, LANES)
    return pl.pallas_call(
        functools.partial(gather_parts_kernel, group),
        in_specs=[WHOLE] * len(given),
        out_specs=ANYWHERE,
        out_shape=jax.ShapeDtypeStruct(shape, F32),
        scratch_shapes=[VMEM(shape, F32), DMA],
        compiler_params=pltpu.CompilerParams(vmem_limit_bytes=SMALL_LIMIT),
        name="probe_parts",
    )(*given)


def probe_rows_kernel(given_ref, out_hbm, out_ref, sem):
    group, rows, _ = given_ref.shape
    receivers, taken, side = out_ref.shape
    total = given_ref[0]
    for k in range(1, group):
        total = total + given_ref[k]
    energy = jnp.sum(total[rows - SUBLANES :], keepdims=True) / (side * side)
    steps = total[: rows - SUBLANES] / (energy + 1e-05)
    steps = jnp.concatenate(
        [steps[k * taken : (k + 1) * taken] for k in range(side // LANES)], axis=1
    )
    for k in range(receivers):
        out_ref[k] = steps
    copy = pltpu.make_async_copy(out_ref, out_hbm, sem)
    copy.start()
    copy.wait()


def probe_rows(given, side, receivers):
    _, rows, _ = given.shape
    shape = (receivers, (rows - SUBLANES) * LANES // side, side)
    return pl.pallas_call(
        probe_rows_kernel,
        in_specs=[WHOLE],
        out_specs=ANYWHERE,
        out_shape=jax.ShapeDtypeStruct(shape, F32),
        scratch_shapes=[VMEM(shape, F32), DMA],
        compiler_params=pltpu.CompilerParams(vmem_limit_bytes=SMALL_LIMIT),
        name="probe_rows",
    )(given)


def turned(value, axis, steps):
    count = lax.axis_size(axis)
    return lax.ppermute(value, axis, [(k, (k + steps) % count) for k in range(count)])


def on_device(
    object_field,
    probe_field,
    amplitudes,
    pos_rows,
    pos_cols,
    counts,
    admm_dual,
    volume,
    proj_weights,
    ray_weights,
    angle_ids,
):
    margin = probe_field.shape[1] // 2
    own = object_field[0]
    tile_cols = own.shape[2]
    flat_axes = ("tile", "proj")
    plane = lax.axis_size("tile") * lax.axis_size("proj")
    proj_count = lax.axis_size("proj")
    layers = lax.axis_size("cuts")
    from_left = shifted(own[:, :, tile_cols - margin :], "tile", 1)
    from_right = shifted(own[:, :, :margin], "tile", -1)
    forward = forward_parts(angle_ids, volume, proj_weights, ray_weights, plane)
    _, from_left, from_right = lax.optimization_barrier((forward, from_left, from_right))
    arrived = lax.all_to_all(forward, flat_axes, 0, 0, tiled=True)
    place = lax.axis_index("proj")
    partial_object, edge_left, edge_right, slab, *grad_parts = patch_updates(
        pos_rows[0, 0],
        pos_cols[0, 0],
        counts[0],
        place[None],
        own,
        from_left,
        from_right,
        probe_field,
        amplitudes[0, 0],
        admm_dual[0],
        proj_count,
        layers,
    )

    share = tile_cols // proj_count
    edge = slab.shape[3] - share
    holders = margin // edge
    slab, arrived = lax.optimization_barrier((slab, arrived))
    pieces = slab.reshape(proj_count * layers, *slab.shape[2:])
    pieces = lax.all_to_all(pieces, ("proj", "cuts"), 0, 0, tiled=True)
    pieces, grad_parts = lax.optimization_barrier((pieces, grad_parts))
    pairs = []
    for tile in range(lax.axis_size("tile") - 1):
        for k in range(holders):
            lower = tile * proj_count + proj_count - holders + k
            upper = (tile + 1) * proj_count + k
            pairs += [(lower, upper), (upper, lower)]
    grads_in = lax.ppermute(pieces[:, :, share:], flat_axes, pairs)
    at_start = jnp.pad(grads_in, ((0, 0), (0, 0), (0, share - edge)))
    at_end = jnp.pad(grads_in, ((0, 0), (0, 0), (share - edge, 0)))
    target = pieces[:, :, :share] + jnp.where(place < holders, at_start, at_end)
    residual = (jnp.sum(arrived, axis=0) - target).astype(BF16)
    copies = jnp.broadcast_to(residual[None], (plane, *residual.shape))

    group_axes = ("tile", "cuts")
    group = lax.axis_size("tile") * layers
    given = [grad_parts[0]]
    for step in range(1, proj_count):
        given.append(turned(grad_parts[step], "proj", step))
    copies, given = lax.optimization_barrier((copies, given))
    residual = lax.all_to_all(copies, flat_axes, 0, 0, tiled=True)
    by_receiver = gather_parts(given, group)
    residual, by_receiver, edge_left, edge_right = lax.optimization_barrier(
        (residual, by_receiver, edge_left, edge_right)
    )
    received = lax.all_to_all(by_receiver, group_axes, 0, 0, tiled=True)
    edge_from_left = shifted(edge_right, "tile", 1)
    back_sums = backward_sums(angle_ids, residual, proj_weights)
    back_sums, received, edge_left = lax.optimization_barrier((back_sums, received, edge_left))
    edge_from_right = shifted(edge_left, "tile", -1)
    steps = probe_rows(received, probe_field.shape[1], plane * layers)
    back_sums, steps, edge_from_left = lax.optimization_barrier(
        (back_sums, steps, edge_from_left)
    )
    steps = lax.all_to_all(steps, ("proj", "tile", "cuts"), 0, 0, tiled=True)
    new_volume = volume_update(angle_ids, back_sums, ray_weights, volume)
    new_volume, steps = lax.optimization_barrier((new_volume, steps))
    new_probe = probe_field + steps.reshape(probe_field.shape)
    rest = tile_cols - margin
    new_object = (
        partial_object
        + jnp.pad(edge_from_left.astype(F32), ((0, 0), (0, 0), (0, rest)))
        + jnp.pad(edge_from_right.astype(F32), ((0, 0), (0, 0), (rest, 0)))
    )
    return (new_object[None], new_probe, new_volume)


def solution(mesh):
    in_specs = (
        P(("proj", "cuts"), None, None, "tile"),
        P(),
        P(("proj", "cuts"), "tile", None, None, None),
        P(("proj", "cuts"), "tile", None),
        P(("proj", "cuts"), "tile", None),
        P(("proj", "cuts"), "tile"),
        P(("proj", "cuts"), None, "tile"),
        P("cuts", ("tile", "proj"), None),
        P(None, ("tile", "proj"), None),
        P(),
        P(),
    )
    out_specs = (P(("proj", "cuts"), None, None, "tile"), P(), P("cuts", ("tile", "proj"), None))
    return jax.shard_map(
        on_device, mesh=mesh, in_specs=in_specs, out_specs=out_specs, check_vma=False
    )
```

```python
import functools
import math

import jax
import jax.numpy as jnp
import numpy as np
from jax import lax
from jax.experimental import pallas as pl
from jax.experimental.pallas import tpu as pltpu
from jax.sharding import PartitionSpec as P

VMEM_LIMIT = 60 * 1024 * 1024
VMEM = pltpu.VMEM
F32 = jnp.float32
BF16 = jnp.bfloat16
LANES = 128
SUBLANES = 8
AHEAD = 4
UPDATE_AHEAD = 6
TOMO_LIMIT = 50 * 1024 * 1024
FORWARD_LIMIT = 44 * 1024 * 1024
SMALL_LIMIT = 16 * 1024 * 1024
ANYWHERE = pl.BlockSpec(memory_space=pl.ANY)
WHOLE = pl.BlockSpec(memory_space=pltpu.VMEM)
SCALARS = pl.BlockSpec(memory_space=pltpu.SMEM)
DMA = pltpu.SemaphoreType.DMA

tomo_step = 1.0


def shifted(value, axis, steps):
    count = lax.axis_size(axis)
    leading, last = (max(0, -steps), min(count, count - steps))
    return lax.ppermute(value, axis, [(source, source + steps) for source in range(leading, last)])


def dft_table(side):
    indices = np.arange(side)
    products = (indices[:, None] * indices[None, :]) % side
    phase = products.astype(np.float32) * np.float32(2.0 * math.pi / side)
    norm = np.float32(1.0 / math.sqrt(side))
    real = np.cos(phase).astype(np.float32) * norm
    imag = -np.sin(phase).astype(np.float32) * norm
    return np.stack([real, imag]).astype(jnp.bfloat16)


def dot(left, right):
    return jnp.dot(left, right, preferred_element_type=F32)


def split_bf16(values):
    high = values.astype(BF16).astype(F32)
    low = (values - high).astype(BF16).astype(F32)
    return high, low


def forward_kernel(
    ids_ref,
    rays_hbm,
    volume_hbm,
    weights_hbm,
    out_hbm,
    rays_ref,
    volume_ref,
    weights_ref,
    out_ref,
    table_ref,
    sums_ref,
    rays_sem,
    volume_sem,
    weights_sem,
    out_sem,
):
    depth, projections, _ = sums_ref.shape
    width, lanes = table_ref.shape
    parts, _, _, share = out_ref.shape

    def volume_copy(z):
        return pltpu.make_async_copy(volume_hbm.at[z], volume_ref.at[z], volume_sem.at[z])

    def weights_copy(a):
        return pltpu.make_async_copy(
            weights_hbm.at[ids_ref[a]], weights_ref.at[a], weights_sem.at[a]
        )

    def out_copy(a):
        return pltpu.make_async_copy(out_ref.at[:, a], out_hbm.at[:, a], out_sem.at[a])

    rays_copy = pltpu.make_async_copy(rays_hbm, rays_ref, rays_sem)
    rays_copy.start()
    for z in range(min(AHEAD, depth)):
        volume_copy(z).start()
    for a in range(min(max(AHEAD - depth, 0), projections)):
        weights_copy(a).start()

    rays_copy.wait()
    rows = jnp.concatenate([rays_ref[pl.ds(ids_ref[a], 1), :] for a in range(projections)], axis=0)
    high, low = split_bf16(rows)
    stacked = [high, low]
    if lanes > 2 * projections:
        stacked.append(jnp.zeros((lanes - 2 * projections, width), F32))
    table_ref[...] = jnp.concatenate(stacked, axis=0).T.astype(BF16)

    @pl.loop(0, depth)
    def _(z):
        volume_copy(z).wait()

        @pl.when(z + AHEAD < depth)
        def _():
            volume_copy(z + AHEAD).start()

        @pl.when(jnp.logical_and(z + AHEAD >= depth, z + AHEAD - depth < projections))
        def _():
            weights_copy(z + AHEAD - depth).start()

        piece = min(512, width)
        total = None
        for k in range(0, width, piece):
            block = volume_ref[z, :, k : k + piece]
            high = block.astype(BF16)
            low = (block - high.astype(F32)).astype(BF16)
            stacked = jnp.concatenate([high, low], axis=0)
            part = dot(stacked, table_ref[k : k + piece, :])
            total = part if total is None else total + part
        rows = volume_ref.shape[1]
        total = (total[:rows] + total[rows:]).T
        sums_ref[z] = total[:projections] + total[projections : 2 * projections]

    @pl.loop(0, projections)
    def _(a):
        weights_copy(a).wait()

        @pl.when(a + AHEAD < projections)
        def _():
            weights_copy(a + AHEAD).start()

        rows = sums_ref[:, pl.ds(a, 1), :].reshape(depth, sums_ref.shape[2])
        result = dot(rows.astype(BF16), weights_ref[a])
        for part in range(parts):
            out_ref[part, a] = result[:, part * share : (part + 1) * share]
        out_copy(a).start()

    @pl.loop(0, projections)
    def _(a):
        out_copy(a).wait()


def forward_parts(angle_ids, volume, proj_weights, ray_weights, parts):
    depth, rows, width = volume.shape
    projections = angle_ids.shape[0]
    lanes = -(-2 * projections // LANES) * LANES
    share = width // parts
    return pl.pallas_call(
        forward_kernel,
        in_specs=[SCALARS] + [ANYWHERE] * 3,
        out_specs=ANYWHERE,
        out_shape=jax.ShapeDtypeStruct((parts, projections, depth, share), F32),
        scratch_shapes=[
            VMEM(ray_weights.shape, F32),
            VMEM(volume.shape, F32),
            VMEM((projections, rows, width), BF16),
            VMEM((parts, projections, depth, share), F32),
            VMEM((width, lanes), BF16),
            VMEM((depth, projections, rows), F32),
            DMA,
            pltpu.SemaphoreType.DMA((depth,)),
            pltpu.SemaphoreType.DMA((projections,)),
            pltpu.SemaphoreType.DMA((projections,)),
        ],
        compiler_params=pltpu.CompilerParams(vmem_limit_bytes=FORWARD_LIMIT),
        cost_estimate=pl.CostEstimate(
            flops=4 * depth * rows * width * lanes,
            bytes_accessed=depth * rows * width * 4 + projections * rows * width * 2,
            transcendentals=0,
        ),
        name="forward",
    )(angle_ids, ray_weights, volume, proj_weights)


def placed(values, down, across):
    rows, cols = values.shape
    tall = jnp.concatenate([values, jnp.zeros((SUBLANES, cols), F32)], axis=0)
    tall = pltpu.roll(tall, down, axis=0)
    wide = jnp.concatenate([tall, jnp.zeros((rows + SUBLANES, LANES), F32)], axis=1)
    return pltpu.roll(wide, across, axis=1)


def patch_kernel(
    rows_ref,
    cols_ref,
    count_ref,
    place_ref,
    own_hbm,
    left_hbm,
    right_hbm,
    probe_hbm,
    amp_hbm,
    table_hbm,
    dual_hbm,
    new_hbm,
    edge_left_hbm,
    edge_right_hbm,
    slab_hbm,
    *rest,
):
    shares = len(rest) - 27
    parts_hbm = rest[:shares]
    (
        probe_ref,
        amp_ref,
        table_ref,
        dft_a_ref,
        dft_b_ref,
        dual_ref,
        new_ref,
        edge_left_ref,
        edge_right_ref,
        slab_ref,
        parts_ref,
        ext_ref,
        sum_ref,
        grad_ref,
        energy_ref,
        *chain_refs,
        in_sem,
        amp_sem,
        parts_sem,
        out_sem,
    ) = rest[shares:]
    chain_refs = [chain_refs[k : k + 4] for k in range(0, len(chain_refs), 4)]
    side = probe_ref.shape[1]
    _, height, margin = edge_left_ref.shape
    tile_cols = new_ref.shape[2]
    window = side + LANES
    chunk = 32
    tall = chunk + SUBLANES
    inner = pl.ds(0, height)

    copies = [
        pltpu.make_async_copy(source, target, in_sem.at[k])
        for k, (source, target) in enumerate(
            (
                (left_hbm, ext_ref.at[:, inner, pl.ds(0, margin)]),
                (own_hbm, ext_ref.at[:, inner, pl.ds(margin, tile_cols)]),
                (right_hbm, ext_ref.at[:, inner, pl.ds(margin + tile_cols, margin)]),
                (probe_hbm, probe_ref),
                (table_hbm, table_ref),
                (dual_hbm, dual_ref),
            )
        )
    ]
    for copy in copies:
        copy.start()
    live_count = count_ref[0]

    def amp_copy(k):
        return pltpu.make_async_copy(amp_hbm.at[k], amp_ref.at[k], amp_sem.at[k])

    @pl.loop(0, live_count)
    def _(k):
        amp_copy(k).start()

    sum_ref[...] = jnp.zeros(sum_ref.shape, F32)
    grad_ref[...] = jnp.zeros(grad_ref.shape, F32)
    energy_ref[...] = jnp.zeros(energy_ref.shape, F32)
    for copy in copies:
        copy.wait()
    real = table_ref[0]
    imag = table_ref[1]
    for ref, sign in ((dft_a_ref, -1), (dft_b_ref, 1)):
        ref[:side, :side] = real
        ref[side:, side:] = real
        ref[:side, side:] = sign * imag
        ref[side:, :side] = -sign * imag

    @pl.loop(0, live_count)
    def _(k):
        amp_copy(k).wait()

    def pair_step(pair, carry):
        chains = []
        for k, refs in enumerate(chain_refs):
            slot = jnp.minimum(2 * pair + k, live_count - 1)
            live = (2 * pair + k < live_count).astype(F32)
            row = rows_ref[slot]
            col = cols_ref[slot]
            lane = lax.rem(col, LANES)
            notch = lax.rem(row, SUBLANES)
            base = pl.multiple_of(col - lane, LANES)
            top = pl.multiple_of(row - notch, SUBLANES)
            chains.append((slot, live, lane, notch, base, top, *refs))
        for slot, live, lane, notch, base, top, patch_ref, wave_ref, half_ref, far_ref in chains:
            back_shift = lax.rem(window - lane, window)
            up_shift = lax.rem(tall - notch, tall)
            for r in range(0, side, chunk):
                cells = pl.ds(top + r, tall)
                here = slice(r, r + chunk)
                below = slice(side + r, side + r + chunk)
                x_re = pltpu.roll(ext_ref[0, cells, pl.ds(base, window)], back_shift, axis=1)
                x_im = pltpu.roll(ext_ref[1, cells, pl.ds(base, window)], back_shift, axis=1)
                x_re = pltpu.roll(x_re[:, :side], up_shift, axis=0)[:chunk]
                x_im = pltpu.roll(x_im[:, :side], up_shift, axis=0)[:chunk]
                p_re = probe_ref[0, here, :]
                p_im = probe_ref[1, here, :]
                patch_ref[here, :] = x_re
                patch_ref[below, :] = x_im
                wave_ref[here, :] = (p_re * x_re - p_im * x_im).astype(BF16)
                wave_ref[below, :] = (p_re * x_im + p_im * x_re).astype(BF16)
                power = x_re * x_re + x_im * x_im
                energy_ref[...] += live * jnp.sum(
                    power.reshape(chunk // SUBLANES, SUBLANES, side), axis=0
                )
        for *_, wave_ref, half_ref, far_ref in chains:
            half_ref[:, :side] = dot(dft_a_ref[:side, :], wave_ref[...]).astype(BF16)
            half_ref[:, side:] = dot(dft_a_ref[side:, :], wave_ref[...]).astype(BF16)
        for *_, half_ref, far_ref in chains:
            far_ref[...] = dot(half_ref[...], dft_b_ref[...])
        for slot, live, *_, wave_ref, half_ref, far_ref in chains:
            for r in range(0, side, chunk):
                here = slice(r, r + chunk)
                below = slice(side + r, side + r + chunk)
                f_re = far_ref[here, :side]
                f_im = far_ref[here, side:]
                inverse = lax.rsqrt(f_re * f_re + f_im * f_im + 0.25)
                factor = amp_ref[slot, here, :].astype(F32) * inverse - 1.0
                wave_ref[here, :] = (f_re * factor).astype(BF16)
                wave_ref[below, :] = (f_im * factor).astype(BF16)
        for *_, wave_ref, half_ref, far_ref in chains:
            half_ref[:, :side] = dot(dft_b_ref[:side, :], wave_ref[...]).astype(BF16)
            half_ref[:, side:] = dot(dft_b_ref[side:, :], wave_ref[...]).astype(BF16)
        for *_, half_ref, far_ref in chains:
            far_ref[...] = dot(half_ref[...], dft_a_ref[...])
        for slot, live, lane, notch, base, top, patch_ref, wave_ref, half_ref, far_ref in chains:
            for r in range(0, side, chunk):
                cells = pl.ds(top + r, tall)
                here = slice(r, r + chunk)
                below = slice(side + r, side + r + chunk)
                b_re = live * far_ref[here, :side]
                b_im = live * far_ref[here, side:]
                p_re = probe_ref[0, here, :]
                p_im = probe_ref[1, here, :]
                x_re = patch_ref[here, :]
                x_im = patch_ref[below, :]
                o_re = p_re * b_re + p_im * b_im
                o_im = p_re * b_im - p_im * b_re
                sum_ref[0, cells, pl.ds(base, window)] += placed(o_re, notch, lane)
                sum_ref[1, cells, pl.ds(base, window)] += placed(o_im, notch, lane)
                grad_ref[here, :] += x_re * b_re + x_im * b_im
                grad_ref[below, :] += x_re * b_im - x_im * b_re
        return carry

    lax.fori_loop(0, lax.div(live_count + 1, 2), pair_step, 0)

    p_re = probe_ref[0]
    p_im = probe_ref[1]
    peak = jnp.max(p_re * p_re + p_im * p_im)
    scale = 1.0 / (jnp.full((1, LANES), peak, F32) + 1e-05)
    wide = jnp.tile(scale, (1, tile_cols // LANES))
    shares, layers, depth, share = slab_ref.shape
    edge = min(share - tile_cols // shares, margin)
    share -= edge
    holders = margin // edge
    first = (height - layers * depth) // 2
    band = pl.ds(first, layers * depth)
    mid = slice(margin, margin + tile_cols)
    far_side = slice(margin + tile_cols, 2 * margin + tile_cols)
    own_band = ext_ref[1, band, mid] + sum_ref[1, band, mid] * wide + dual_ref[...]
    left_band = sum_ref[1, band, :margin] * scale
    right_band = sum_ref[1, band, far_side] * scale
    for layer in range(layers):
        rows = slice(layer * depth, (layer + 1) * depth)
        for p in range(shares):
            slab_ref[p, layer, :, :share] = own_band[rows, p * share : (p + 1) * share]
            begin = (p - shares + holders) * edge
            if p < holders:
                outgoing = left_band[rows, p * edge : (p + 1) * edge]
            elif p >= shares - holders:
                outgoing = right_band[rows, begin : begin + edge]
            else:
                outgoing = jnp.zeros((depth, edge), F32)
            slab_ref[p, layer, :, share:] = outgoing
    slab_copy = pltpu.make_async_copy(slab_ref, slab_hbm, out_sem.at[3])
    slab_copy.start()
    part_rows = parts_ref.shape[1] - SUBLANES
    last_copies = [slab_copy]
    for step in range(shares):
        begin = pl.multiple_of(lax.rem(place_ref[0] + step, shares) * part_rows, SUBLANES)
        parts_ref[step, :part_rows, :] = grad_ref[pl.ds(begin, part_rows), :]
        parts_ref[step, part_rows:, :] = energy_ref[...]
        copy = pltpu.make_async_copy(parts_ref.at[step], parts_hbm[step], parts_sem.at[step])
        copy.start()
        last_copies.append(copy)
    for c in range(2):
        new_ref[c] = ext_ref[c, inner, mid] + sum_ref[c, inner, mid] * wide
        edge_left_ref[c] = (sum_ref[c, inner, :margin] * scale).astype(BF16)
        edge_right_ref[c] = (sum_ref[c, inner, far_side] * scale).astype(BF16)
    for k, (source, target) in enumerate(
        ((new_ref, new_hbm), (edge_left_ref, edge_left_hbm), (edge_right_ref, edge_right_hbm))
    ):
        copy = pltpu.make_async_copy(source, target, out_sem.at[k])
        copy.start()
        last_copies.append(copy)
    for copy in last_copies:
        copy.wait()


def patch_updates(
    rows, cols, count, place, own, left, right, probe, amplitudes, dual, shares, layers
):
    side = probe.shape[1]
    _, height, tile_cols = own.shape
    margin = left.shape[2]
    slots = amplitudes.shape[0]
    slab_rows = dual.shape[0]
    share = tile_cols // shares
    edge = min(share, margin)
    table = dft_table(side)
    extent = tile_cols + 2 * margin + LANES
    shape = jax.ShapeDtypeStruct
    slab_shape = (shares, layers, slab_rows // layers, share + edge)
    part_rows = 2 * side // shares + SUBLANES
    chain = [
        VMEM((2 * side, side), F32),
        VMEM((2 * side, side), BF16),
        VMEM((side, 2 * side), BF16),
        VMEM((side, 2 * side), F32),
    ]
    return pl.pallas_call(
        patch_kernel,
        in_specs=[SCALARS] * 4 + [ANYWHERE] * 7,
        out_specs=[ANYWHERE] * (4 + shares),
        out_shape=[
            shape((2, height, tile_cols), F32),
            shape((2, height, margin), BF16),
            shape((2, height, margin), BF16),
            shape(slab_shape, F32),
        ]
        + [shape((part_rows, side), F32)] * shares,
        scratch_shapes=[
            VMEM(probe.shape, F32),
            VMEM(amplitudes.shape, BF16),
            VMEM(table.shape, BF16),
            VMEM((2 * side, 2 * side), BF16),
            VMEM((2 * side, 2 * side), BF16),
            VMEM(dual.shape, F32),
            VMEM((2, height, tile_cols), F32),
            VMEM((2, height, margin), BF16),
            VMEM((2, height, margin), BF16),
            VMEM(slab_shape, F32),
            VMEM((shares, part_rows, side), F32),
            VMEM((2, height + SUBLANES, extent), F32),
            VMEM((2, height + SUBLANES, extent), F32),
            VMEM((2 * side, side), F32),
            VMEM((SUBLANES, side), F32),
            *chain,
            *chain,
            pltpu.SemaphoreType.DMA((6,)),
            pltpu.SemaphoreType.DMA((slots,)),
            pltpu.SemaphoreType.DMA((shares,)),
            pltpu.SemaphoreType.DMA((4,)),
        ],
        compiler_params=pltpu.CompilerParams(vmem_limit_bytes=VMEM_LIMIT),
        cost_estimate=pl.CostEstimate(
            flops=slots * 32 * side**3,
            bytes_accessed=8 * height * tile_cols * 4,
            transcendentals=slots * side * side,
        ),
        name="patches",
    )(
        rows,
        cols,
        count,
        place,
        own,
        left,
        right,
        probe,
        amplitudes,
        jnp.asarray(table),
        dual,
    )


def backward_kernel(
    ids_ref, residual_hbm, weights_hbm, out_ref, residual_ref, weights_ref, turned_ref, sem, weights_sem
):
    parts, projections, depth, share = residual_ref.shape
    both = projections * depth

    def weights_copy(a):
        return pltpu.make_async_copy(
            weights_hbm.at[ids_ref[a]], weights_ref.at[a], weights_sem.at[a]
        )

    residual_copy = pltpu.make_async_copy(residual_hbm, residual_ref, sem)
    residual_copy.start()
    for a in range(min(AHEAD, projections)):
        weights_copy(a).start()
    residual_copy.wait()
    for part in range(parts):
        block = residual_ref[part].astype(F32).reshape(both, share)
        turned_ref[part * share : (part + 1) * share, :] = block.T
    out_ref[...] = jnp.zeros(out_ref.shape, F32)

    members = math.gcd(projections, 2)

    @pl.loop(0, projections, step=members)
    def _(first):
        for a in range(members):
            weights_copy(first + a).wait()
        for a in range(members):
            item = first + a + AHEAD

            @pl.when(item < projections)
            def _():
                weights_copy(item).start()

        lane = lax.broadcasted_iota(jnp.int32, turned_ref.shape, 1)
        total = out_ref[...]
        for a in range(members):
            begin = (first + a) * depth
            kept = jnp.logical_and(lane >= begin, lane < begin + depth)
            chosen = jnp.where(kept, turned_ref[...], 0.0).astype(BF16)
            total += dot(weights_ref[first + a], chosen)
        out_ref[...] = total


def backward_sums(angle_ids, residual, proj_weights):
    _, rows, width = proj_weights.shape
    _, projections, depth, _ = residual.shape
    return pl.pallas_call(
        backward_kernel,
        in_specs=[SCALARS, ANYWHERE, ANYWHERE],
        out_specs=WHOLE,
        out_shape=jax.ShapeDtypeStruct((rows, projections * depth), F32),
        scratch_shapes=[
            VMEM(residual.shape, BF16),
            VMEM((projections, rows, width), BF16),
            VMEM((width, projections * depth), F32),
            DMA,
            pltpu.SemaphoreType.DMA((projections,)),
        ],
        compiler_params=pltpu.CompilerParams(vmem_limit_bytes=TOMO_LIMIT),
        cost_estimate=pl.CostEstimate(
            flops=2 * rows * width * projections * projections * depth,
            bytes_accessed=projections * rows * width * 2,
            transcendentals=0,
        ),
        name="backward",
    )(angle_ids, residual, proj_weights)


def update_kernel(
    ids_ref,
    sums_ref,
    rays_hbm,
    volume_hbm,
    out_hbm,
    rays_ref,
    stack_ref,
    spread_ref,
    volume_ref,
    done_ref,
    rays_sem,
    volume_sem,
    out_sem,
):
    depth = volume_ref.shape[0]
    slots = done_ref.shape[0]
    width = rays_ref.shape[1]
    projections = sums_ref.shape[1] // depth
    both = sums_ref.shape[1]

    def volume_copy(z):
        return pltpu.make_async_copy(volume_hbm.at[z], volume_ref.at[z], volume_sem.at[z])

    def out_copy(z):
        slot = lax.rem(z, slots)
        return pltpu.make_async_copy(done_ref.at[slot], out_hbm.at[z], out_sem.at[slot])

    rays_copy = pltpu.make_async_copy(rays_hbm, rays_ref, rays_sem)
    rays_copy.start()
    for z in range(min(UPDATE_AHEAD, depth)):
        volume_copy(z).start()
    high, low = split_bf16(sums_ref[...])
    stack_ref[...] = jnp.concatenate([high, low, high, low], axis=1)
    rays_copy.wait()
    rows = [
        jnp.broadcast_to(rays_ref[pl.ds(ids_ref[a], 1), :], (depth, width))
        for a in range(projections)
    ]
    high, low = split_bf16(jnp.concatenate(rows, axis=0))
    for place, block in enumerate((high, high, low, low)):
        spread_ref[place * both : (place + 1) * both, :] = block.astype(BF16)

    @pl.loop(0, depth)
    def _(z):
        volume_copy(z).wait()

        @pl.when(z + UPDATE_AHEAD < depth)
        def _():
            volume_copy(z + UPDATE_AHEAD).start()

        @pl.when(z >= slots)
        def _():
            out_copy(z - slots).wait()

        lane = lax.broadcasted_iota(jnp.int32, stack_ref.shape, 1)
        kept = lax.rem(lane, depth) == z
        chosen = jnp.where(kept, stack_ref[...], 0.0).astype(BF16)
        done_ref[lax.rem(z, slots)] = volume_ref[z] - tomo_step * dot(chosen, spread_ref[...])
        out_copy(z).start()

    for z in range(max(depth - slots, 0), depth):
        out_copy(z).wait()


def volume_update(angle_ids, sums, rays, volume):
    depth, rows, width = volume.shape
    slots = min(4, depth)
    return pl.pallas_call(
        update_kernel,
        in_specs=[SCALARS, WHOLE] + [ANYWHERE] * 2,
        out_specs=ANYWHERE,
        out_shape=jax.ShapeDtypeStruct(volume.shape, F32),
        scratch_shapes=[
            VMEM(rays.shape, F32),
            VMEM((rows, 4 * sums.shape[1]), F32),
            VMEM((4 * sums.shape[1], width), BF16),
            VMEM(volume.shape, F32),
            VMEM((slots, rows, width), F32),
            DMA,
            pltpu.SemaphoreType.DMA((depth,)),
            pltpu.SemaphoreType.DMA((slots,)),
        ],
        compiler_params=pltpu.CompilerParams(vmem_limit_bytes=VMEM_LIMIT),
        cost_estimate=pl.CostEstimate(
            flops=8 * rows * width * sums.shape[1] * depth,
            bytes_accessed=2 * depth * rows * width * 4,
            transcendentals=0,
        ),
        name="update",
    )(angle_ids, sums, rays, volume)


def gather_parts_kernel(group, *refs):
    *given, out_hbm, out_ref, sem = refs
    total = given[0][...]
    for ref in given[1:]:
        total = total + ref[...]
    blocks = total.shape[1] // LANES
    rows = (out_ref.shape[1] - SUBLANES) // blocks
    columns = [total[:, k * LANES : (k + 1) * LANES] for k in range(blocks)]
    energy = columns[0][group * rows :]
    for block in columns[1:]:
        energy = energy + block[group * rows :]
    for k in range(group):
        for place, block in enumerate(columns):
            out_ref[k, place * rows : (place + 1) * rows, :] = block[k * rows : (k + 1) * rows]
        out_ref[k, blocks * rows :, :] = energy
    copy = pltpu.make_async_copy(out_ref, out_hbm, sem)
    copy.start()
    copy.wait()


def gather_parts(given, group):
    total_rows, side = given[0].shape
    rows = (total_rows - SUBLANES) // group * (side // LANES) + SUBLANES
    shape = (group, rows, LANES)
    return pl.pallas_call(
        functools.partial(gather_parts_kernel, group),
        in_specs=[WHOLE] * len(given),
        out_specs=ANYWHERE,
        out_shape=jax.ShapeDtypeStruct(shape, F32),
        scratch_shapes=[VMEM(shape, F32), DMA],
        compiler_params=pltpu.CompilerParams(vmem_limit_bytes=SMALL_LIMIT),
        name="probe_parts",
    )(*given)


def probe_rows_kernel(given_ref, out_hbm, out_ref, sem):
    group, rows, _ = given_ref.shape
    receivers, taken, side = out_ref.shape
    total = given_ref[0]
    for k in range(1, group):
        total = total + given_ref[k]
    energy = jnp.sum(total[rows - SUBLANES :], keepdims=True) / (side * side)
    steps = total[: rows - SUBLANES] / (energy + 1e-05)
    steps = jnp.concatenate(
        [steps[k * taken : (k + 1) * taken] for k in range(side // LANES)], axis=1
    )
    for k in range(receivers):
        out_ref[k] = steps
    copy = pltpu.make_async_copy(out_ref, out_hbm, sem)
    copy.start()
    copy.wait()


def probe_rows(given, side, receivers):
    _, rows, _ = given.shape
    shape = (receivers, (rows - SUBLANES) * LANES // side, side)
    return pl.pallas_call(
        probe_rows_kernel,
        in_specs=[WHOLE],
        out_specs=ANYWHERE,
        out_shape=jax.ShapeDtypeStruct(shape, F32),
        scratch_shapes=[VMEM(shape, F32), DMA],
        compiler_params=pltpu.CompilerParams(vmem_limit_bytes=SMALL_LIMIT),
        name="probe_rows",
    )(given)


def turned(value, axis, steps):
    count = lax.axis_size(axis)
    return lax.ppermute(value, axis, [(k, (k + steps) % count) for k in range(count)])


def on_device(
    object_field,
    probe_field,
    amplitudes,
    pos_rows,
    pos_cols,
    counts,
    admm_dual,
    volume,
    proj_weights,
    ray_weights,
    angle_ids,
):
    margin = probe_field.shape[1] // 2
    own = object_field[0]
    tile_cols = own.shape[2]
    flat_axes = ("tile", "proj")
    plane = lax.axis_size("tile") * lax.axis_size("proj")
    proj_count = lax.axis_size("proj")
    layers = lax.axis_size("cuts")
    from_left = shifted(own[:, :, tile_cols - margin :], "tile", 1)
    from_right = shifted(own[:, :, :margin], "tile", -1)
    forward = forward_parts(angle_ids, volume, proj_weights, ray_weights, plane)
    _, from_left, from_right = lax.optimization_barrier((forward, from_left, from_right))
    arrived = lax.all_to_all(forward, flat_axes, 0, 0, tiled=True)
    place = lax.axis_index("proj")
    partial_object, edge_left, edge_right, slab, *grad_parts = patch_updates(
        pos_rows[0, 0],
        pos_cols[0, 0],
        counts[0],
        place[None],
        own,
        from_left,
        from_right,
        probe_field,
        amplitudes[0, 0],
        admm_dual[0],
        proj_count,
        layers,
    )

    share = tile_cols // proj_count
    edge = slab.shape[3] - share
    holders = margin // edge
    slab, arrived = lax.optimization_barrier((slab, arrived))
    pieces = slab.reshape(proj_count * layers, *slab.shape[2:])
    pieces = lax.all_to_all(pieces, ("proj", "cuts"), 0, 0, tiled=True)
    pieces, grad_parts = lax.optimization_barrier((pieces, grad_parts))
    pairs = []
    for tile in range(lax.axis_size("tile") - 1):
        for k in range(holders):
            lower = tile * proj_count + proj_count - holders + k
            upper = (tile + 1) * proj_count + k
            pairs += [(lower, upper), (upper, lower)]
    grads_in = lax.ppermute(pieces[:, :, share:], flat_axes, pairs)
    at_start = jnp.pad(grads_in, ((0, 0), (0, 0), (0, share - edge)))
    at_end = jnp.pad(grads_in, ((0, 0), (0, 0), (share - edge, 0)))
    target = pieces[:, :, :share] + jnp.where(place < holders, at_start, at_end)
    residual = (jnp.sum(arrived, axis=0) - target).astype(BF16)
    copies = jnp.broadcast_to(residual[None], (plane, *residual.shape))

    group_axes = ("tile", "cuts")
    group = lax.axis_size("tile") * layers
    given = [grad_parts[0]]
    for step in range(1, proj_count):
        given.append(turned(grad_parts[step], "proj", step))
    copies, given = lax.optimization_barrier((copies, given))
    residual = lax.all_to_all(copies, flat_axes, 0, 0, tiled=True)
    by_receiver = gather_parts(given, group)
    residual, by_receiver, edge_left, edge_right = lax.optimization_barrier(
        (residual, by_receiver, edge_left, edge_right)
    )
    received = lax.all_to_all(by_receiver, group_axes, 0, 0, tiled=True)
    edge_from_left = shifted(edge_right, "tile", 1)
    back_sums = backward_sums(angle_ids, residual, proj_weights)
    back_sums, received, edge_left = lax.optimization_barrier((back_sums, received, edge_left))
    edge_from_right = shifted(edge_left, "tile", -1)
    steps = probe_rows(received, probe_field.shape[1], plane * layers)
    back_sums, steps, edge_from_left = lax.optimization_barrier(
        (back_sums, steps, edge_from_left)
    )
    steps = lax.all_to_all(steps, ("proj", "tile", "cuts"), 0, 0, tiled=True)
    new_volume = volume_update(angle_ids, back_sums, ray_weights, volume)
    new_volume, steps = lax.optimization_barrier((new_volume, steps))
    new_probe = probe_field + steps.reshape(probe_field.shape)
    rest = tile_cols - margin
    new_object = (
        partial_object
        + jnp.pad(edge_from_left.astype(F32), ((0, 0), (0, 0), (0, rest)))
        + jnp.pad(edge_from_right.astype(F32), ((0, 0), (0, 0), (rest, 0)))
    )
    return (new_object[None], new_probe, new_volume)


def solution(mesh):
    in_specs = (
        P(("proj", "cuts"), None, None, "tile"),
        P(),
        P(("proj", "cuts"), "tile", None, None, None),
        P(("proj", "cuts"), "tile", None),
        P(("proj", "cuts"), "tile", None),
        P(("proj", "cuts"), "tile"),
        P(("proj", "cuts"), None, "tile"),
        P("cuts", ("tile", "proj"), None),
        P(None, ("tile", "proj"), None),
        P(),
        P(),
    )
    out_specs = (P(("proj", "cuts"), None, None, "tile"), P(), P("cuts", ("tile", "proj"), None))
    return jax.shard_map(
        on_device, mesh=mesh, in_specs=in_specs, out_specs=out_specs, check_vma=False
    )
```
